512 devices in a mesh: stream: 64 (over x, z), cross: 8 (over y, core).
Axes of the slice: x: 4, y: 4, z: 16, core: 2. Of those that a mesh axis runs over, the one named last changes fastest.
Arguments:
- source: float32 [512, 64, 128], P('stream', 'cross'), may hold values from -6 to 6
- metric: float32 [64, 8, 16], P('stream', 'cross'), may hold values from 0.5 to 4
- base_velocity: float32 [3, 512, 64, 128], P(None, 'stream', 'cross'), may hold values from -6 to 6
- drop_elem: int32 [64, 8, 5, 128], P('stream', 'cross'), may hold values from 0 to 8191, as said below
- drop_coord: float32 [64, 8, 5, 3, 128], P('stream', 'cross'), may hold values from -1 to 1
- drop_vel: float32 [64, 8, 5, 3, 128], P('stream', 'cross'), may hold values from -6 to 6
- drop_prop: float32 [64, 8, 5, 2, 128], P('stream', 'cross'), may hold values from 0.5 to 4
- drop_counts: int32 [64, 8, 5], P('stream', 'cross'), may hold values from 0 to 128, as said below
Outputs:
- pressure: float32 [512, 64, 128], P('stream', 'cross')
- momentum_source: float32 [3, 512, 64, 128], P(None, 'stream', 'cross')
- drop_accel: float32 [64, 8, 5, 3, 128], P('stream', 'cross')
The draws below stay inside these ranges and needn't reach their ends.
Inputs may be any that keep to these rules, and one draw needn't show every extreme that they name: `drop_elem`: elements are numbered (ex * 8 + ey) * 16 + ez. The owner element of every slot of block b of holder (s, c) lies in slab s + b - 2 (streamwise element index from (s + b - 2) * 1 to that plus 1 - 1) and column c (element index from c * 1 to c + 1 - 1); this holds for slots that are not live as well, for blocks whose slab lies in the grid. `drop_counts`: A block whose owner slab s + b - 2 lies outside 0 to 63 has count 0. In every draw some slab of some column receives 128 live droplets from each of its 5 holder slabs.
All inputs are finite; a program needn't handle non-finite values.
Results may differ from the reference program's by a relative error of at most 0.0003.
Values sent between devices are 32-bit elements; how exact they have to be, the bound alone decides.
A program may use at most 64 MiB of HBM per device.

```python
import math
import jax
import jax.numpy as jnp
import numpy as np
from jax import lax

EX = 1
EY = 1
EZ = 16
CAP = 128
SWEEPS = 3
DRIFT = 2
REACH = 5
SLABS = 64
COLS = 8
EXT = 64
EYT = 8
XT = 512
YT = 64
ZT = 128


def draw_drop_elem(key, part):
    slab_index = jnp.arange(SLABS, dtype=jnp.int32)
    offsets = jnp.arange(REACH, dtype=jnp.int32) - DRIFT
    target = jnp.clip(slab_index[:, None] + offsets[None, :], 0, SLABS - 1)
    shape_all = (SLABS, COLS, REACH, CAP)
    pick_x = jax.random.randint(jax.random.fold_in(key, 11), shape_all, 0, EX)
    pick_y = jax.random.randint(jax.random.fold_in(key, 12), shape_all, 0, EY)
    pick_z = jax.random.randint(jax.random.fold_in(key, 13), shape_all, 0, EZ)
    elem_x = target[:, None, :, None] * EX + pick_x
    col_index = jnp.arange(COLS, dtype=jnp.int32)
    elem_y = col_index[None, :, None, None] * EY + pick_y
    return ((elem_x * EYT + elem_y) * EZ + pick_z).astype(jnp.int32)


def draw_drop_counts(key, part):
    base_counts = jax.random.randint(jax.random.fold_in(key, 21), (SLABS, COLS, REACH), CAP // 3, CAP + 1)
    slab_index = jnp.arange(SLABS, dtype=jnp.int32)
    offsets = jnp.arange(REACH, dtype=jnp.int32) - DRIFT
    owner_slab = slab_index[:, None] + offsets[None, :]
    inside = (owner_slab >= 0) & (owner_slab < SLABS)
    full_slab = jax.random.randint(jax.random.fold_in(key, 22), (), DRIFT, SLABS - DRIFT)
    full_col = jax.random.randint(jax.random.fold_in(key, 23), (), 0, COLS)
    col_index = jnp.arange(COLS, dtype=jnp.int32)
    hit_slab = owner_slab == full_slab
    hit = hit_slab[:, None, :] & (col_index == full_col)[None, :, None]
    counts = jnp.where(hit, CAP, base_counts)
    return jnp.where(inside[:, None, :], counts, 0).astype(jnp.int32)


def steps_of(own_key, dims, shards, low, high):
    def one(position, parts):
        draws = jax.random.uniform(jax.random.fold_in(jax.random.fold_in(own_key, 6), position), (parts,), jnp.float32, low / len(shards), high / len(shards))
        return jnp.repeat(jnp.exp(draws), dims[position] // parts).reshape((-1,) + (1,) * (len(dims) - position - 1))

    factor_of = one(*shards[0])
    for cut in shards[1:]:
        factor_of = factor_of * one(*cut)
    return factor_of


def bell_draw(key, extent, scale, most, split=(), kind=jnp.bfloat16):
    entries = scale * jax.random.normal(key, extent, jnp.float32)
    if split:
        entries = entries * steps_of(key, extent, split, -0.22, 0.18)
    return jnp.clip(entries, -most, most).astype(kind)


def setup_inputs(seed: int = 0) -> dict:
    arg_keys = jax.random.split(jax.random.key(seed), 9)
    source = bell_draw(arg_keys[0], (XT, YT, ZT), 1.0, 6.0, ((0, 64), (1, 8)), jnp.float32)
    metric = jnp.clip(jnp.exp(math.log(4.0) - 2.0794415 * jax.random.uniform(arg_keys[1], (EXT, EYT, EZ), jnp.float32) ** steps_of(arg_keys[1], (EXT, EYT, EZ), ((0, 64), (1, 8)), -0.2, 0.2)), 0.5, 4.0)
    base_velocity = bell_draw(arg_keys[2], (3, XT, YT, ZT), 1.0, 6.0, ((1, 64), (2, 8)), jnp.float32)
    drop_elem = draw_drop_elem(jax.random.fold_in(arg_keys[8], 71), 0)
    drop_coord = jnp.clip(jax.random.uniform(arg_keys[4], (SLABS, COLS, REACH, 3, CAP), jnp.float32, -1.0, 1.0) * steps_of(arg_keys[4], (SLABS, COLS, REACH, 3, CAP), ((0, 64), (1, 8)), -0.4, 0.0), -1.0, 1.0)
    drop_vel = bell_draw(arg_keys[5], (SLABS, COLS, REACH, 3, CAP), 1.0, 6.0, ((0, 64), (1, 8)), jnp.float32)
    drop_prop = jnp.clip(jnp.exp(math.log(4.0) - 2.0794415 * jax.random.uniform(arg_keys[6], (SLABS, COLS, REACH, 2, CAP), jnp.float32) ** steps_of(arg_keys[6], (SLABS, COLS, REACH, 2, CAP), ((0, 64), (1, 8)), -0.2, 0.2)), 0.5, 4.0)
    drop_counts = draw_drop_counts(jax.random.fold_in(arg_keys[8], 71), 0)
    return dict(source=source, metric=metric, base_velocity=base_velocity, drop_elem=drop_elem, drop_coord=drop_coord, drop_vel=drop_vel, drop_prop=drop_prop, drop_counts=drop_counts)


HIGHEST_PREC = lax.Precision.HIGHEST
MASS_SHIFT = 1.0
UPPER_BOUND = 2.5
LOWER_BOUND = UPPER_BOUND / 30.0
GLL_POINTS = [-1.0, -0.8717401485096066, -0.5917001814331423, -0.2092992179024789,
              0.2092992179024789, 0.5917001814331423, 0.8717401485096066, 1.0]


def legendre_seven(points):
    before = points * 0.0 + 1.0
    current = points
    for order in range(1, 7):
        following = ((2.0 * order + 1.0) * points * current - order * before) / (order + 1.0)
        before = current
        current = following
    return current


def outer_three(first, second, third):
    return first[:, None, None] * second[None, :, None] * third[None, None, :]


def gll_tables():
    gll_nodes = np.array(GLL_POINTS)
    values = legendre_seven(gll_nodes)
    weights = 2.0 / (56.0 * values * values)
    deriv_mat = np.zeros((8, 8))
    for row_idx in range(8):
        for col_idx in range(8):
            if row_idx != col_idx:
                deriv_mat[row_idx, col_idx] = values[row_idx] / (values[col_idx] * (gll_nodes[row_idx] - gll_nodes[col_idx]))
    deriv_mat[0, 0] = -14.0
    deriv_mat[7, 7] = 14.0
    return gll_nodes, weights, deriv_mat


def weight_cube():
    gll_nodes, weights, deriv_mat = gll_tables()
    cube_table = outer_three(weights, weights, weights)
    return jnp.asarray(cube_table.reshape(1, 8, 1, 8, 1, 8), jnp.float32)


def split_cells(grid_field):
    size_x, size_y, size_z = grid_field.shape[-3:]
    return grid_field.reshape(grid_field.shape[:-3] + (size_x // 8, 8, size_y // 8, 8, size_z // 8, 8))


def scale_of(metric):
    return metric[:, None, :, None, :, None]


def derivatives(cells):
    gll_nodes, weights, deriv_mat = gll_tables()
    dmat = jnp.asarray(deriv_mat, jnp.float32)
    grad_x = jnp.einsum("ia,xaybzc->xiybzc", dmat, cells, precision=HIGHEST_PREC)
    grad_y = jnp.einsum("jb,xaybzc->xayjzc", dmat, cells, precision=HIGHEST_PREC)
    grad_z = jnp.einsum("kc,xaybzc->xaybzk", dmat, cells, precision=HIGHEST_PREC)
    return grad_x, grad_y, grad_z


def operator_local(grid_field, metric):
    gll_nodes, weights, deriv_mat = gll_tables()
    dmat = jnp.asarray(deriv_mat, jnp.float32)
    cells = split_cells(grid_field)
    wcube = weight_cube()
    grad_x, grad_y, grad_z = derivatives(cells)
    back_x = jnp.einsum("ai,xaybzc->xiybzc", dmat, wcube * grad_x, precision=HIGHEST_PREC)
    back_y = jnp.einsum("bj,xaybzc->xayjzc", dmat, wcube * grad_y, precision=HIGHEST_PREC)
    back_z = jnp.einsum("ck,xaybzc->xaybzk", dmat, wcube * grad_z, precision=HIGHEST_PREC)
    result = scale_of(metric) * (back_x + back_y + back_z) + MASS_SHIFT * wcube * cells
    return result.reshape(grid_field.shape)


def diagonal_local(metric, field_shape):
    gll_nodes, weights, deriv_mat = gll_tables()
    stiff_diag = (deriv_mat * deriv_mat * weights[:, None]).sum(0)
    cube_table = (outer_three(stiff_diag, weights, weights)
                  + outer_three(weights, stiff_diag, weights)
                  + outer_three(weights, weights, stiff_diag))
    stiff_cube = jnp.asarray(cube_table.reshape(1, 8, 1, 8, 1, 8), jnp.float32)
    result = scale_of(metric) * stiff_cube + MASS_SHIFT * weight_cube()
    return result.reshape(field_shape)


def pair_sum(padded, along):
    length = padded.shape[along] - 2
    count = length // 8
    interior = lax.slice_in_dim(padded, 1, length + 1, axis=along)
    before_rows = lax.slice_in_dim(padded, 0, length, 8, along)
    after_rows = lax.slice_in_dim(padded, 9, length + 2, 8, along)
    split_shape = interior.shape[:along] + (count, 8) + interior.shape[along + 1:]
    blocks = interior.reshape(split_shape)
    first_row = lax.slice_in_dim(blocks, 0, 1, axis=along + 1) + jnp.expand_dims(before_rows, along + 1)
    middle = lax.slice_in_dim(blocks, 1, 7, axis=along + 1)
    last_row = lax.slice_in_dim(blocks, 7, 8, axis=along + 1) + jnp.expand_dims(after_rows, along + 1)
    return jnp.concatenate([first_row, middle, last_row], along + 1).reshape(interior.shape)


def assemble(padded):
    first_axis = padded.ndim - 3
    summed = pair_sum(padded, first_axis)
    summed = pair_sum(summed, first_axis + 1)
    pad_width = [(0, 0)] * (summed.ndim - 1) + [(1, 1)]
    return pair_sum(jnp.pad(summed, pad_width), first_axis + 2)


def zero_rim(grid_field):
    pad_width = [(0, 0)] * (grid_field.ndim - 3) + [(1, 1), (1, 1), (0, 0)]
    return jnp.pad(grid_field, pad_width)


def chebyshev(source, metric, summer):
    center = (UPPER_BOUND + LOWER_BOUND) / 2.0
    half_width = (UPPER_BOUND - LOWER_BOUND) / 2.0
    ratio_bound = center / half_width
    cheb_rho = 1.0 / ratio_bound
    cells = split_cells(source)
    right_side = summer((weight_cube() * cells).reshape(source.shape))
    diagonal = summer(diagonal_local(metric, source.shape))
    inv_diag = 1.0 / diagonal
    residual = right_side
    update = inv_diag * residual / center
    iterate = jnp.zeros_like(source)
    for sweep in range(SWEEPS):
        iterate = iterate + update
        residual = residual - summer(operator_local(update, metric))
        rho_next = 1.0 / (2.0 * ratio_bound - cheb_rho)
        update = (rho_next * cheb_rho) * update + (2.0 * rho_next / half_width) * (inv_diag * residual)
        cheb_rho = rho_next
    return iterate + update


def velocity_table(pressure, base_velocity, metric):
    cells = split_cells(pressure)
    grad_x, grad_y, grad_z = derivatives(cells)
    scale_cube = scale_of(metric)
    gradient = jnp.stack([scale_cube * grad_x, scale_cube * grad_y, scale_cube * grad_z], 0)
    velocity = split_cells(base_velocity) - gradient
    velocity = velocity.transpose(1, 3, 5, 0, 2, 4, 6)
    return velocity.reshape(metric.shape[0] * metric.shape[1] * metric.shape[2], 1536)


def table_to_field(source_table, metric):
    elem_x, elem_y, elem_z = metric.shape
    cube = source_table.reshape(elem_x, elem_y, elem_z, 3, 8, 8, 8).transpose(3, 0, 4, 1, 5, 2, 6)
    return cube.reshape(3, 8 * elem_x, 8 * elem_y, 8 * elem_z)


def lagrange(coords):
    gll_nodes, weights, deriv_mat = gll_tables()
    factors = []
    for node_idx in range(8):
        factor = jnp.ones_like(coords)
        for other_idx in range(8):
            if other_idx != node_idx:
                factor = factor * (coords - float(gll_nodes[other_idx])) / float(gll_nodes[node_idx] - gll_nodes[other_idx])
        factors.append(factor)
    return jnp.stack(factors, 0)


def droplet_terms(gathered, drop_state, is_live):
    slot_count = gathered.shape[0]
    basis_r = lagrange(drop_state[0])
    basis_s = lagrange(drop_state[1])
    basis_t = lagrange(drop_state[2])
    partial_value = jnp.einsum("ncijk,kn->ncij", gathered, basis_t, precision=HIGHEST_PREC)
    partial_value = jnp.einsum("ncij,jn->nci", partial_value, basis_s, precision=HIGHEST_PREC)
    fluid_vel = jnp.einsum("nci,in->cn", partial_value, basis_r, precision=HIGHEST_PREC)
    drag_accel = jnp.where(is_live[None, :], drop_state[6][None, :] * (fluid_vel - drop_state[3:6]), 0.0)
    drag_force = -drop_state[7][None, :] * drag_accel
    spread = jnp.einsum("cn,in,jn,kn->ncijk", drag_force, basis_r, basis_s, basis_t, precision=HIGHEST_PREC)
    return drag_accel, spread.reshape(slot_count, 1536)


def reference(source, metric, base_velocity, drop_elem, drop_coord, drop_vel, drop_prop, drop_counts):
    pressure = chebyshev(source, metric, lambda grid_field: assemble(zero_rim(grid_field)))
    vel_table = velocity_table(pressure, base_velocity, metric)
    holders = SLABS * COLS
    slot_total = REACH * CAP
    drop_state = jnp.concatenate([drop_coord, drop_vel, drop_prop], axis=3)
    drop_state = drop_state.reshape(holders, REACH, 8, CAP).transpose(0, 2, 1, 3).reshape(holders, 8, slot_total)
    owner_ids = drop_elem.reshape(holders, slot_total).astype(jnp.int32)
    slot_index = jnp.arange(CAP, dtype=jnp.int32)
    is_live = (slot_index[None, None, :] < drop_counts.reshape(holders, REACH)[:, :, None]).reshape(holders, slot_total)

    def per_holder(running, inputs):
        holder_ids, holder_state, holder_live = inputs
        gathered = jnp.take(vel_table, holder_ids, axis=0).reshape(slot_total, 3, 8, 8, 8)
        drag_accel, spread = droplet_terms(gathered, holder_state, holder_live)
        running = running.at[holder_ids].add(spread)
        return running, drag_accel

    empty_table = jnp.zeros((EXT * EYT * EZ, 1536), jnp.float32)
    source_table, accels = lax.scan(per_holder, empty_table, (owner_ids, drop_state, is_live))
    drop_accel = accels.reshape(holders, 3, REACH, CAP).transpose(0, 2, 1, 3).reshape(SLABS, COLS, REACH, 3, CAP)
    momentum_source = assemble(zero_rim(table_to_field(source_table, metric)))
    return pressure, momentum_source, drop_accel
```

```python
import functools

import jax
import jax.numpy as jnp
import numpy as np
from jax import lax
from jax.experimental import pallas as pl
from jax.experimental.pallas import tpu as pltpu
from jax.sharding import PartitionSpec as P

SWEEPS = 3
UPPER_BOUND = 2.5
LOWER_BOUND = UPPER_BOUND / 30.0
REACH = 5
DRIFT = 2
CAP = 128
EZ = 16
GLL_POINTS = [
    -1.0,
    -0.8717401485096066,
    -0.5917001814331423,
    -0.2092992179024789,
    0.2092992179024789,
    0.5917001814331423,
    0.8717401485096066,
    1.0,
]
F32 = jnp.float32
BF16 = jnp.bfloat16
MESH = pl.DeviceIdType.MESH

DIRS = [(1, 0), (-1, 0), (0, 1), (0, -1), (1, 1), (1, -1), (-1, 1), (-1, -1)]
SLOT = {d: k for k, d in enumerate(DIRS)}
ORDER = [4, 5, 6, 7, 0, 1, 2, 3]


def legendre_seven(points):
    before = points * 0.0 + 1.0
    current = points
    for order in range(1, 7):
        following = ((2.0 * order + 1.0) * points * current - order * before) / (order + 1.0)
        before = current
        current = following
    return current


def gll_tables():
    nodes = np.array(GLL_POINTS)
    values = legendre_seven(nodes)
    weights = 2.0 / (56.0 * values * values)
    deriv = np.zeros((8, 8))
    for row in range(8):
        for col in range(8):
            if row != col:
                deriv[row, col] = values[row] / (values[col] * (nodes[row] - nodes[col]))
    deriv[0, 0] = -14.0
    deriv[7, 7] = 14.0
    return nodes, weights, deriv


NODES, WEIGHTS, DERIV = gll_tables()
STIFF = DERIV.T @ (WEIGHTS[:, None] * DERIV)
QDIAG = np.diag(STIFF)

T_WK, T_QK, T_KT, T_EYE, T_WJ, T_QJ, T_CY, T_DT, T_LAG, T_ZM = 0, 1, 2, 3, 4, 5, 6, 14, 22, 23
TILES = 24


def constant_tiles():
    lane = np.arange(128)
    row = np.arange(8)
    tiles = np.zeros((TILES, 8, 128))
    tiles[T_WK] = WEIGHTS[lane % 8][None, :]
    tiles[T_QK] = QDIAG[lane % 8][None, :]
    tiles[T_KT] = STIFF[lane % 8, :].T
    tiles[T_EYE] = lane[None, :] % 8 == row[:, None]
    tiles[T_WJ] = WEIGHTS[:, None]
    tiles[T_QJ] = QDIAG[:, None]
    for turn in range(8):
        tiles[T_CY + turn] = STIFF[row, (row - turn) % 8][:, None]
        tiles[T_DT + turn] = DERIV[(row - turn) % 8, row][:, None]
    gaps = NODES[:, None] - NODES[None, :] + np.eye(8)
    tiles[T_LAG] = (1.0 / gaps.prod(1))[:, None]
    last = (lane % 8 == 7) & (lane < 127)
    first = (lane % 8 == 0) & (lane > 0)
    tiles[T_ZM] = (last | first)[None, :]
    return tiles.astype(np.float32)


def iota(dim):
    return lax.broadcasted_iota(jnp.int32, (8, 128), dim)


def total(terms):
    terms = list(terms)
    while len(terms) > 1:
        pairs = [a + b for a, b in zip(terms[::2], terms[1::2])]
        if len(terms) % 2:
            pairs.append(terms[-1])
        terms = pairs
    return terms[0]


def wide(row):
    return jnp.broadcast_to(row, (8, 128))


def halves(value):
    high = value.astype(BF16)
    return high, (value - high.astype(F32)).astype(BF16)


def stiff_x(u):
    even = [u[m] + u[7 - m] for m in range(4)]
    odd = [u[m] - u[7 - m] for m in range(4)]
    out = [None] * 8
    for i in range(4):
        e = total(float((STIFF[i, m] + STIFF[i, 7 - m]) / 2.0) * even[m] for m in range(4))
        o = total(float((STIFF[i, m] - STIFF[i, 7 - m]) / 2.0) * odd[m] for m in range(4))
        out[i] = e + o
        out[7 - i] = e - o
    return out


def turned(value, tab, first):
    terms = [tab[first] * value]
    for turn in range(1, 8):
        terms.append(tab[first + turn] * pltpu.roll(value, turn, 0))
    return total(terms)


def kernel(
    src, met, bvel, elem, coord, dvel, dprop, cnt, tab,
    p_out, m_out, acc_out,
    qb, mb, bmat, lz, ld, lx, dx, ly, dy, fbase,
    hsend0, hrecv0, hsend, hrecv, fsend, frecv, dsend, drecv, rsend, rrecv,
    s0, r0, s1, r1, s4, r4, sd, rd, sr, rr,
):
    slabs, cols = lax.axis_size("stream"), lax.axis_size("cross")
    slab, col = lax.axis_index("stream"), lax.axis_index("cross")

    def device(ds, dc):
        return (lax.rem(slab + (ds + slabs), slabs), lax.rem(col + (dc + cols), cols))

    barrier = pltpu.get_barrier_semaphore()
    partners = DIRS + [(2, 0), (-2, 0)]
    for d in partners:
        pl.semaphore_signal(barrier, inc=1, device_id=device(*d), device_id_type=MESH)

    sub, lane = iota(0), iota(1)
    perm = jnp.clip(
        lane + jnp.where(lane % 8 == 7, 1, 0) - jnp.where(lane % 8 == 0, 1, 0), 0, 127
    )
    zmask = tab[T_ZM]
    wk, wj = tab[T_WK], tab[T_WJ]
    elane = lane // 8
    eperm = perm // 8

    def moved(value):
        return zmask * jnp.take_along_axis(value, perm, axis=1)

    def sum_z(value):
        return value + moved(value)

    from_x = {1: (slab > 0).astype(F32), -1: (slab < slabs - 1).astype(F32)}
    from_y = {1: (col > 0).astype(F32), -1: (col < cols - 1).astype(F32)}
    rowmask = {
        1: jnp.where(sub == 0, from_y[1], 0.0),
        -1: jnp.where(sub == 7, from_y[-1], 0.0),
    }
    edge_row = {1: 7, -1: 0}

    amet = jnp.zeros((8, 128), F32)
    for e in range(EZ):
        amet = jnp.where(elane == e, met[0, 0, e], amet)
    aw = amet * wk
    a1 = sum_z(aw)
    a23 = sum_z(amet * tab[T_QK] + wk)
    rhs = [sum_z(wk * src[i]) for i in range(8)]

    def stage(value, send, rows):
        for i in range(8):
            qb[8 * i : 8 * i + 8, :] = value[i]
        send[0, 0:8, :] = value[7]
        send[1, 0:8, :] = value[0]
        send[2, 0:8, :] = qb[pl.ds(7, 8, stride=8), :]
        send[3, 0:8, :] = qb[pl.ds(0, 8, stride=8), :]

    def tile_of(d):
        return SLOT[(d[0], 0)] if d[0] else SLOT[d]

    def copies(send, recv, send_sems, recv_sems):
        return [
            pltpu.make_async_remote_copy(
                src_ref=send.at[tile_of(DIRS[k])],
                dst_ref=recv.at[k],
                send_sem=send_sems.at[k],
                recv_sem=recv_sems.at[k],
                device_id=device(*DIRS[k]),
                device_id_type=MESH,
            )
            for k in ORDER
        ]

    def combine(value, recv, row):
        def face(side):
            full = recv(SLOT[(side, 0)])[0:8, :]
            full += rowmask[1] * row(recv(SLOT[(side, 1)]), 7)
            full += rowmask[-1] * row(recv(SLOT[(side, -1)]), 0)
            return from_x[side] * full

        out = []
        for i in range(8):
            terms = [value[i]]
            terms.append(rowmask[1] * row(recv(SLOT[(0, 1)]), i))
            terms.append(rowmask[-1] * row(recv(SLOT[(0, -1)]), i))
            if i == 0:
                terms.append(face(1))
            if i == 7:
                terms.append(face(-1))
            out.append(total(terms))
        return out

    def row_of(ref, i):
        return wide(ref[i : i + 1, :])

    stage(rhs, hsend0, 8)
    rows = jnp.where(sub == 0, a1, a23)
    for k in range(4):
        hsend0[k, 8:16, :] = rows

    for b in range(REACH):
        dsend[b, 0:3, :] = coord[b]
        dsend[b, 3:6, :] = dvel[b]
        dsend[b, 6:7, :] = dprop[b, 0:1, :] * dprop[b, 1:2, :]
        dsend[b, 7:8, :] = jnp.where(
            lane[0:1] < cnt[0, 0, b], (elem[b] % EZ).astype(F32), -1.0
        )

    def drop_copy(b):
        return pltpu.make_async_remote_copy(
            src_ref=dsend.at[b],
            dst_ref=drecv.at[b],
            send_sem=sd.at[b],
            recv_sem=rd.at[b],
            device_id=device(b - DRIFT, 0),
            device_id_type=MESH,
        )

    def back_copy(b):
        return pltpu.make_async_remote_copy(
            src_ref=rsend.at[b],
            dst_ref=rrecv.at[b],
            send_sem=sr.at[b],
            recv_sem=rr.at[b],
            device_id=device(DRIFT - b, 0),
            device_id_type=MESH,
        )

    away = [0, 4, 1, 3]

    pl.semaphore_wait(barrier, len(partners))
    flight0 = copies(hsend0, hrecv0, s0, r0)
    for copy in flight0:
        copy.start()
    drops = [drop_copy(b) for b in away]
    for copy in drops:
        copy.start()

    t8 = tab[T_KT] * amet + tab[T_EYE] * wk
    g8 = moved(t8)
    bfull = jnp.concatenate(
        [
            jnp.where(elane == e, t8, 0.0) + jnp.where(eperm == e, g8, 0.0)
            for e in range(EZ)
        ],
        axis=0,
    )
    bhigh, blow = halves(bfull)
    bmat[0:128, 0:128] = bhigh
    bmat[0:128, 128:256] = blow
    bmat[128:256, 0:128] = bhigh
    bmat[128:256, 128:256] = jnp.zeros((128, 128), BF16)

    def operator(u):
        high, low = halves(jnp.concatenate(u, axis=0))
        both = jnp.dot(
            jnp.concatenate([high, low], axis=1), bmat[...], preferred_element_type=F32
        )
        along_z = both[:, 0:128] + both[:, 128:256]
        along_x = stiff_x(u)
        out = []
        for i in range(8):
            along_y = turned(u[i], tab, T_CY)
            plane = (wj * along_x[i] + float(WEIGHTS[i]) * along_y) * aw
            first = (float(WEIGHTS[i]) * wj) * along_z[8 * i : 8 * i + 8, :]
            out.append(first + sum_z(plane))
        return out

    def basis_block(b):
        def basis(r):
            value = tab[T_LAG]
            for m in range(8):
                value = value * jnp.where(sub == m, 1.0, r - float(NODES[m]))
            return value, turned(value, tab, T_DT)

        tile = drecv.at[b] if b != DRIFT else dsend.at[b]
        eid = row_of(tile, 7)
        lx[b], dx[b] = basis(row_of(tile, 0))
        ly[b], dy[b] = basis(row_of(tile, 1))
        span = slice(b * CAP, b * CAP + CAP)
        for part, ref in zip(basis(row_of(tile, 2)), (lz, ld)):
            high = part.astype(BF16).astype(F32)
            for piece, start in ((high, 0), (part - high, 128)):
                spread = jnp.concatenate(
                    [jnp.where(eid == float(e), piece, 0.0) for e in range(EZ)], axis=0
                )
                ref[start : start + 128, span] = spread.astype(BF16)

    def contract(planes, span, first, second):
        inner = total(row_of(first, i) * planes[i][:, span] for i in range(8))
        return jnp.sum(second[...] * inner, axis=0, keepdims=True)

    def base_values():
        flat = jnp.concatenate([bvel[c, i] for c in range(3) for i in range(8)], axis=0)
        high, low = halves(flat)
        left = jnp.concatenate(
            [
                jnp.concatenate([high, high], axis=1),
                jnp.concatenate([low, jnp.zeros_like(low)], axis=1),
            ],
            axis=0,
        )
        for b in range(REACH):
            span = slice(b * CAP, b * CAP + CAP)
            both = jnp.dot(left, lz[:, span], preferred_element_type=F32)
            both = both[0:192, :] + both[192:384, :]
            for c in range(3):
                planes = [both[64 * c + 8 * i : 64 * c + 8 * i + 8, :] for i in range(8)]
                fbase[b, c : c + 1, :] = contract(planes, slice(0, 128), lx.at[b], ly.at[b])

    basis_block(DRIFT)

    for copy in flight0:
        copy.wait_recv()
    residual = combine(rhs, lambda k: hrecv0.at[k], row_of)

    def diag_rows(own, offset):
        def from_slot(d):
            return row_of(hrecv0.at[SLOT[d]], 8 + offset)

        middle = own + rowmask[1] * from_slot((0, 1)) + rowmask[-1] * from_slot((0, -1))
        ends = {}
        for side in (1, -1):
            extra = from_slot((side, 0))
            extra += rowmask[1] * from_slot((side, 1)) + rowmask[-1] * from_slot((side, -1))
            ends[side] = middle + from_x[side] * extra
        return [ends[1]] + [middle] * 6 + [ends[-1]]

    center = (UPPER_BOUND + LOWER_BOUND) / 2.0
    half_width = (UPPER_BOUND - LOWER_BOUND) / 2.0
    bound = center / half_width
    rho = 1.0 / bound

    a1_all, a23_all = diag_rows(a1, 0), diag_rows(a23, 1)
    inv_diag, update = [], []
    for i in range(8):
        w_i, q_i = float(WEIGHTS[i]), float(QDIAG[i])
        residual[i] = (w_i * wj) * residual[i]
        diagonal = (q_i * wj + w_i * tab[T_QJ]) * a1_all[i] + (w_i * wj) * a23_all[i]
        inv_diag.append(1.0 / diagonal)
        update.append(inv_diag[i] * residual[i] * (1.0 / center))
    iterate = update

    flights = []
    for sweep in range(SWEEPS):
        local = operator(update)
        stage(local, hsend.at[sweep], 8)
        flight = copies(hsend.at[sweep], hrecv.at[sweep], s1.at[sweep], r1.at[sweep])
        for copy in flight:
            copy.start()
        flights.append(flight)
        if sweep == 0:
            for copy in drops:
                copy.wait_recv()
            basis_block(1)
            basis_block(3)
        elif sweep == 1:
            basis_block(0)
            basis_block(4)
        elif sweep == 2:
            base_values()
        for copy in flight:
            copy.wait_recv()
        step = combine(local, lambda k: hrecv.at[sweep, k], row_of)
        rho_next = 1.0 / (2.0 * bound - rho)
        for i in range(8):
            residual[i] = residual[i] - step[i]
        update = [
            (rho_next * rho) * update[i]
            + (2.0 * rho_next / half_width) * (inv_diag[i] * residual[i])
            for i in range(8)
        ]
        rho = rho_next
        iterate = [iterate[i] + update[i] for i in range(8)]

    for i in range(8):
        p_out[i] = iterate[i]

    scaled = jnp.concatenate([amet * iterate[i] for i in range(8)], axis=0)
    high, low = halves(scaled)
    left = jnp.concatenate(
        [
            jnp.concatenate([high, high], axis=1),
            jnp.concatenate([low, jnp.zeros_like(low)], axis=1),
        ],
        axis=0,
    )
    forces = []
    for b in range(REACH):
        span = slice(b * CAP, b * CAP + CAP)
        whole = slice(0, 128)

        def planes_of(ref):
            both = jnp.dot(left, ref[:, span], preferred_element_type=F32)
            both = both[0:64, :] + both[64:128, :]
            return [both[8 * i : 8 * i + 8, :] for i in range(8)]

        flat, slope = planes_of(lz), planes_of(ld)
        grads = [
            contract(flat, whole, dx.at[b], ly.at[b]),
            contract(flat, whole, lx.at[b], dy.at[b]),
            contract(slope, whole, lx.at[b], ly.at[b]),
        ]
        tile = drecv.at[b] if b != DRIFT else dsend.at[b]
        force = []
        for c in range(3):
            fluid = fbase[b, c : c + 1, :] - grads[c]
            rsend[b, c : c + 1, :] = fluid
            force.append(tile[6:7, :] * (tile[3 + c : 4 + c, :] - fluid))
        forces.append(force)
    backs = [back_copy(b) for b in away]
    for copy in backs:
        copy.start()

    columns_high, columns_low = [], []
    for b in range(REACH):
        rows_ = []
        for c in range(3):
            weighted = wide(forces[b][c]) * ly[b]
            rows_ += [weighted * row_of(lx.at[b], i) for i in range(8)]
        high, low = halves(jnp.concatenate(rows_, axis=0))
        columns_high.append(high)
        columns_low.append(low)
    left = jnp.concatenate(
        [jnp.concatenate(columns_high, axis=1), jnp.concatenate(columns_low, axis=1)], axis=0
    )
    both = lax.dot_general(
        left, lz[...], (((1,), (1,)), ((), ())), preferred_element_type=F32
    )
    drag = both[0:192, 0:128] + both[0:192, 128:256] + both[192:384, 0:128]
    drag = [sum_z(drag[8 * i : 8 * i + 8, :]) for i in range(24)]
    for i in range(24):
        mb[8 * i : 8 * i + 8, :] = drag[i]
    for c in range(3):
        fsend[0, c] = drag[8 * c + 7]
        fsend[1, c] = drag[8 * c]
        fsend[2, c] = mb[pl.ds(64 * c + 7, 8, stride=8), :]
        fsend[3, c] = mb[pl.ds(64 * c, 8, stride=8), :]
    flight4 = copies(fsend, frecv, s4, r4)
    for copy in flight4:
        copy.start()

    for copy in backs:
        copy.wait_recv()
    for b in range(REACH):
        tile = rrecv.at[b] if b != DRIFT else rsend.at[b]
        accel = dprop[b, 0:1, :] * (tile[0:3, :] - dvel[b])
        acc_out[b] = jnp.where(iota(1)[0:3] < cnt[0, 0, b], accel, 0.0)

    for copy in flight4:
        copy.wait_recv()
    for c in range(3):
        value = combine(drag[8 * c : 8 * c + 8], lambda k: frecv.at[k, c], row_of)
        for i in range(8):
            m_out[c, i] = value[i]

    for copy in flight0 + drops + flights[0] + flights[1] + flights[2] + backs + flight4:
        copy.wait_send()


def on_device(source, metric, base, elem, coord, dvel, dprop, counts):
    vmem = pl.BlockSpec(memory_space=pltpu.VMEM)
    smem = pl.BlockSpec(memory_space=pltpu.SMEM)
    dma = pltpu.SemaphoreType.DMA
    elem = elem.reshape(REACH, 1, CAP)
    coord = coord.reshape(REACH, 3, CAP)
    dvel = dvel.reshape(REACH, 3, CAP)
    dprop = dprop.reshape(REACH, 2, CAP)
    tile = (8, 128)
    outs = pl.pallas_call(
        kernel,
        out_shape=(
            jax.ShapeDtypeStruct((8, 8, 128), F32),
            jax.ShapeDtypeStruct((3, 8, 8, 128), F32),
            jax.ShapeDtypeStruct((REACH, 3, CAP), F32),
        ),
        in_specs=[vmem, smem, vmem, vmem, vmem, vmem, vmem, smem, vmem],
        out_specs=(vmem, vmem, vmem),
        scratch_shapes=[
            pltpu.VMEM((64, 128), F32),
            pltpu.VMEM((192, 128), F32),
            pltpu.VMEM((256, 256), BF16),
            pltpu.VMEM((256, REACH * CAP), BF16),
            pltpu.VMEM((256, REACH * CAP), BF16),
            pltpu.VMEM((REACH,) + tile, F32),
            pltpu.VMEM((REACH,) + tile, F32),
            pltpu.VMEM((REACH,) + tile, F32),
            pltpu.VMEM((REACH,) + tile, F32),
            pltpu.VMEM((REACH,) + tile, F32),
            pltpu.VMEM((4, 16, 128), F32),
            pltpu.VMEM((8, 16, 128), F32),
            pltpu.VMEM((SWEEPS, 4) + tile, F32),
            pltpu.VMEM((SWEEPS, 8) + tile, F32),
            pltpu.VMEM((4, 3) + tile, F32),
            pltpu.VMEM((8, 3) + tile, F32),
            pltpu.VMEM((REACH,) + tile, F32),
            pltpu.VMEM((REACH,) + tile, F32),
            pltpu.VMEM((REACH,) + tile, F32),
            pltpu.VMEM((REACH,) + tile, F32),
            dma((8,)),
            dma((8,)),
            dma((SWEEPS, 8)),
            dma((SWEEPS, 8)),
            dma((8,)),
            dma((8,)),
            dma((REACH,)),
            dma((REACH,)),
            dma((REACH,)),
            dma((REACH,)),
        ],
        compiler_params=pltpu.CompilerParams(
            collective_id=0, has_side_effects=True, vmem_limit_bytes=32 * 1024 * 1024
        ),
    )(source, metric, base, elem, coord, dvel, dprop, counts, jnp.asarray(constant_tiles()))
    pressure, momentum, accel = outs
    return pressure, momentum, accel[None, None]


def solution(mesh):
    in_specs = (
        P("stream", "cross", None),
        P("stream", "cross", None),
        P(None, "stream", "cross", None),
        P("stream", "cross", None, None),
        P("stream", "cross", None, None, None),
        P("stream", "cross", None, None, None),
        P("stream", "cross", None, None, None),
        P("stream", "cross", None),
    )
    out_specs = (
        P("stream", "cross", None),
        P(None, "stream", "cross", None),
        P("stream", "cross", None, None, None),
    )
    return jax.shard_map(
        on_device, mesh=mesh, in_specs=in_specs, out_specs=out_specs, check_vma=False
    )
```

```python
import functools

import jax
import jax.numpy as jnp
import numpy as np
from jax import lax
from jax.experimental import pallas as pl
from jax.experimental.pallas import tpu as pltpu
from jax.sharding import PartitionSpec as P

SWEEPS = 3
UPPER_BOUND = 2.5
LOWER_BOUND = UPPER_BOUND / 30.0
REACH = 5
DRIFT = 2
CAP = 128
EZ = 16
GLL_POINTS = [
    -1.0,
    -0.8717401485096066,
    -0.5917001814331423,
    -0.2092992179024789,
    0.2092992179024789,
    0.5917001814331423,
    0.8717401485096066,
    1.0,
]
F32 = jnp.float32
BF16 = jnp.bfloat16
MESH = pl.DeviceIdType.MESH

DIRS = [(1, 0), (-1, 0), (0, 1), (0, -1), (1, 1), (1, -1), (-1, 1), (-1, -1)]
SLOT = {d: k for k, d in enumerate(DIRS)}
ORDER = [4, 5, 6, 7, 0, 1, 2, 3]
AWAY = [0, 4, 1, 3]


def legendre_seven(points):
    before = points * 0.0 + 1.0
    current = points
    for order in range(1, 7):
        following = ((2.0 * order + 1.0) * points * current - order * before) / (order + 1.0)
        before = current
        current = following
    return current


def gll_tables():
    nodes = np.array(GLL_POINTS)
    values = legendre_seven(nodes)
    weights = 2.0 / (56.0 * values * values)
    deriv = np.zeros((8, 8))
    for row in range(8):
        for col in range(8):
            if row != col:
                deriv[row, col] = values[row] / (values[col] * (nodes[row] - nodes[col]))
    deriv[0, 0] = -14.0
    deriv[7, 7] = 14.0
    return nodes, weights, deriv


NODES, WEIGHTS, DERIV = gll_tables()
STIFF = DERIV.T @ (WEIGHTS[:, None] * DERIV)
QDIAG = np.diag(STIFF)

PACKED = 5
T_WK, T_QK, T_KT, T_ZM, T_WJ, T_QJ, T_CY, T_DT, T_LAG = 0, 1, 2, 3, 4, 5, 6, 14, 22
TILES = 23


def constant_tiles():
    lane = np.arange(128)
    row = np.arange(8)
    tiles = np.zeros((PACKED, 8, 128))
    tiles[T_WK] = WEIGHTS[lane % 8][None, :]
    tiles[T_QK] = QDIAG[lane % 8][None, :]
    tiles[T_KT] = STIFF[lane % 8, :].T
    last = (lane % 8 == 7) & (lane < 127)
    first = (lane % 8 == 0) & (lane > 0)
    tiles[T_ZM] = (last | first)[None, :]
    columns = tiles[PACKED - 1]
    columns[:, T_WJ] = WEIGHTS
    columns[:, T_QJ] = QDIAG
    for turn in range(8):
        columns[:, T_CY + turn] = STIFF[row, (row - turn) % 8]
        columns[:, T_DT + turn] = DERIV[(row - turn) % 8, row]
    gaps = NODES[:, None] - NODES[None, :] + np.eye(8)
    columns[:, T_LAG] = 1.0 / gaps.prod(1)
    return tiles.astype(np.float32)


def iota(dim):
    return lax.broadcasted_iota(jnp.int32, (8, 128), dim)


def total(terms):
    terms = list(terms)
    while len(terms) > 1:
        pairs = [a + b for a, b in zip(terms[::2], terms[1::2])]
        if len(terms) % 2:
            pairs.append(terms[-1])
        terms = pairs
    return terms[0]


def wide(row):
    return jnp.broadcast_to(row, (8, 128))


def halves(value):
    high = value.astype(BF16)
    return high, (value - high.astype(F32)).astype(BF16)


def stiff_x(u):
    even = [u[m] + u[7 - m] for m in range(4)]
    odd = [u[m] - u[7 - m] for m in range(4)]
    out = [None] * 8
    for i in range(4):
        e = total(float((STIFF[i, m] + STIFF[i, 7 - m]) / 2.0) * even[m] for m in range(4))
        o = total(float((STIFF[i, m] - STIFF[i, 7 - m]) / 2.0) * odd[m] for m in range(4))
        out[i] = e + o
        out[7 - i] = e - o
    return out


def turned(value, tab, first):
    terms = [tab[first] * value]
    for turn in range(1, 8):
        terms.append(tab[first + turn] * pltpu.roll(value, turn, 0))
    return total(terms)


def kernel(
    src_h, met_h, bvel_h, elem_h, coord_h, dvel_h, dprop_h, cnt_h, tab_h,
    p_out, m_out, acc_out,
    src, met, bvel, elem, coord, dvel, dprop, cnt, pack, tab,
    ub, mb, kz, lz, ld, lx, dx, ly, dy, fbase,
    hsend, hrecv, nsend, nrecv, fsend, frecv, dsend, drecv, rsend, rrecv,
    si, s0, r0, s1, r1, s4, r4, sd, rd, sr, rr,
):
    slabs, cols = lax.axis_size("stream"), lax.axis_size("cross")
    slab, col = lax.axis_index("stream"), lax.axis_index("cross")

    loads = [
        pltpu.make_async_copy(far, near, si.at[n])
        for n, (far, near) in enumerate(
            [
                (tab_h, pack), (met_h, met), (src_h, src), (cnt_h, cnt), (elem_h, elem),
                (coord_h, coord), (dvel_h, dvel), (dprop_h, dprop), (bvel_h, bvel),
            ]
        )
    ]
    for load in loads:
        load.start()

    def device(ds, dc):
        return (slab + ds, col + dc)

    def exists(ds, dc):
        found = (slab + ds >= 0) & (slab + ds < slabs)
        return found & (col + dc >= 0) & (col + dc < cols)

    def each(copies, act):
        for copy, there in copies:
            pl.when(there)(functools.partial(act, copy))

    def start(copy):
        copy.start()

    def wait_recv(copy):
        copy.wait_recv()

    def wait_send(copy):
        copy.wait_send()

    inside = (slab >= DRIFT) & (slab < slabs - DRIFT) & (col > 0) & (col < cols - 1)

    @pl.when(jnp.logical_not(inside))
    def _():
        for ref in (hrecv, nrecv, frecv, drecv, rrecv):
            ref[...] = jnp.zeros_like(ref)

    barrier = pltpu.get_barrier_semaphore()
    partners = DIRS + [(2, 0), (-2, 0)]
    greeted = jnp.int32(0)
    for d in partners:
        there = exists(*d)
        greeted += there.astype(jnp.int32)

        @pl.when(there)
        def _():
            pl.semaphore_signal(barrier, inc=1, device_id=device(*d), device_id_type=MESH)

    sub, lane = iota(0), iota(1)
    perm = jnp.clip(
        lane + jnp.where(lane % 8 == 7, 1, 0) - jnp.where(lane % 8 == 0, 1, 0), 0, 127
    )
    elane = lane // 8
    top, bottom = sub == 0, sub == 7

    loads[0].wait()
    tab[0:4] = pack[0:4]
    columns = pack[PACKED - 1]
    for t in range(T_WJ, TILES):
        tab[t] = wide(columns[:, t : t + 1])
    wk, wj = pack[T_WK], tab[T_WJ]

    def sum_z(value):
        return value + tab[T_ZM] * jnp.take_along_axis(value, perm, axis=1)

    def edges(low, high):
        return jnp.where(top, low, jnp.where(bottom, high, 0.0))

    def row_of(ref, i):
        return wide(ref[i : i + 1, :])

    loads[1].wait()
    amet = jnp.zeros((8, 128), F32)
    for e in range(EZ):
        amet = jnp.where(elane == e, met[0, 0, e], amet)
    loads[2].wait()
    rhs = [sum_z(wk * src[i]) for i in range(8)]

    for i in range(8):
        ub[8 * i : 8 * i + 8, :] = rhs[i]
    hsend[0, 0:8, :] = rhs[7]
    hsend[1, 0:8, :] = rhs[0]
    hsend[2, 0:8, :] = ub[pl.ds(7, 8, stride=8), :]
    hsend[3, 0:8, :] = ub[pl.ds(0, 8, stride=8), :]
    for k in range(4):
        hsend[k, 8:16, :] = amet

    def tile_of(d):
        return SLOT[(d[0], 0)] if d[0] else SLOT[d]

    def copies(send, recv, send_sems, recv_sems, order):
        sent = [
            pltpu.make_async_remote_copy(
                src_ref=send.at[tile_of(DIRS[k])],
                dst_ref=recv.at[k],
                send_sem=send_sems.at[k],
                recv_sem=recv_sems.at[k],
                device_id=device(*DIRS[k]),
                device_id_type=MESH,
            )
            for k in order
        ]
        to = [exists(*DIRS[k]) for k in order]
        of = [exists(-DIRS[k][0], -DIRS[k][1]) for k in order]
        return list(zip(sent, to)), list(zip(sent, of))

    def combine(value, recv):
        def face(side):
            near = recv(SLOT[(side, 0)])[0:8, :]
            return near + edges(
                row_of(recv(SLOT[(side, 1)]), 7), row_of(recv(SLOT[(side, -1)]), 0)
            )

        out = []
        for i in range(8):
            term = value[i] + edges(
                row_of(recv(SLOT[(0, 1)]), i), row_of(recv(SLOT[(0, -1)]), i)
            )
            if i == 0:
                term += face(1)
            if i == 7:
                term += face(-1)
            out.append(term)
        return out

    def stage_drops():
        for b in range(REACH):
            for c in range(3):
                dsend[b, c : c + 1, :] = coord[3 * b + c]
                dsend[b, 3 + c : 4 + c, :] = dvel[3 * b + c]
            dsend[b, 6:7, :] = dprop[b, 0:1, :] * dprop[b, 1:2, :]
            dsend[b, 7:8, :] = jnp.where(
                lane[0:1] < cnt[0, 0, b], (elem[b] % EZ).astype(F32), -1.0
            )

    def block_copies(send, recv, send_sems, recv_sems, way):
        sent = [
            pltpu.make_async_remote_copy(
                src_ref=send.at[b],
                dst_ref=recv.at[b],
                send_sem=send_sems.at[b],
                recv_sem=recv_sems.at[b],
                device_id=device(way * (b - DRIFT), 0),
                device_id_type=MESH,
            )
            for b in AWAY
        ]
        to = [exists(way * (b - DRIFT), 0) for b in AWAY]
        of = [exists(-way * (b - DRIFT), 0) for b in AWAY]
        return list(zip(sent, to)), list(zip(sent, of))

    for load in loads[3:8]:
        load.wait()
    stage_drops()

    pl.semaphore_wait(barrier, greeted)
    first_out, first_in = copies(hsend, hrecv, s0, r0, ORDER)
    each(first_out, start)
    drops_out, drops_in = block_copies(dsend, drecv, sd, rd, 1)
    each(drops_out, start)

    khigh, klow = halves(
        jnp.concatenate([jnp.where(elane == e, tab[T_KT], 0.0) for e in range(EZ)], axis=0)
    )
    kz[0:128, 0:128] = khigh
    kz[0:128, 128:256] = klow
    kz[128:256, 0:128] = khigh
    kz[128:256, 128:256] = jnp.zeros((128, 128), BF16)

    def along_z(u):
        high, low = halves(jnp.concatenate(u, axis=0))
        both = jnp.dot(
            jnp.concatenate([high, low], axis=1), kz[...], preferred_element_type=F32
        )
        both = both[:, 0:128] + both[:, 128:256]
        return [both[8 * i : 8 * i + 8, :] for i in range(8)]

    def basis_block(b):
        def basis(r):
            value = tab[T_LAG]
            for m in range(8):
                value = value * jnp.where(sub == m, 1.0, r - float(NODES[m]))
            return value, turned(value, tab, T_DT)

        tile = drecv.at[b] if b != DRIFT else dsend.at[b]
        eid = row_of(tile, 7)
        lx[b], dx[b] = basis(row_of(tile, 0))
        ly[b], dy[b] = basis(row_of(tile, 1))
        span = slice(b * CAP, b * CAP + CAP)
        for part, ref in zip(basis(row_of(tile, 2)), (lz, ld)):
            high = part.astype(BF16).astype(F32)
            for piece, first in ((high, 0), (part - high, 128)):
                spread = jnp.concatenate(
                    [jnp.where(eid == float(e), piece, 0.0) for e in range(EZ)], axis=0
                )
                ref[first : first + 128, span] = spread.astype(BF16)

    def contract(planes, first, second):
        inner = total(row_of(first, i) * planes[i] for i in range(8))
        return jnp.sum(second[...] * inner, axis=0, keepdims=True)

    def stacked(value):
        high, low = halves(value)
        return jnp.concatenate(
            [
                jnp.concatenate([high, high], axis=1),
                jnp.concatenate([low, jnp.zeros_like(low)], axis=1),
            ],
            axis=0,
        )

    def base_values():
        loads[8].wait()
        left = stacked(jnp.concatenate([bvel[c, i] for c in range(3) for i in range(8)], axis=0))
        for b in range(REACH):
            span = slice(b * CAP, b * CAP + CAP)
            both = jnp.dot(left, lz[:, span], preferred_element_type=F32)
            both = both[0:192, :] + both[192:384, :]
            for c in range(3):
                planes = [both[64 * c + 8 * i : 64 * c + 8 * i + 8, :] for i in range(8)]
                fbase[b, c : c + 1, :] = contract(planes, lx.at[b], ly.at[b])

    basis_block(DRIFT)

    each(first_in, wait_recv)
    residual = combine(rhs, lambda k: hrecv.at[k])
    factor = {(0, 0): amet}
    for d in DIRS:
        factor[(-d[0], -d[1])] = row_of(hrecv.at[SLOT[d]], 8)
    own_x = amet + edges(factor[(0, -1)], factor[(0, 1)])
    side_x = {
        side: factor[(side, 0)] + edges(factor[(side, -1)], factor[(side, 1)])
        for side in (-1, 1)
    }
    side_y = edges(factor[(0, -1)], factor[(0, 1)])
    a_sum = [own_x + side_x[-1]] + [own_x] * 6 + [own_x + side_x[1]]
    a_y = [amet + factor[(-1, 0)]] + [amet] * 6 + [amet + factor[(1, 0)]]
    b_y = (
        [side_y + edges(factor[(-1, -1)], factor[(-1, 1)])]
        + [side_y] * 6
        + [side_y + edges(factor[(1, -1)], factor[(1, 1)])]
    )

    def present(ds, dc):
        return exists(ds, dc).astype(F32)

    count_y = 1.0 + edges(present(0, -1), present(0, 1))
    count_x = [1.0 + present(-1, 0)] + [1.0] * 6 + [1.0 + present(1, 0)]

    center = (UPPER_BOUND + LOWER_BOUND) / 2.0
    half_width = (UPPER_BOUND - LOWER_BOUND) / 2.0
    bound = center / half_width
    rho = 1.0 / bound

    wkj = wk * wj
    mass = [wkj * (count_x[i] * count_y) for i in range(8)]
    planes = {}
    for i in (0, 1, 7):
        planes[i] = (sum_z(wk * a_sum[i]), sum_z(tab[T_QK] * a_sum[i] + wk * (count_x[i] * count_y)))
    inv_diag, update = [], []
    for i in range(8):
        w_i, q_i = float(WEIGHTS[i]), float(QDIAG[i])
        first, second = planes[i if i in planes else 1]
        residual[i] = (w_i * wj) * residual[i]
        diagonal = (q_i * wj + w_i * tab[T_QJ]) * first + (w_i * wj) * second
        inv_diag.append(1.0 / diagonal)
        update.append(inv_diag[i] * residual[i] * (1.0 / center))
    iterate = update

    flights = []
    for sweep in range(SWEEPS):
        send, recv = nsend.at[sweep], nrecv.at[sweep]
        for i in range(8):
            ub[8 * i : 8 * i + 8, :] = update[i]
        lines = [ub[pl.ds(j, 8, stride=8), :] for j in range(8)]
        for k, (group, row) in enumerate([(update, 7), (update, 0), (lines, 7), (lines, 0)]):
            send[k] = total(float(STIFF[row, m]) * group[m] for m in range(8))
        out, into = copies(send, recv, s1.at[sweep], r1.at[sweep], [0, 1, 2, 3])
        each(out, start)
        flights.append(out)

        own = []
        flat, across = along_z(update), stiff_x(update)
        for i in range(8):
            w_i = float(WEIGHTS[i])
            own.append(
                wkj * own_x * across[i]
                + (w_i * wk) * a_y[i] * turned(update[i], tab, T_CY)
                + (w_i * wj) * a_sum[i] * flat[i]
                + w_i * mass[i] * update[i]
            )
        if sweep == 0:
            each(drops_in, wait_recv)
            basis_block(1)
            basis_block(3)
        elif sweep == 1:
            basis_block(0)
            basis_block(4)
        elif sweep == 2:
            base_values()

        each(into, wait_recv)
        for i in range(8):
            w_i = float(WEIGHTS[i])
            beside = edges(row_of(recv.at[2], i), row_of(recv.at[3], i))
            own[i] += (w_i * wk) * b_y[i] * beside
        own[0] += wkj * side_x[-1] * recv[0]
        own[7] += wkj * side_x[1] * recv[1]
        rho_next = 1.0 / (2.0 * bound - rho)
        for i in range(8):
            residual[i] = residual[i] - sum_z(own[i])
        update = [
            (rho_next * rho) * update[i]
            + (2.0 * rho_next / half_width) * (inv_diag[i] * residual[i])
            for i in range(8)
        ]
        rho = rho_next
        iterate = [iterate[i] + update[i] for i in range(8)]

    for i in range(8):
        p_out[i] = iterate[i]

    left = stacked(jnp.concatenate([amet * iterate[i] for i in range(8)], axis=0))
    forces = []
    for b in range(REACH):
        span = slice(b * CAP, b * CAP + CAP)

        def planes_of(ref):
            both = jnp.dot(left, ref[:, span], preferred_element_type=F32)
            both = both[0:64, :] + both[64:128, :]
            return [both[8 * i : 8 * i + 8, :] for i in range(8)]

        flat, slope = planes_of(lz), planes_of(ld)
        grads = [
            contract(flat, dx.at[b], ly.at[b]),
            contract(flat, lx.at[b], dy.at[b]),
            contract(slope, lx.at[b], ly.at[b]),
        ]
        tile = drecv.at[b] if b != DRIFT else dsend.at[b]
        force = []
        for c in range(3):
            fluid = fbase[b, c : c + 1, :] - grads[c]
            rsend[b, c : c + 1, :] = fluid
            force.append(tile[6:7, :] * (tile[3 + c : 4 + c, :] - fluid))
        forces.append(force)
    backs_out, backs_in = block_copies(rsend, rrecv, sr, rr, -1)
    each(backs_out, start)

    columns_high, columns_low = [], []
    for b in range(REACH):
        rows_ = []
        for c in range(3):
            weighted = wide(forces[b][c]) * ly[b]
            rows_ += [weighted * row_of(lx.at[b], i) for i in range(8)]
        high, low = halves(jnp.concatenate(rows_, axis=0))
        columns_high.append(high)
        columns_low.append(low)
    left = jnp.concatenate(
        [jnp.concatenate(columns_high, axis=1), jnp.concatenate(columns_low, axis=1)], axis=0
    )
    both = lax.dot_general(
        left, lz[...], (((1,), (1,)), ((), ())), preferred_element_type=F32
    )
    drag = both[0:192, 0:128] + both[0:192, 128:256] + both[192:384, 0:128]
    drag = [sum_z(drag[8 * i : 8 * i + 8, :]) for i in range(24)]
    for i in range(24):
        mb[8 * i : 8 * i + 8, :] = drag[i]
    for c in range(3):
        fsend[0, c] = drag[8 * c + 7]
        fsend[1, c] = drag[8 * c]
        fsend[2, c] = mb[pl.ds(64 * c + 7, 8, stride=8), :]
        fsend[3, c] = mb[pl.ds(64 * c, 8, stride=8), :]
    last_out, last_in = copies(fsend, frecv, s4, r4, ORDER)
    each(last_out, start)

    each(backs_in, wait_recv)
    for b in range(REACH):
        tile = rrecv.at[b] if b != DRIFT else rsend.at[b]
        for c in range(3):
            accel = dprop[b, 0:1, :] * (tile[c : c + 1, :] - dvel[3 * b + c])
            acc_out[3 * b + c] = jnp.where(lane[0:1] < cnt[0, 0, b], accel, 0.0)

    each(last_in, wait_recv)
    for c in range(3):
        value = combine(drag[8 * c : 8 * c + 8], lambda k: frecv.at[k, c])
        for i in range(8):
            m_out[c, i] = value[i]

    for sent in [first_out, drops_out] + flights + [backs_out, last_out]:
        each(sent, wait_send)


def deliver(p_in, m_in, acc_in, p_out, m_out, acc_out, sems):
    copies = [
        pltpu.make_async_copy(near, far, sems.at[n])
        for n, (near, far) in enumerate([(m_in, m_out), (p_in, p_out), (acc_in, acc_out)])
    ]
    for copy in copies:
        copy.start()
    for copy in copies:
        copy.wait()


def on_device(source, metric, base, elem, coord, dvel, dprop, counts):
    vmem = pl.BlockSpec(memory_space=pltpu.VMEM)
    hbm = pl.BlockSpec(memory_space=pltpu.HBM)
    dma = pltpu.SemaphoreType.DMA
    elem = elem.reshape(REACH, 1, CAP)
    coord = coord.reshape(REACH * 3, 1, CAP)
    dvel = dvel.reshape(REACH * 3, 1, CAP)
    dprop = dprop.reshape(REACH, 2, CAP)
    tile = (8, 128)
    blocks = pltpu.VMEM((REACH,) + tile, F32)
    shapes = (
        jax.ShapeDtypeStruct((8, 8, 128), F32),
        jax.ShapeDtypeStruct((3, 8, 8, 128), F32),
        jax.ShapeDtypeStruct((REACH * 3, 1, CAP), F32),
    )
    operands = (source, metric, base, elem, coord, dvel, dprop, counts)
    operands += (jnp.asarray(constant_tiles()),)
    outs = pl.pallas_call(
        kernel,
        out_shape=shapes,
        in_specs=[hbm] * 9,
        out_specs=(vmem,) * 3,
        scratch_shapes=[
            pltpu.VMEM((8, 8, 128), F32),
            pltpu.SMEM((1, 1, EZ), F32),
            pltpu.VMEM((3, 8, 8, 128), F32),
            pltpu.VMEM((REACH, 1, CAP), jnp.int32),
            pltpu.VMEM((REACH * 3, 1, CAP), F32),
            pltpu.VMEM((REACH * 3, 1, CAP), F32),
            pltpu.VMEM((REACH, 2, CAP), F32),
            pltpu.SMEM((1, 1, REACH), jnp.int32),
            pltpu.VMEM((PACKED,) + tile, F32),
            pltpu.VMEM((TILES,) + tile, F32),
            pltpu.VMEM((64, 128), F32),
            pltpu.VMEM((192, 128), F32),
            pltpu.VMEM((256, 256), BF16),
            pltpu.VMEM((256, REACH * CAP), BF16),
            pltpu.VMEM((256, REACH * CAP), BF16),
            blocks,
            blocks,
            blocks,
            blocks,
            blocks,
            pltpu.VMEM((4, 16, 128), F32),
            pltpu.VMEM((8, 16, 128), F32),
            pltpu.VMEM((SWEEPS, 4) + tile, F32),
            pltpu.VMEM((SWEEPS, 4) + tile, F32),
            pltpu.VMEM((4, 3) + tile, F32),
            pltpu.VMEM((8, 3) + tile, F32),
            blocks,
            blocks,
            blocks,
            blocks,
            dma((9,)),
            dma((8,)),
            dma((8,)),
            dma((SWEEPS, 4)),
            dma((SWEEPS, 4)),
            dma((8,)),
            dma((8,)),
            dma((REACH,)),
            dma((REACH,)),
            dma((REACH,)),
            dma((REACH,)),
        ],
        compiler_params=pltpu.CompilerParams(
            collective_id=0, has_side_effects=True, vmem_limit_bytes=32 * 1024 * 1024
        ),
    )(*[pltpu.with_memory_space_constraint(operand, pltpu.HBM) for operand in operands])
    pressure, momentum, accel = pl.pallas_call(
        deliver,
        out_shape=shapes,
        in_specs=[vmem] * 3,
        out_specs=(hbm,) * 3,
        scratch_shapes=[dma((3,))],
        compiler_params=pltpu.CompilerParams(vmem_limit_bytes=1024 * 1024),
    )(*outs)
    return pressure, momentum, accel.reshape(1, 1, REACH, 3, CAP)


def solution(mesh):
    in_specs = (
        P("stream", "cross", None),
        P("stream", "cross", None),
        P(None, "stream", "cross", None),
        P("stream", "cross", None, None),
        P("stream", "cross", None, None, None),
        P("stream", "cross", None, None, None),
        P("stream", "cross", None, None, None),
        P("stream", "cross", None),
    )
    out_specs = (
        P("stream", "cross", None),
        P(None, "stream", "cross", None),
        P("stream", "cross", None, None, None),
    )
    return jax.shard_map(
        on_device, mesh=mesh, in_specs=in_specs, out_specs=out_specs, check_vma=False
    )
```

```python
import functools

import jax
import jax.numpy as jnp
import numpy as np
from jax import lax
from jax.experimental import pallas as pl
from jax.experimental.pallas import tpu as pltpu
from jax.sharding import PartitionSpec as P

SWEEPS = 3
UPPER_BOUND = 2.5
LOWER_BOUND = UPPER_BOUND / 30.0
REACH = 5
DRIFT = 2
CAP = 128
EZ = 16
GLL_POINTS = [
    -1.0,
    -0.8717401485096066,
    -0.5917001814331423,
    -0.2092992179024789,
    0.2092992179024789,
    0.5917001814331423,
    0.8717401485096066,
    1.0,
]
F32 = jnp.float32
BF16 = jnp.bfloat16
MESH = pl.DeviceIdType.MESH

DIRS = [(1, 0), (-1, 0), (0, 1), (0, -1), (1, 1), (1, -1), (-1, 1), (-1, -1)]
SLOT = {d: k for k, d in enumerate(DIRS)}
ORDER = [4, 5, 6, 7, 0, 1, 2, 3]
FACES = DIRS[:4]
CORNERS = DIRS[4:]
PLACE = {(1, 0): 0, (0, 1): 1, (-1, 0): 2, (0, -1): 3}
PAIR = {(1, 1): 0, (-1, 1): 1, (-1, -1): 2, (1, -1): 3}
COEF = {(-1, 0): 0, (1, 0): 2, (0, -1): 4, (0, 1): 6}
AWAY = [0, 4, 1, 3]


def legendre_seven(points):
    before = points * 0.0 + 1.0
    current = points
    for order in range(1, 7):
        following = ((2.0 * order + 1.0) * points * current - order * before) / (order + 1.0)
        before = current
        current = following
    return current


def gll_tables():
    nodes = np.array(GLL_POINTS)
    values = legendre_seven(nodes)
    weights = 2.0 / (56.0 * values * values)
    deriv = np.zeros((8, 8))
    for row in range(8):
        for col in range(8):
            if row != col:
                deriv[row, col] = values[row] / (values[col] * (nodes[row] - nodes[col]))
    deriv[0, 0] = -14.0
    deriv[7, 7] = 14.0
    return nodes, weights, deriv


NODES, WEIGHTS, DERIV = gll_tables()
STIFF = DERIV.T @ (WEIGHTS[:, None] * DERIV)
QDIAG = np.diag(STIFF)

PACKED = 5
T_WK, T_QK, T_KT, T_ZM, T_WJ, T_QJ, T_CY, T_DT, T_LAG, T_END = 0, 1, 2, 3, 4, 5, 6, 14, 22, 23
TILES = 25


def constant_tiles():
    lane = np.arange(128)
    row = np.arange(8)
    tiles = np.zeros((PACKED, 8, 128))
    tiles[T_WK] = WEIGHTS[lane % 8][None, :]
    tiles[T_QK] = QDIAG[lane % 8][None, :]
    tiles[T_KT] = STIFF[lane % 8, :].T
    last = (lane % 8 == 7) & (lane < 127)
    first = (lane % 8 == 0) & (lane > 0)
    tiles[T_ZM] = (last | first)[None, :]
    columns = tiles[PACKED - 1]
    columns[:, T_WJ] = WEIGHTS
    columns[:, T_QJ] = QDIAG
    for turn in range(8):
        columns[:, T_CY + turn] = STIFF[row, (row - turn) % 8]
        columns[:, T_DT + turn] = DERIV[(row - turn) % 8, row]
    gaps = NODES[:, None] - NODES[None, :] + np.eye(8)
    columns[:, T_LAG] = 1.0 / gaps.prod(1)
    columns[0:7, T_END] = STIFF[7, 0:7]
    columns[1:8, T_END + 1] = STIFF[0, 1:8]
    return tiles.astype(np.float32)


def iota(dim):
    return lax.broadcasted_iota(jnp.int32, (8, 128), dim)


def total(terms):
    terms = list(terms)
    while len(terms) > 1:
        pairs = [a + b for a, b in zip(terms[::2], terms[1::2])]
        if len(terms) % 2:
            pairs.append(terms[-1])
        terms = pairs
    return terms[0]


def wide(row):
    return jnp.broadcast_to(row, (8, 128))


def halves(value):
    high = value.astype(BF16)
    return high, (value - high.astype(F32)).astype(BF16)


def stiff_x(u):
    even = [u[m] + u[7 - m] for m in range(4)]
    odd = [u[m] - u[7 - m] for m in range(4)]
    out = [None] * 8
    for i in range(4):
        e = total(float((STIFF[i, m] + STIFF[i, 7 - m]) / 2.0) * even[m] for m in range(4))
        o = total(float((STIFF[i, m] - STIFF[i, 7 - m]) / 2.0) * odd[m] for m in range(4))
        out[i] = e + o
        out[7 - i] = e - o
    return out


def turned(value, tab, first):
    terms = [tab[first] * value]
    for turn in range(1, 8):
        terms.append(tab[first + turn] * pltpu.roll(value, turn, 0))
    return total(terms)


def kernel(
    src_h, met_h, bvel_h, elem_h, coord_h, dvel_h, dprop_h, cnt_h, tab_h,
    p_out, m_out, acc_out,
    src, met, bvel, elem, coord, dvel, dprop, cnt, pack, tab,
    ub, mb, kz, lz, ld, lx, dx, ly, dy, fbase,
    hsend, hrecv, nsend, nrecv, fsend, frecv, dsend, drecv, rsend, rrecv,
    csend, crecv, tsend, trecv, farrecv, crnrecv,
    si, s0, r0, s1, r1, s4, r4, sd, rd, sr, rr, sc, rc, st, rt, sf, rf, sk, rk,
):
    slabs, cols = lax.axis_size("stream"), lax.axis_size("cross")
    slab, col = lax.axis_index("stream"), lax.axis_index("cross")

    loads = [
        pltpu.make_async_copy(far, near, si.at[n])
        for n, (far, near) in enumerate(
            [
                (tab_h, pack), (met_h, met), (src_h, src), (cnt_h, cnt), (elem_h, elem),
                (coord_h, coord), (dvel_h, dvel), (dprop_h, dprop), (bvel_h, bvel),
            ]
        )
    ]
    for load in loads:
        load.start()

    def device(ds, dc):
        return (slab + ds, col + dc)

    def exists(ds, dc):
        found = (slab + ds >= 0) & (slab + ds < slabs)
        return found & (col + dc >= 0) & (col + dc < cols)

    def each(copies, act):
        for copy, there in copies:
            pl.when(there)(functools.partial(act, copy))

    def start(copy):
        copy.start()

    def wait_recv(copy):
        copy.wait_recv()

    def wait_send(copy):
        copy.wait_send()

    inside = (slab >= 2) & (slab < slabs - 2) & (col >= 2) & (col < cols - 2)

    @pl.when(jnp.logical_not(inside))
    def _():
        for ref in (hrecv, nrecv, frecv, drecv, rrecv, crecv, trecv, farrecv, crnrecv):
            ref[...] = jnp.zeros_like(ref)

    barrier = pltpu.get_barrier_semaphore()
    partners = DIRS + [(2, 0), (-2, 0), (0, 2), (0, -2)]
    greeted = jnp.int32(0)
    for d in partners:
        there = exists(*d)
        greeted += there.astype(jnp.int32)

        @pl.when(there)
        def _():
            pl.semaphore_signal(barrier, inc=1, device_id=device(*d), device_id_type=MESH)

    sub, lane = iota(0), iota(1)
    perm = jnp.clip(
        lane + jnp.where(lane % 8 == 7, 1, 0) - jnp.where(lane % 8 == 0, 1, 0), 0, 127
    )
    elane = lane // 8
    top, bottom = sub == 0, sub == 7

    loads[0].wait()
    tab[0:4] = pack[0:4]
    columns = pack[PACKED - 1]
    for t in range(T_WJ, TILES):
        tab[t] = wide(columns[:, t : t + 1])
    wk, wj = pack[T_WK], tab[T_WJ]

    def sum_z(value):
        return value + tab[T_ZM] * jnp.take_along_axis(value, perm, axis=1)

    def edges(low, high):
        return jnp.where(top, low, jnp.where(bottom, high, 0.0))

    def row_of(ref, i):
        return wide(ref[i : i + 1, :])

    loads[1].wait()
    amet = jnp.zeros((8, 128), F32)
    for e in range(EZ):
        amet = jnp.where(elane == e, met[0, 0, e], amet)
    loads[2].wait()
    rhs = [sum_z(wk * src[i]) for i in range(8)]

    for i in range(8):
        ub[8 * i : 8 * i + 8, :] = rhs[i]
    hsend[0, 0:8, :] = rhs[7]
    hsend[1, 0:8, :] = rhs[0]
    hsend[2, 0:8, :] = ub[pl.ds(7, 8, stride=8), :]
    hsend[3, 0:8, :] = ub[pl.ds(0, 8, stride=8), :]
    for k in range(4):
        hsend[k, 8:16, :] = amet

    def tile_of(d):
        return SLOT[(d[0], 0)] if d[0] else SLOT[d]

    def copies(send, recv, send_sems, recv_sems, order):
        sent = [
            pltpu.make_async_remote_copy(
                src_ref=send.at[tile_of(DIRS[k])],
                dst_ref=recv.at[k],
                send_sem=send_sems.at[k],
                recv_sem=recv_sems.at[k],
                device_id=device(*DIRS[k]),
                device_id_type=MESH,
            )
            for k in order
        ]
        to = [exists(*DIRS[k]) for k in order]
        of = [exists(-DIRS[k][0], -DIRS[k][1]) for k in order]
        return list(zip(sent, to)), list(zip(sent, of))

    def combine(value, recv):
        def face(side):
            near = recv(SLOT[(side, 0)])[0:8, :]
            return near + edges(
                row_of(recv(SLOT[(side, 1)]), 7), row_of(recv(SLOT[(side, -1)]), 0)
            )

        out = []
        for i in range(8):
            term = value[i] + edges(
                row_of(recv(SLOT[(0, 1)]), i), row_of(recv(SLOT[(0, -1)]), i)
            )
            if i == 0:
                term += face(1)
            if i == 7:
                term += face(-1)
            out.append(term)
        return out

    def stage_drops():
        for b in range(REACH):
            for c in range(3):
                dsend[b, c : c + 1, :] = coord[3 * b + c]
                dsend[b, 3 + c : 4 + c, :] = dvel[3 * b + c]
            dsend[b, 6:7, :] = dprop[b, 0:1, :] * dprop[b, 1:2, :]
            dsend[b, 7:8, :] = jnp.where(
                lane[0:1] < cnt[0, 0, b], (elem[b] % EZ).astype(F32), -1.0
            )

    def block_copies(send, recv, send_sems, recv_sems, way):
        sent = [
            pltpu.make_async_remote_copy(
                src_ref=send.at[b],
                dst_ref=recv.at[b],
                send_sem=send_sems.at[b],
                recv_sem=recv_sems.at[b],
                device_id=device(way * (b - DRIFT), 0),
                device_id_type=MESH,
            )
            for b in AWAY
        ]
        to = [exists(way * (b - DRIFT), 0) for b in AWAY]
        of = [exists(-way * (b - DRIFT), 0) for b in AWAY]
        return list(zip(sent, to)), list(zip(sent, of))

    for load in loads[3:8]:
        load.wait()
    stage_drops()

    pl.semaphore_wait(barrier, greeted)
    first_out, first_in = copies(hsend, hrecv, s0, r0, ORDER)
    each(first_out, start)
    drops_out, drops_in = block_copies(dsend, drecv, sd, rd, 1)
    each(drops_out, start)

    khigh, klow = halves(
        jnp.concatenate([jnp.where(elane == e, tab[T_KT], 0.0) for e in range(EZ)], axis=0)
    )
    kz[0:128, 0:128] = khigh
    kz[0:128, 128:256] = klow
    kz[128:256, 0:128] = khigh
    kz[128:256, 128:256] = jnp.zeros((128, 128), BF16)

    def along_z(u):
        high, low = halves(jnp.concatenate(u, axis=0))
        both = jnp.dot(
            jnp.concatenate([high, low], axis=1), kz[...], preferred_element_type=F32
        )
        both = both[:, 0:128] + both[:, 128:256]
        return [both[8 * i : 8 * i + 8, :] for i in range(8)]

    def basis_block(b):
        def basis(r):
            value = tab[T_LAG]
            for m in range(8):
                value = value * jnp.where(sub == m, 1.0, r - float(NODES[m]))
            return value, turned(value, tab, T_DT)

        tile = drecv.at[b] if b != DRIFT else dsend.at[b]
        eid = row_of(tile, 7)
        lx[b], dx[b] = basis(row_of(tile, 0))
        ly[b], dy[b] = basis(row_of(tile, 1))
        span = slice(b * CAP, b * CAP + CAP)
        for part, ref in zip(basis(row_of(tile, 2)), (lz, ld)):
            high = part.astype(BF16).astype(F32)
            for piece, first in ((high, 0), (part - high, 128)):
                spread = jnp.concatenate(
                    [jnp.where(eid == float(e), piece, 0.0) for e in range(EZ)], axis=0
                )
                ref[first : first + 128, span] = spread.astype(BF16)

    def contract(planes, first, second):
        inner = total(row_of(first, i) * planes[i] for i in range(8))
        return jnp.sum(second[...] * inner, axis=0, keepdims=True)

    def stacked(value):
        high, low = halves(value)
        return jnp.concatenate(
            [
                jnp.concatenate([high, high], axis=1),
                jnp.concatenate([low, jnp.zeros_like(low)], axis=1),
            ],
            axis=0,
        )

    def base_values():
        loads[8].wait()
        left = stacked(jnp.concatenate([bvel[c, i] for c in range(3) for i in range(8)], axis=0))
        for b in range(REACH):
            span = slice(b * CAP, b * CAP + CAP)
            both = jnp.dot(left, lz[:, span], preferred_element_type=F32)
            both = both[0:192, :] + both[192:384, :]
            for c in range(3):
                planes = [both[64 * c + 8 * i : 64 * c + 8 * i + 8, :] for i in range(8)]
                fbase[b, c : c + 1, :] = contract(planes, lx.at[b], ly.at[b])

    basis_block(DRIFT)

    each(first_in, wait_recv)
    residual = combine(rhs, lambda k: hrecv.at[k])
    factor = {(0, 0): amet}
    for d in DIRS:
        factor[(-d[0], -d[1])] = row_of(hrecv.at[SLOT[d]], 8)
    own_x = amet + edges(factor[(0, -1)], factor[(0, 1)])
    a_y = [amet + factor[(-1, 0)]] + [amet] * 6 + [amet + factor[(1, 0)]]
    side = {
        (t, 0): factor[(t, 0)] + edges(factor[(t, -1)], factor[(t, 1)]) for t in (-1, 1)
    }
    side |= {
        (0, t): factor[(0, t)] + edges(factor[(-1, t)], factor[(1, t)]) for t in (-1, 1)
    }
    a_sum = [own_x + side[(-1, 0)]] + [own_x] * 6 + [own_x + side[(1, 0)]]

    def present(ds, dc):
        return exists(ds, dc).astype(F32)

    count_y = 1.0 + edges(present(0, -1), present(0, 1))
    count_x = [1.0 + present(-1, 0)] + [1.0] * 6 + [1.0 + present(1, 0)]

    center = (UPPER_BOUND + LOWER_BOUND) / 2.0
    half_width = (UPPER_BOUND - LOWER_BOUND) / 2.0
    bound = center / half_width
    rho = 1.0 / bound

    wkj = wk * wj
    mass = [wkj * (count_x[i] * count_y) for i in range(8)]
    planes = {}
    for i in (0, 1, 7):
        planes[i] = (sum_z(wk * a_sum[i]), sum_z(tab[T_QK] * a_sum[i] + wk * (count_x[i] * count_y)))
    inv_diag, update = [], []
    for i in range(8):
        w_i, q_i = float(WEIGHTS[i]), float(QDIAG[i])
        first, second = planes[i if i in planes else 1]
        residual[i] = (w_i * wj) * residual[i]
        diagonal = (q_i * wj + w_i * tab[T_QJ]) * first + (w_i * wj) * second
        inv_diag.append(1.0 / diagonal)
        update.append(inv_diag[i] * residual[i] * (1.0 / center))
    iterate = update

    across = {d: wkj * side[d] for d in FACES}
    for i in range(8):
        mb[8 * i : 8 * i + 8, :] = inv_diag[i]
    inv_face = {
        (-1, 0): inv_diag[0],
        (1, 0): inv_diag[7],
        (0, -1): mb[pl.ds(0, 8, stride=8), :],
        (0, 1): mb[pl.ds(7, 8, stride=8), :],
    }
    for d in FACES:
        csend[COEF[d]] = across[d]
        csend[COEF[d] + 1] = inv_face[d]

    def to_faces(source, recv, send_sems, recv_sems, dirs):
        sent = [
            pltpu.make_async_remote_copy(
                src_ref=source(d),
                dst_ref=recv.at[n],
                send_sem=send_sems.at[n],
                recv_sem=recv_sems.at[n],
                device_id=device(*d),
                device_id_type=MESH,
            )
            for n, d in enumerate(dirs)
        ]
        to = [exists(*d) for d in dirs]
        of = [exists(-d[0], -d[1]) for d in dirs]
        return list(zip(sent, to)), list(zip(sent, of))

    def lines_of(u):
        for i in range(8):
            ub[8 * i : 8 * i + 8, :] = u[i]
        return [ub[pl.ds(j, 8, stride=8), :] for j in range(8)]

    def ends(u, send, inner):
        lines = lines_of(u)
        for d, group, row in (
            ((1, 0), u, 7), ((-1, 0), u, 0), ((0, 1), lines, 7), ((0, -1), lines, 0)
        ):
            send[PLACE[d]] = total(
                float(STIFF[row, m]) * group[m] for m in range(8) if not (inner and m == row)
            )

    def own_part(u):
        flat, slope = along_z(u), stiff_x(u)
        out = []
        for i in range(8):
            w_i = float(WEIGHTS[i])
            out.append(
                sum_z(
                    wkj * own_x * slope[i]
                    + (w_i * wk) * a_y[i] * turned(u[i], tab, T_CY)
                    + (w_i * wj) * a_sum[i] * flat[i]
                    + w_i * mass[i] * u[i]
                )
            )
        return out

    def less_beside(value, flow):
        part = {d: sum_z(across[d] * flow[d]) for d in FACES}
        out = [
            value[i]
            - edges(wide(part[(0, -1)][i : i + 1, :]), wide(part[(0, 1)][i : i + 1, :]))
            for i in range(8)
        ]
        out[0] -= part[(-1, 0)]
        out[7] -= part[(1, 0)]
        return out

    steps = []
    for sweep in range(SWEEPS):
        rho_next = 1.0 / (2.0 * bound - rho)
        steps.append((rho_next * rho, 2.0 * rho_next / half_width))
        rho = rho_next

    def advanced(u, left, step):
        return [step[0] * u[i] + step[1] * (inv_diag[i] * left[i]) for i in range(8)]

    def opposite(d):
        return (-d[0], -d[1])

    ends(update, nsend.at[0], False)
    near_out, near_in = to_faces(
        lambda d: nsend.at[0, PLACE[d]], nrecv.at[0], s1.at[0], r1.at[0], FACES
    )
    each(near_out, start)
    coef_out, coef_in = to_faces(lambda d: csend, crecv, sc, rc, FACES)
    each(coef_out, start)
    own = own_part(update)
    residual = [residual[i] - own[i] for i in range(8)]
    each(drops_in, wait_recv)
    basis_block(1)
    basis_block(3)
    each(near_in, wait_recv)
    residual = less_beside(residual, {opposite(d): nrecv[0, n] for n, d in enumerate(FACES)})
    update = advanced(update, residual, steps[0])
    iterate = [iterate[i] + update[i] for i in range(8)]
    flights = [near_out, coef_out]

    send = nsend.at[1]
    ends(update, send, False)
    send[4] = send[0]
    far_out, far_in = to_faces(
        lambda d: send.at[PLACE[(d[0] // 2, d[1] // 2)]],
        farrecv, sf, rf, [(2 * x, 2 * y) for x, y in FACES],
    )
    corner_out, corner_in = to_faces(
        lambda d: send.at[pl.ds(PAIR[d], 2)], crnrecv, sk, rk, CORNERS
    )
    near_out, near_in = to_faces(lambda d: send.at[PLACE[d]], nrecv.at[1], s1.at[1], r1.at[1], FACES)
    each(far_out, start)
    each(corner_out, start)
    each(near_out, start)
    own = own_part(update)
    residual = [residual[i] - own[i] for i in range(8)]
    ends(advanced(update, residual, steps[1]), tsend, True)
    tilde_out, tilde_in = to_faces(lambda d: tsend.at[PLACE[d]], trecv, st, rt, FACES)
    each(tilde_out, start)
    flights += [far_out, corner_out, near_out, tilde_out]
    basis_block(0)
    basis_block(4)
    base_values()

    each(near_in, wait_recv)
    residual = less_beside(residual, {opposite(d): nrecv[1, n] for n, d in enumerate(FACES)})
    update = advanced(update, residual, steps[1])
    iterate = [iterate[i] + update[i] for i in range(8)]
    lines = lines_of(update)
    own = own_part(update)
    residual = [residual[i] - own[i] for i in range(8)]

    for arrived in (coef_in, far_in, corner_in, tilde_in):
        each(arrived, wait_recv)

    def from_corner(at, along):
        d = opposite(at)
        return crnrecv[CORNERS.index(d), (PLACE[along] - PAIR[d]) % 4]

    flow = {}
    for n, d in enumerate(FACES):
        at = opposite(d)
        coef = crecv.at[n]

        def change(face, across_it):
            spread = sum_z(coef[COEF[face]] * across_it)
            return (-steps[1][1]) * (coef[COEF[face] + 1] * spread)

        forward = d[0] + d[1] > 0
        far_weight = float(STIFF[7, 0] if forward else STIFF[0, 7])
        near_weight = float(STIFF[7, 7] if forward else STIFF[0, 0])
        weights = tab[T_END if forward else T_END + 1]
        rims = []
        for t in (-1, 1):
            rim = (0, t) if d[0] else (t, 0)
            corner = (at[0] + rim[0], at[1] + rim[1])
            changed = change(rim, from_corner(corner, opposite(rim)))
            rims.append(wide(jnp.sum(weights * changed, axis=0, keepdims=True)))
        if d[0]:
            shared = update[0 if forward else 7]
        else:
            shared = lines[0 if forward else 7]
        flow[at] = (
            trecv[n] + far_weight * change(at, farrecv[n]) + edges(*rims) + near_weight * shared
        )
    residual = less_beside(residual, flow)
    update = advanced(update, residual, steps[2])
    iterate = [iterate[i] + update[i] for i in range(8)]

    for i in range(8):
        p_out[i] = iterate[i]

    left = stacked(jnp.concatenate([amet * iterate[i] for i in range(8)], axis=0))
    forces = []
    for b in range(REACH):
        span = slice(b * CAP, b * CAP + CAP)

        def planes_of(ref):
            both = jnp.dot(left, ref[:, span], preferred_element_type=F32)
            both = both[0:64, :] + both[64:128, :]
            return [both[8 * i : 8 * i + 8, :] for i in range(8)]

        flat, slope = planes_of(lz), planes_of(ld)
        grads = [
            contract(flat, dx.at[b], ly.at[b]),
            contract(flat, lx.at[b], dy.at[b]),
            contract(slope, lx.at[b], ly.at[b]),
        ]
        tile = drecv.at[b] if b != DRIFT else dsend.at[b]
        force = []
        for c in range(3):
            fluid = fbase[b, c : c + 1, :] - grads[c]
            rsend[b, c : c + 1, :] = fluid
            force.append(tile[6:7, :] * (tile[3 + c : 4 + c, :] - fluid))
        forces.append(force)
    backs_out, backs_in = block_copies(rsend, rrecv, sr, rr, -1)
    each(backs_out, start)

    columns_high, columns_low = [], []
    for b in range(REACH):
        rows_ = []
        for c in range(3):
            weighted = wide(forces[b][c]) * ly[b]
            rows_ += [weighted * row_of(lx.at[b], i) for i in range(8)]
        high, low = halves(jnp.concatenate(rows_, axis=0))
        columns_high.append(high)
        columns_low.append(low)
    left = jnp.concatenate(
        [jnp.concatenate(columns_high, axis=1), jnp.concatenate(columns_low, axis=1)], axis=0
    )
    both = lax.dot_general(
        left, lz[...], (((1,), (1,)), ((), ())), preferred_element_type=F32
    )
    drag = both[0:192, 0:128] + both[0:192, 128:256] + both[192:384, 0:128]
    drag = [sum_z(drag[8 * i : 8 * i + 8, :]) for i in range(24)]
    for i in range(24):
        mb[8 * i : 8 * i + 8, :] = drag[i]
    for c in range(3):
        fsend[0, c] = drag[8 * c + 7]
        fsend[1, c] = drag[8 * c]
        fsend[2, c] = mb[pl.ds(64 * c + 7, 8, stride=8), :]
        fsend[3, c] = mb[pl.ds(64 * c, 8, stride=8), :]
    last_out, last_in = copies(fsend, frecv, s4, r4, ORDER)
    each(last_out, start)

    each(backs_in, wait_recv)
    for b in range(REACH):
        tile = rrecv.at[b] if b != DRIFT else rsend.at[b]
        for c in range(3):
            accel = dprop[b, 0:1, :] * (tile[c : c + 1, :] - dvel[3 * b + c])
            acc_out[3 * b + c] = jnp.where(lane[0:1] < cnt[0, 0, b], accel, 0.0)

    each(last_in, wait_recv)
    for c in range(3):
        value = combine(drag[8 * c : 8 * c + 8], lambda k: frecv.at[k, c])
        for i in range(8):
            m_out[c, i] = value[i]

    for sent in [first_out, drops_out] + flights + [backs_out, last_out]:
        each(sent, wait_send)


def deliver(p_in, m_in, acc_in, p_out, m_out, acc_out, sems):
    copies = [
        pltpu.make_async_copy(near, far, sems.at[n])
        for n, (near, far) in enumerate([(m_in, m_out), (p_in, p_out), (acc_in, acc_out)])
    ]
    for copy in copies:
        copy.start()
    for copy in copies:
        copy.wait()


def on_device(source, metric, base, elem, coord, dvel, dprop, counts):
    vmem = pl.BlockSpec(memory_space=pltpu.VMEM)
    hbm = pl.BlockSpec(memory_space=pltpu.HBM)
    dma = pltpu.SemaphoreType.DMA
    elem = elem.reshape(REACH, 1, CAP)
    coord = coord.reshape(REACH * 3, 1, CAP)
    dvel = dvel.reshape(REACH * 3, 1, CAP)
    dprop = dprop.reshape(REACH, 2, CAP)
    tile = (8, 128)
    blocks = pltpu.VMEM((REACH,) + tile, F32)
    shapes = (
        jax.ShapeDtypeStruct((8, 8, 128), F32),
        jax.ShapeDtypeStruct((3, 8, 8, 128), F32),
        jax.ShapeDtypeStruct((REACH * 3, 1, CAP), F32),
    )
    operands = (source, metric, base, elem, coord, dvel, dprop, counts)
    operands += (jnp.asarray(constant_tiles()),)
    outs = pl.pallas_call(
        kernel,
        out_shape=shapes,
        in_specs=[hbm] * 9,
        out_specs=(vmem,) * 3,
        scratch_shapes=[
            pltpu.VMEM((8, 8, 128), F32),
            pltpu.SMEM((1, 1, EZ), F32),
            pltpu.VMEM((3, 8, 8, 128), F32),
            pltpu.VMEM((REACH, 1, CAP), jnp.int32),
            pltpu.VMEM((REACH * 3, 1, CAP), F32),
            pltpu.VMEM((REACH * 3, 1, CAP), F32),
            pltpu.VMEM((REACH, 2, CAP), F32),
            pltpu.SMEM((1, 1, REACH), jnp.int32),
            pltpu.VMEM((PACKED,) + tile, F32),
            pltpu.VMEM((TILES,) + tile, F32),
            pltpu.VMEM((64, 128), F32),
            pltpu.VMEM((192, 128), F32),
            pltpu.VMEM((256, 256), BF16),
            pltpu.VMEM((256, REACH * CAP), BF16),
            pltpu.VMEM((256, REACH * CAP), BF16),
            blocks,
            blocks,
            blocks,
            blocks,
            blocks,
            pltpu.VMEM((4, 16, 128), F32),
            pltpu.VMEM((8, 16, 128), F32),
            pltpu.VMEM((2, 5) + tile, F32),
            pltpu.VMEM((2, 4) + tile, F32),
            pltpu.VMEM((4, 3) + tile, F32),
            pltpu.VMEM((8, 3) + tile, F32),
            blocks,
            blocks,
            blocks,
            blocks,
            pltpu.VMEM((8,) + tile, F32),
            pltpu.VMEM((4, 8) + tile, F32),
            pltpu.VMEM((4,) + tile, F32),
            pltpu.VMEM((4,) + tile, F32),
            pltpu.VMEM((4,) + tile, F32),
            pltpu.VMEM((4, 2) + tile, F32),
            dma((9,)),
            dma((8,)),
            dma((8,)),
            dma((2, 4)),
            dma((2, 4)),
            dma((8,)),
            dma((8,)),
            dma((REACH,)),
            dma((REACH,)),
            dma((REACH,)),
            dma((REACH,)),
            dma((4,)),
            dma((4,)),
            dma((4,)),
            dma((4,)),
            dma((4,)),
            dma((4,)),
            dma((4,)),
            dma((4,)),
        ],
        compiler_params=pltpu.CompilerParams(
            collective_id=0, has_side_effects=True, vmem_limit_bytes=32 * 1024 * 1024
        ),
    )(*[pltpu.with_memory_space_constraint(operand, pltpu.HBM) for operand in operands])
    pressure, momentum, accel = pl.pallas_call(
        deliver,
        out_shape=shapes,
        in_specs=[vmem] * 3,
        out_specs=(hbm,) * 3,
        scratch_shapes=[dma((3,))],
        compiler_params=pltpu.CompilerParams(vmem_limit_bytes=1024 * 1024),
    )(*outs)
    return pressure, momentum, accel.reshape(1, 1, REACH, 3, CAP)


def solution(mesh):
    in_specs = (
        P("stream", "cross", None),
        P("stream", "cross", None),
        P(None, "stream", "cross", None),
        P("stream", "cross", None, None),
        P("stream", "cross", None, None, None),
        P("stream", "cross", None, None, None),
        P("stream", "cross", None, None, None),
        P("stream", "cross", None),
    )
    out_specs = (
        P("stream", "cross", None),
        P(None, "stream", "cross", None),
        P("stream", "cross", None, None, None),
    )
    return jax.shard_map(
        on_device, mesh=mesh, in_specs=in_specs, out_specs=out_specs, check_vma=False
    )
```

```python
import jax
import jax.numpy as jnp
import numpy as np
from jax import lax
from jax.experimental import pallas as pl
from jax.experimental.pallas import tpu as pltpu
from jax.sharding import PartitionSpec as P

SWEEPS = 3
UPPER_BOUND = 2.5
LOWER_BOUND = UPPER_BOUND / 30.0
REACH = 5
DRIFT = 2
CAP = 128
EZ = 16
GLL_POINTS = [
    -1.0,
    -0.8717401485096066,
    -0.5917001814331423,
    -0.2092992179024789,
    0.2092992179024789,
    0.5917001814331423,
    0.8717401485096066,
    1.0,
]
F32 = jnp.float32
BF16 = jnp.bfloat16
MESH = pl.DeviceIdType.MESH

FACES = [(1, 0), (-1, 0), (0, 1), (0, -1)]
CORNERS = [(1, 1), (1, -1), (-1, 1), (-1, -1)]
AWAY = [0, 4, 1, 3]
PLACE = {(1, 0): 0, (0, 1): 1, (-1, 0): 2, (0, -1): 3}
PAIR = {(1, 1): 0, (-1, 1): 1, (-1, -1): 2, (1, -1): 3}
COEF = {(-1, 0): 0, (1, 0): 2, (0, -1): 4, (0, 1): 6}
AWAY = [0, 4, 1, 3]


def legendre_seven(points):
    before = points * 0.0 + 1.0
    current = points
    for order in range(1, 7):
        following = ((2.0 * order + 1.0) * points * current - order * before) / (order + 1.0)
        before = current
        current = following
    return current


def gll_tables():
    nodes = np.array(GLL_POINTS)
    values = legendre_seven(nodes)
    weights = 2.0 / (56.0 * values * values)
    deriv = np.zeros((8, 8))
    for row in range(8):
        for col in range(8):
            if row != col:
                deriv[row, col] = values[row] / (values[col] * (nodes[row] - nodes[col]))
    deriv[0, 0] = -14.0
    deriv[7, 7] = 14.0
    return nodes, weights, deriv


NODES, WEIGHTS, DERIV = gll_tables()
STIFF = DERIV.T @ (WEIGHTS[:, None] * DERIV)
QDIAG = np.diag(STIFF)

PACKED = 5
T_WK, T_QK, T_KT, T_ZM, T_WJ, T_QJ, T_CY, T_DT, T_LAG, T_END = 0, 1, 2, 3, 4, 5, 6, 14, 22, 23
TILES = 25


def constant_tiles():
    lane = np.arange(128)
    row = np.arange(8)
    tiles = np.zeros((PACKED, 8, 128))
    tiles[T_WK] = WEIGHTS[lane % 8][None, :]
    tiles[T_QK] = QDIAG[lane % 8][None, :]
    tiles[T_KT] = STIFF[lane % 8, :].T
    last = (lane % 8 == 7) & (lane < 127)
    first = (lane % 8 == 0) & (lane > 0)
    tiles[T_ZM] = (last | first)[None, :]
    columns = tiles[PACKED - 1]
    columns[:, T_WJ] = WEIGHTS
    columns[:, T_QJ] = QDIAG
    for turn in range(8):
        columns[:, T_CY + turn] = STIFF[row, (row - turn) % 8]
        columns[:, T_DT + turn] = DERIV[(row - turn) % 8, row]
    gaps = NODES[:, None] - NODES[None, :] + np.eye(8)
    columns[:, T_LAG] = 1.0 / gaps.prod(1)
    columns[0:7, T_END] = STIFF[7, 0:7]
    columns[1:8, T_END + 1] = STIFF[0, 1:8]
    return tiles.astype(np.float32)


def iota(dim):
    return lax.broadcasted_iota(jnp.int32, (8, 128), dim)


def total(terms):
    terms = list(terms)
    while len(terms) > 1:
        pairs = [a + b for a, b in zip(terms[::2], terms[1::2])]
        if len(terms) % 2:
            pairs.append(terms[-1])
        terms = pairs
    return terms[0]


def wide(row):
    return jnp.broadcast_to(row, (8, 128))


def halves(value):
    high = value.astype(BF16)
    return high, (value - high.astype(F32)).astype(BF16)


def stiff_x(u):
    even = [u[m] + u[7 - m] for m in range(4)]
    odd = [u[m] - u[7 - m] for m in range(4)]
    out = [None] * 8
    for i in range(4):
        e = total(float((STIFF[i, m] + STIFF[i, 7 - m]) / 2.0) * even[m] for m in range(4))
        o = total(float((STIFF[i, m] - STIFF[i, 7 - m]) / 2.0) * odd[m] for m in range(4))
        out[i] = e + o
        out[7 - i] = e - o
    return out


def turned(value, tab, first):
    terms = [tab[first] * value]
    for turn in range(1, 8):
        terms.append(tab[first + turn] * pltpu.roll(value, turn, 0))
    return total(terms)


def kernel(
    src_h, met_h, bvel_h, elem_h, coord_h, dvel_h, dprop_h, cnt_h, tab_h,
    p_out, m_out, acc_out,
    src, met, bvel, elem, coord, dvel, dprop, cnt, pack, tab,
    ub, mb, kz, lz, ld, lx, dx, ly, dy, fbase,
    hsend, hrecv, hcs, hcr, nsend, nrecv, fsend, frecv, fcs, fcr,
    dsend, drecv, rsend, rrecv, csend, crecv, tsend, trecv, grecv, zeros, zero_rows,
    *rest,
):
    *spare, ledger, load_ledger, si, send_sems, recv_sems = rest
    slabs, cols = lax.axis_size("stream"), lax.axis_size("cross")
    slab, col = lax.axis_index("stream"), lax.axis_index("cross")

    loads = [
        pltpu.make_async_copy(far, near, si.at[n])
        for far, near, n in [
            (tab_h, pack, 0), (src_h, src, 1), (met_h, met, 2), (cnt_h, cnt, 3), (elem_h, elem, 4),
            (coord_h, coord, 4), (dvel_h, dvel, 4), (dprop_h, dprop, 4), (bvel_h, bvel, 5),
        ]
    ]
    for load in loads:
        load.start()

    def device(ds, dc):
        return (slab + ds, col + dc)

    def exists(ds, dc):
        found = (slab + ds >= 0) & (slab + ds < slabs)
        return found & (col + dc >= 0) & (col + dc < cols)

    inside = (slab >= 2) & (slab < slabs - 2) & (col >= 2) & (col < cols - 2)
    groups = []

    class Group:
        def __init__(self, recv, messages):
            self.recv, self.messages = recv, messages
            self.sem = recv_sems.at[len(groups)]
            self.spare = spare[len(groups)]
            groups.append(self)

        def start(self):
            for d, source, slot in self.messages:
                copy = pltpu.make_async_remote_copy(
                    src_ref=source,
                    dst_ref=self.recv.at[slot],
                    send_sem=send_sems.at[0],
                    recv_sem=self.sem,
                    device_id=device(*d),
                    device_id_type=MESH,
                )
                pl.when(exists(*d))(copy.start)

        def wait(self):
            pltpu.make_async_copy(self.recv, self.recv, self.sem).wait()

        def fill(self):
            for d, _, slot in self.messages:
                near, away = self.recv.at[slot], self.spare.at[slot]
                pool = zero_rows if near.shape[-2] == 1 else zeros
                none = pool.at[0] if len(near.shape) == 2 else pool.at[pl.ds(0, near.shape[0])]
                pl.when(jnp.logical_not(exists(-d[0], -d[1])))(
                    pltpu.make_async_copy(none, near, self.sem).start
                )
                pl.when(jnp.logical_not(exists(*d)))(
                    pltpu.make_async_copy(none, away, send_sems.at[0]).start
                )

    barrier = pltpu.get_barrier_semaphore()
    partners = FACES + CORNERS + [(2, 0), (-2, 0), (0, 2), (0, -2)]
    greeted = jnp.int32(0)
    for d in partners:
        there = exists(*d)
        greeted += there.astype(jnp.int32)

        @pl.when(there)
        def _():
            pl.semaphore_signal(barrier, inc=1, device_id=device(*d), device_id_type=MESH)

    sub, lane = iota(0), iota(1)
    perm = jnp.clip(
        lane + jnp.where(lane % 8 == 7, 1, 0) - jnp.where(lane % 8 == 0, 1, 0), 0, 127
    )
    elane = lane // 8
    top, bottom = sub == 0, sub == 7

    loads[0].wait()
    tab[0:4] = pack[0:4]
    columns = pack[PACKED - 1]
    for t in range(T_WJ, TILES):
        tab[t] = wide(columns[:, t : t + 1])
    wk, wj = pack[T_WK], tab[T_WJ]

    def sum_z(value):
        return value + tab[T_ZM] * jnp.take_along_axis(value, perm, axis=1)

    def edges(low, high):
        return jnp.where(top, low, jnp.where(bottom, high, 0.0))

    def row_of(ref, i):
        return wide(ref[i : i + 1, :])

    loads[2].wait()
    amet = jnp.zeros((8, 128), F32)
    for e in range(EZ):
        amet = jnp.where(elane == e, met[0, 0, e], amet)
    loads[1].wait()
    rhs = [sum_z(wk * src[i]) for i in range(8)]

    def lines_of(u):
        for i in range(8):
            ub[8 * i : 8 * i + 8, :] = u[i]
        return [ub[pl.ds(j, 8, stride=8), :] for j in range(8)]

    def edge_row(d):
        return 7 if d > 0 else 0

    lines = lines_of(rhs)
    for n, d in enumerate(FACES):
        hsend[n, 0] = (rhs if d[0] else lines)[edge_row(d[0] + d[1])]
        hsend[n, 1] = amet
    for n, d in enumerate(CORNERS):
        row = edge_row(d[1])
        hcs[n, 0] = rhs[edge_row(d[0])][row : row + 1, :]
        hcs[n, 1] = amet[0:1, :]

    def slots(dirs, source):
        return [(d, source(n, d), n) for n, d in enumerate(dirs)]

    blocks_to = [((b - DRIFT, 0), dsend.at[b], n) for n, b in enumerate(AWAY)]
    blocks_back = [((DRIFT - b, 0), rsend.at[b], n) for n, b in enumerate(AWAY)]
    first, second = nsend.at[0], nsend.at[1]
    heads = Group(hrecv, slots(FACES, lambda n, d: hsend.at[n]))
    head_corners = Group(hcr, slots(CORNERS, lambda n, d: hcs.at[n]))
    drops = Group(drecv, blocks_to)
    near_one = Group(nrecv.at[0], slots(FACES, lambda n, d: first.at[PLACE[d]]))
    coefs = Group(crecv, slots(FACES, lambda n, d: csend))
    near_two = Group(nrecv.at[1], slots(FACES, lambda n, d: second.at[PLACE[d]]))
    far_two = Group(
        grecv,
        [((2 * d[0], 2 * d[1]), second.at[PLACE[d]], n) for n, d in enumerate(FACES)]
        + [(d, second.at[pl.ds(PAIR[d], 2)], pl.ds(4 + 2 * n, 2)) for n, d in enumerate(CORNERS)],
    )
    tilde = Group(trecv, slots(FACES, lambda n, d: tsend.at[PLACE[d]]))
    backs = Group(rrecv, blocks_back)
    tails = Group(frecv, slots(FACES, lambda n, d: fsend.at[n]))
    tail_corners = Group(fcr, slots(CORNERS, lambda n, d: fcs.at[n]))

    @pl.when(jnp.logical_not(inside))
    def _():
        zeros[...] = jnp.zeros_like(zeros)
        zero_rows[...] = jnp.zeros_like(zero_rows)
        for group in groups:
            group.fill()

    def combine(value, recv, corner):
        def face(t):
            return recv(FACES.index((t, 0))) + edges(
                wide(corner(CORNERS.index((t, 1)))), wide(corner(CORNERS.index((t, -1))))
            )

        low, high = recv(FACES.index((0, 1))), recv(FACES.index((0, -1)))
        out = []
        for i in range(8):
            term = value[i] + edges(wide(low[i : i + 1, :]), wide(high[i : i + 1, :]))
            if i == 0:
                term += face(1)
            if i == 7:
                term += face(-1)
            out.append(term)
        return out

    def stage_drops():
        for b in range(REACH):
            for c in range(3):
                dsend[b, c : c + 1, :] = coord[3 * b + c]
                dsend[b, 3 + c : 4 + c, :] = dvel[3 * b + c]
            dsend[b, 6:7, :] = dprop[b, 0:1, :] * dprop[b, 1:2, :]
            dsend[b, 7:8, :] = jnp.where(
                lane[0:1] < cnt[0, 0, b], (elem[b] % EZ).astype(F32), -1.0
            )

    loads[3].wait()
    pltpu.make_async_copy(load_ledger, load_ledger, si.at[4]).wait()
    stage_drops()

    pl.semaphore_wait(barrier, greeted)
    head_corners.start()
    heads.start()
    drops.start()

    khigh, klow = halves(
        jnp.concatenate([jnp.where(elane == e, tab[T_KT], 0.0) for e in range(EZ)], axis=0)
    )
    kz[0:128, 0:128] = khigh
    kz[0:128, 128:256] = klow
    kz[128:256, 0:128] = khigh
    kz[128:256, 128:256] = jnp.zeros((128, 128), BF16)

    def along_z(u):
        high, low = halves(jnp.concatenate(u, axis=0))
        both = jnp.dot(
            jnp.concatenate([high, low], axis=1), kz[...], preferred_element_type=F32
        )
        both = both[:, 0:128] + both[:, 128:256]
        return [both[8 * i : 8 * i + 8, :] for i in range(8)]

    def block_of(arrived, own, b):
        return own.at[b] if b == DRIFT else arrived.at[AWAY.index(b)]

    def basis_block(b):
        def basis(r):
            value = tab[T_LAG]
            for m in range(8):
                value = value * jnp.where(sub == m, 1.0, r - float(NODES[m]))
            return value, turned(value, tab, T_DT)

        tile = block_of(drecv, dsend, b)
        eid = row_of(tile, 7)
        lx[b], dx[b] = basis(row_of(tile, 0))
        ly[b], dy[b] = basis(row_of(tile, 1))
        span = slice(b * CAP, b * CAP + CAP)
        for part, ref in zip(basis(row_of(tile, 2)), (lz, ld)):
            high = part.astype(BF16).astype(F32)
            for piece, first in ((high, 0), (part - high, 128)):
                spread = jnp.concatenate(
                    [jnp.where(eid == float(e), piece, 0.0) for e in range(EZ)], axis=0
                )
                ref[first : first + 128, span] = spread.astype(BF16)

    def contract(planes, first, second):
        inner = total(row_of(first, i) * planes[i] for i in range(8))
        return jnp.sum(second[...] * inner, axis=0, keepdims=True)

    def stacked(value):
        high, low = halves(value)
        return jnp.concatenate(
            [
                jnp.concatenate([high, high], axis=1),
                jnp.concatenate([low, jnp.zeros_like(low)], axis=1),
            ],
            axis=0,
        )

    def base_values():
        loads[8].wait()
        left = stacked(jnp.concatenate([bvel[c, i] for c in range(3) for i in range(8)], axis=0))
        for b in range(REACH):
            span = slice(b * CAP, b * CAP + CAP)
            both = jnp.dot(left, lz[:, span], preferred_element_type=F32)
            both = both[0:192, :] + both[192:384, :]
            for c in range(3):
                planes = [both[64 * c + 8 * i : 64 * c + 8 * i + 8, :] for i in range(8)]
                fbase[b, c : c + 1, :] = contract(planes, lx.at[b], ly.at[b])

    basis_block(DRIFT)

    heads.wait()
    head_corners.wait()
    residual = combine(rhs, lambda n: hrecv[n, 0], lambda n: hcr[n, 0])
    factor = {(0, 0): amet}
    for n, d in enumerate(FACES):
        factor[(-d[0], -d[1])] = hrecv[n, 1]
    for n, d in enumerate(CORNERS):
        factor[(-d[0], -d[1])] = wide(hcr[n, 1])
    own_x = amet + edges(factor[(0, -1)], factor[(0, 1)])
    a_y = [amet + factor[(-1, 0)]] + [amet] * 6 + [amet + factor[(1, 0)]]
    side = {
        (t, 0): factor[(t, 0)] + edges(factor[(t, -1)], factor[(t, 1)]) for t in (-1, 1)
    }
    side |= {
        (0, t): factor[(0, t)] + edges(factor[(-1, t)], factor[(1, t)]) for t in (-1, 1)
    }
    a_sum = [own_x + side[(-1, 0)]] + [own_x] * 6 + [own_x + side[(1, 0)]]

    def present(ds, dc):
        return exists(ds, dc).astype(F32)

    count_y = 1.0 + edges(present(0, -1), present(0, 1))
    count_x = [1.0 + present(-1, 0)] + [1.0] * 6 + [1.0 + present(1, 0)]

    center = (UPPER_BOUND + LOWER_BOUND) / 2.0
    half_width = (UPPER_BOUND - LOWER_BOUND) / 2.0
    bound = center / half_width
    rho = 1.0 / bound

    wkj = wk * wj
    mass = [wkj * (count_x[i] * count_y) for i in range(8)]
    planes = {}
    for i in (0, 1, 7):
        planes[i] = (sum_z(wk * a_sum[i]), sum_z(tab[T_QK] * a_sum[i] + wk * (count_x[i] * count_y)))
    inv_diag, update = [], []
    for i in range(8):
        w_i, q_i = float(WEIGHTS[i]), float(QDIAG[i])
        plane, mixed = planes[i if i in planes else 1]
        residual[i] = (w_i * wj) * residual[i]
        diagonal = (q_i * wj + w_i * tab[T_QJ]) * plane + (w_i * wj) * mixed
        inv_diag.append(1.0 / diagonal)
        update.append(inv_diag[i] * residual[i] * (1.0 / center))
    iterate = update

    across = {d: wkj * side[d] for d in FACES}
    for i in range(8):
        mb[8 * i : 8 * i + 8, :] = inv_diag[i]
    inv_face = {
        (-1, 0): inv_diag[0],
        (1, 0): inv_diag[7],
        (0, -1): mb[pl.ds(0, 8, stride=8), :],
        (0, 1): mb[pl.ds(7, 8, stride=8), :],
    }
    for d in FACES:
        csend[COEF[d]] = across[d]
        csend[COEF[d] + 1] = inv_face[d]

    def ends(u, send, inner):
        lines = lines_of(u)
        for d, group, row in (
            ((1, 0), u, 7), ((-1, 0), u, 0), ((0, 1), lines, 7), ((0, -1), lines, 0)
        ):
            send[PLACE[d]] = total(
                float(STIFF[row, m]) * group[m] for m in range(8) if not (inner and m == row)
            )

    def own_part(u):
        flat, slope = along_z(u), stiff_x(u)
        out = []
        for i in range(8):
            w_i = float(WEIGHTS[i])
            out.append(
                sum_z(
                    wkj * own_x * slope[i]
                    + (w_i * wk) * a_y[i] * turned(u[i], tab, T_CY)
                    + (w_i * wj) * a_sum[i] * flat[i]
                    + w_i * mass[i] * u[i]
                )
            )
        return out

    def less_beside(value, flow):
        part = {d: sum_z(across[d] * flow[d]) for d in FACES}
        out = [
            value[i]
            - edges(wide(part[(0, -1)][i : i + 1, :]), wide(part[(0, 1)][i : i + 1, :]))
            for i in range(8)
        ]
        out[0] -= part[(-1, 0)]
        out[7] -= part[(1, 0)]
        return out

    steps = []
    for sweep in range(SWEEPS):
        rho_next = 1.0 / (2.0 * bound - rho)
        steps.append((rho_next * rho, 2.0 * rho_next / half_width))
        rho = rho_next

    def advanced(u, left, step):
        return [step[0] * u[i] + step[1] * (inv_diag[i] * left[i]) for i in range(8)]

    def opposite(d):
        return (-d[0], -d[1])

    ends(update, first, False)
    near_one.start()
    own = own_part(update)
    residual = [residual[i] - own[i] for i in range(8)]
    coefs.start()
    drops.wait()
    basis_block(1)
    basis_block(3)
    near_one.wait()
    residual = less_beside(residual, {opposite(d): nrecv[0, n] for n, d in enumerate(FACES)})
    update = advanced(update, residual, steps[0])
    iterate = [iterate[i] + update[i] for i in range(8)]

    ends(update, second, False)
    second[4] = second[0]
    near_two.start()
    far_two.start()
    own = own_part(update)
    residual = [residual[i] - own[i] for i in range(8)]
    ends(advanced(update, residual, steps[1]), tsend, True)
    tilde.start()
    basis_block(0)
    basis_block(4)
    base_values()

    near_two.wait()
    residual = less_beside(residual, {opposite(d): nrecv[1, n] for n, d in enumerate(FACES)})
    update = advanced(update, residual, steps[1])
    iterate = [iterate[i] + update[i] for i in range(8)]
    lines = lines_of(update)
    own = own_part(update)
    residual = [residual[i] - own[i] for i in range(8)]

    for group in (coefs, far_two, tilde):
        group.wait()

    def from_corner(at, along):
        d = opposite(at)
        return grecv[4 + 2 * CORNERS.index(d) + (PLACE[along] - PAIR[d]) % 4]

    flow = {}
    for n, d in enumerate(FACES):
        at = opposite(d)
        coef = crecv.at[n]

        def change(face, across_it):
            spread = sum_z(coef[COEF[face]] * across_it)
            return (-steps[1][1]) * (coef[COEF[face] + 1] * spread)

        forward = d[0] + d[1] > 0
        far_weight = float(STIFF[7, 0] if forward else STIFF[0, 7])
        near_weight = float(STIFF[7, 7] if forward else STIFF[0, 0])
        weights = tab[T_END if forward else T_END + 1]
        rims = []
        for t in (-1, 1):
            rim = (0, t) if d[0] else (t, 0)
            corner = (at[0] + rim[0], at[1] + rim[1])
            changed = change(rim, from_corner(corner, opposite(rim)))
            rims.append(wide(jnp.sum(weights * changed, axis=0, keepdims=True)))
        if d[0]:
            shared = update[0 if forward else 7]
        else:
            shared = lines[0 if forward else 7]
        flow[at] = (
            trecv[n] + far_weight * change(at, grecv[n]) + edges(*rims) + near_weight * shared
        )
    residual = less_beside(residual, flow)
    update = advanced(update, residual, steps[2])
    iterate = [iterate[i] + update[i] for i in range(8)]

    for i in range(8):
        p_out[i] = iterate[i]

    left = stacked(jnp.concatenate([amet * iterate[i] for i in range(8)], axis=0))
    forces = []
    for b in range(REACH):
        span = slice(b * CAP, b * CAP + CAP)

        def planes_of(ref):
            both = jnp.dot(left, ref[:, span], preferred_element_type=F32)
            both = both[0:64, :] + both[64:128, :]
            return [both[8 * i : 8 * i + 8, :] for i in range(8)]

        flat, slope = planes_of(lz), planes_of(ld)
        grads = [
            contract(flat, dx.at[b], ly.at[b]),
            contract(flat, lx.at[b], dy.at[b]),
            contract(slope, lx.at[b], ly.at[b]),
        ]
        tile = block_of(drecv, dsend, b)
        force = []
        for c in range(3):
            fluid = fbase[b, c : c + 1, :] - grads[c]
            rsend[b, c : c + 1, :] = fluid
            force.append(tile[6:7, :] * (tile[3 + c : 4 + c, :] - fluid))
        forces.append(force)
    backs.start()

    columns_high, columns_low = [], []
    for b in range(REACH):
        rows_ = []
        for c in range(3):
            weighted = wide(forces[b][c]) * ly[b]
            rows_ += [weighted * row_of(lx.at[b], i) for i in range(8)]
        high, low = halves(jnp.concatenate(rows_, axis=0))
        columns_high.append(high)
        columns_low.append(low)
    left = jnp.concatenate(
        [jnp.concatenate(columns_high, axis=1), jnp.concatenate(columns_low, axis=1)], axis=0
    )
    both = lax.dot_general(
        left, lz[...], (((1,), (1,)), ((), ())), preferred_element_type=F32
    )
    drag = both[0:192, 0:128] + both[0:192, 128:256] + both[192:384, 0:128]
    drag = [sum_z(drag[8 * i : 8 * i + 8, :]) for i in range(24)]
    for i in range(24):
        mb[8 * i : 8 * i + 8, :] = drag[i]
    for c in range(3):
        for n, d in enumerate(CORNERS):
            row = edge_row(d[1])
            fcs[n, c] = drag[8 * c + edge_row(d[0])][row : row + 1, :]
        for n, d in enumerate(FACES):
            row = edge_row(d[0] + d[1])
            if d[0]:
                fsend[n, c] = drag[8 * c + row]
            else:
                fsend[n, c] = mb[pl.ds(64 * c + row, 8, stride=8), :]
    tail_corners.start()
    tails.start()

    backs.wait()
    for b in range(REACH):
        tile = block_of(rrecv, rsend, b)
        for c in range(3):
            accel = dprop[b, 0:1, :] * (tile[c : c + 1, :] - dvel[3 * b + c])
            acc_out[3 * b + c] = jnp.where(lane[0:1] < cnt[0, 0, b], accel, 0.0)

    tails.wait()
    tail_corners.wait()
    for c in range(3):
        value = combine(
            drag[8 * c : 8 * c + 8], lambda n: frecv[n, c], lambda n: fcr[n, c]
        )
        for i in range(8):
            m_out[c, i] = value[i]

    pltpu.make_async_copy(ledger, ledger, send_sems.at[0]).wait()


def deliver(p_in, m_in, acc_in, p_out, m_out, acc_out, sems):
    copies = [
        pltpu.make_async_copy(near, far, sems.at[n])
        for n, (near, far) in enumerate([(m_in, m_out), (p_in, p_out), (acc_in, acc_out)])
    ]
    for copy in copies:
        copy.start()
    for copy in copies:
        copy.wait()


def on_device(source, metric, base, elem, coord, dvel, dprop, counts):
    vmem = pl.BlockSpec(memory_space=pltpu.VMEM)
    hbm = pl.BlockSpec(memory_space=pltpu.HBM)
    dma = pltpu.SemaphoreType.DMA
    elem = elem.reshape(REACH, 1, CAP)
    coord = coord.reshape(REACH * 3, 1, CAP)
    dvel = dvel.reshape(REACH * 3, 1, CAP)
    dprop = dprop.reshape(REACH, 2, CAP)
    tile = (8, 128)
    row = (1, 128)
    blocks = pltpu.VMEM((REACH,) + tile, F32)
    arrive_shapes = [
        (4, 2) + tile, (4, 2) + row, (4,) + tile, (4,) + tile, (4, 8) + tile, (4,) + tile,
        (12,) + tile, (4,) + tile, (4,) + tile, (4, 3) + tile, (4, 3) + row,
    ]
    arrive = [pltpu.VMEM(shape, F32) for shape in arrive_shapes]
    total_rows = sum(int(np.prod(shape)) for shape in arrive_shapes) // 128
    shapes = (
        jax.ShapeDtypeStruct((8, 8, 128), F32),
        jax.ShapeDtypeStruct((3, 8, 8, 128), F32),
        jax.ShapeDtypeStruct((REACH * 3, 1, CAP), F32),
    )
    operands = (source, metric, base, elem, coord, dvel, dprop, counts)
    operands += (jnp.asarray(constant_tiles()),)
    outs = pl.pallas_call(
        kernel,
        out_shape=shapes,
        in_specs=[hbm] * 9,
        out_specs=(vmem,) * 3,
        scratch_shapes=[
            pltpu.VMEM((8, 8, 128), F32),
            pltpu.SMEM((1, 1, EZ), F32),
            pltpu.VMEM((3, 8, 8, 128), F32),
            pltpu.VMEM((REACH, 1, CAP), jnp.int32),
            pltpu.VMEM((REACH * 3, 1, CAP), F32),
            pltpu.VMEM((REACH * 3, 1, CAP), F32),
            pltpu.VMEM((REACH, 2, CAP), F32),
            pltpu.SMEM((1, 1, REACH), jnp.int32),
            pltpu.VMEM((PACKED,) + tile, F32),
            pltpu.VMEM((TILES,) + tile, F32),
            pltpu.VMEM((64, 128), F32),
            pltpu.VMEM((192, 128), F32),
            pltpu.VMEM((256, 256), BF16),
            pltpu.VMEM((256, REACH * CAP), BF16),
            pltpu.VMEM((256, REACH * CAP), BF16),
            blocks,
            blocks,
            blocks,
            blocks,
            blocks,
            pltpu.VMEM((4, 2) + tile, F32),
            arrive[0],
            pltpu.VMEM((4, 2) + row, F32),
            arrive[1],
            pltpu.VMEM((2, 5) + tile, F32),
            pltpu.VMEM((2, 4) + tile, F32),
            pltpu.VMEM((4, 3) + tile, F32),
            arrive[9],
            pltpu.VMEM((4, 3) + row, F32),
            arrive[10],
            blocks,
            arrive[2],
            blocks,
            arrive[8],
            pltpu.VMEM((8,) + tile, F32),
            arrive[4],
            pltpu.VMEM((4,) + tile, F32),
            arrive[7],
            arrive[6],
            pltpu.VMEM((8,) + tile, F32),
            pltpu.VMEM((3,) + row, F32),
            *arrive,
            pltpu.VMEM((total_rows,) + row, F32),
            pltpu.VMEM((REACH * 9,) + row, F32),
            dma((6,)),
            dma((1,)),
            dma((len(arrive),)),
        ],
        compiler_params=pltpu.CompilerParams(
            collective_id=0, has_side_effects=True, vmem_limit_bytes=32 * 1024 * 1024
        ),
    )(*[pltpu.with_memory_space_constraint(operand, pltpu.HBM) for operand in operands])
    pressure, momentum, accel = pl.pallas_call(
        deliver,
        out_shape=shapes,
        in_specs=[vmem] * 3,
        out_specs=(hbm,) * 3,
        scratch_shapes=[dma((3,))],
        compiler_params=pltpu.CompilerParams(vmem_limit_bytes=1024 * 1024),
    )(*outs)
    return pressure, momentum, accel.reshape(1, 1, REACH, 3, CAP)


def solution(mesh):
    in_specs = (
        P("stream", "cross", None),
        P("stream", "cross", None),
        P(None, "stream", "cross", None),
        P("stream", "cross", None, None),
        P("stream", "cross", None, None, None),
        P("stream", "cross", None, None, None),
        P("stream", "cross", None, None, None),
        P("stream", "cross", None),
    )
    out_specs = (
        P("stream", "cross", None),
        P(None, "stream", "cross", None),
        P("stream", "cross", None, None, None),
    )
    return jax.shard_map(
        on_device, mesh=mesh, in_specs=in_specs, out_specs=out_specs, check_vma=False
    )
```

```python
import jax
import jax.numpy as jnp
import numpy as np
from jax import lax
from jax.experimental import pallas as pl
from jax.experimental.pallas import tpu as pltpu
from jax.sharding import PartitionSpec as P

SWEEPS = 3
UPPER_BOUND = 2.5
LOWER_BOUND = UPPER_BOUND / 30.0
REACH = 5
DRIFT = 2
CAP = 128
EZ = 16
GLL_POINTS = [
    -1.0,
    -0.8717401485096066,
    -0.5917001814331423,
    -0.2092992179024789,
    0.2092992179024789,
    0.5917001814331423,
    0.8717401485096066,
    1.0,
]
F32 = jnp.float32
BF16 = jnp.bfloat16
MESH = pl.DeviceIdType.MESH

FACES = [(1, 0), (-1, 0), (0, 1), (0, -1)]
CORNERS = [(1, 1), (1, -1), (-1, 1), (-1, -1)]
FAR = [(2, 0), (-2, 0), (0, 2), (0, -2)]
FAR_CORNERS = [(2, 1), (2, -1), (-2, 1), (-2, -1), (1, 2), (1, -2), (-1, 2), (-1, -2)]
AWAY = [0, 4, 1, 3]
PLACE = {(1, 0): 0, (0, 1): 1, (-1, 0): 2, (0, -1): 3}
PAIR = {(1, 1): 0, (-1, 1): 1, (-1, -1): 2, (1, -1): 3}


def legendre_seven(points):
    before = points * 0.0 + 1.0
    current = points
    for order in range(1, 7):
        following = ((2.0 * order + 1.0) * points * current - order * before) / (order + 1.0)
        before = current
        current = following
    return current


def gll_tables():
    nodes = np.array(GLL_POINTS)
    values = legendre_seven(nodes)
    weights = 2.0 / (56.0 * values * values)
    deriv = np.zeros((8, 8))
    for row in range(8):
        for col in range(8):
            if row != col:
                deriv[row, col] = values[row] / (values[col] * (nodes[row] - nodes[col]))
    deriv[0, 0] = -14.0
    deriv[7, 7] = 14.0
    return nodes, weights, deriv


NODES, WEIGHTS, DERIV = gll_tables()
STIFF = DERIV.T @ (WEIGHTS[:, None] * DERIV)
QDIAG = np.diag(STIFF)

PACKED = 5
T_WK, T_QK, T_KT, T_ZM, T_WJ, T_QJ, T_CY, T_DT, T_LAG, T_END = 0, 1, 2, 3, 4, 5, 6, 14, 22, 23
TILES = 27


def constant_tiles():
    lane = np.arange(128)
    row = np.arange(8)
    tiles = np.zeros((PACKED, 8, 128))
    tiles[T_WK] = WEIGHTS[lane % 8][None, :]
    tiles[T_QK] = QDIAG[lane % 8][None, :]
    tiles[T_KT] = STIFF[lane % 8, :].T
    last = (lane % 8 == 7) & (lane < 127)
    first = (lane % 8 == 0) & (lane > 0)
    tiles[T_ZM] = (last | first)[None, :]
    columns = tiles[PACKED - 1]
    columns[:, T_WJ] = WEIGHTS
    columns[:, T_QJ] = QDIAG
    for turn in range(8):
        columns[:, T_CY + turn] = STIFF[row, (row - turn) % 8]
        columns[:, T_DT + turn] = DERIV[(row - turn) % 8, row]
    gaps = NODES[:, None] - NODES[None, :] + np.eye(8)
    columns[:, T_LAG] = 1.0 / gaps.prod(1)
    columns[0:7, T_END] = STIFF[7, 0:7]
    columns[1:8, T_END + 1] = STIFF[0, 1:8]
    columns[1:7, T_END + 2] = STIFF[7, 1:7]
    columns[1:7, T_END + 3] = STIFF[0, 1:7]
    return tiles.astype(np.float32)


def iota(dim):
    return lax.broadcasted_iota(jnp.int32, (8, 128), dim)


def total(terms):
    terms = list(terms)
    while len(terms) > 1:
        pairs = [a + b for a, b in zip(terms[::2], terms[1::2])]
        if len(terms) % 2:
            pairs.append(terms[-1])
        terms = pairs
    return terms[0]


def wide(row):
    return jnp.broadcast_to(row, (8, 128))


def halves(value):
    high = value.astype(BF16)
    return high, (value - high.astype(F32)).astype(BF16)


def stiff_x(u):
    even = [u[m] + u[7 - m] for m in range(4)]
    odd = [u[m] - u[7 - m] for m in range(4)]
    out = [None] * 8
    for i in range(4):
        e = total(float((STIFF[i, m] + STIFF[i, 7 - m]) / 2.0) * even[m] for m in range(4))
        o = total(float((STIFF[i, m] - STIFF[i, 7 - m]) / 2.0) * odd[m] for m in range(4))
        out[i] = e + o
        out[7 - i] = e - o
    return out


def turned(value, tab, first):
    terms = [tab[first] * value]
    for turn in range(1, 8):
        terms.append(tab[first + turn] * pltpu.roll(value, turn, 0))
    return total(terms)


def kernel(
    src_h, met_h, bvel_h, elem_h, coord_h, dvel_h, dprop_h, cnt_h, tab_h,
    p_out, m_out, acc_out,
    src, met, bvel, elem, coord, dvel, dprop, cnt, pack, tab,
    ub, mb, kz, lz, ld, lx, dx, ly, dy, fbase,
    hsend, hrecv, hcs, hcr, hfr, hrs, hrr, nsend, nrecv, fsend, frecv, fcs, fcr,
    dsend, drecv, rsend, rrecv, tsend, trecv, grecv, zeros, zero_rows,
    *rest,
):
    *spare, ledger, load_ledger, si, send_sems, recv_sems = rest
    slabs, cols = lax.axis_size("stream"), lax.axis_size("cross")
    slab, col = lax.axis_index("stream"), lax.axis_index("cross")

    loads = [
        pltpu.make_async_copy(far, near, si.at[n])
        for far, near, n in [
            (tab_h, pack, 0), (src_h, src, 1), (met_h, met, 2), (cnt_h, cnt, 3), (elem_h, elem, 4),
            (coord_h, coord, 4), (dvel_h, dvel, 4), (dprop_h, dprop, 4), (bvel_h, bvel, 5),
        ]
    ]
    for load in loads:
        load.start()

    def device(ds, dc):
        return (slab + ds, col + dc)

    def exists(ds, dc):
        found = (slab + ds >= 0) & (slab + ds < slabs)
        return found & (col + dc >= 0) & (col + dc < cols)

    inside = (slab >= 2) & (slab < slabs - 2) & (col >= 2) & (col < cols - 2)
    groups = []

    class Group:
        def __init__(self, recv, messages):
            self.recv, self.messages = recv, messages
            self.sem = recv_sems.at[len(groups)]
            self.spare = spare[len(groups)]
            groups.append(self)

        def start(self):
            for d, source, slot in self.messages:
                copy = pltpu.make_async_remote_copy(
                    src_ref=source,
                    dst_ref=self.recv.at[slot],
                    send_sem=send_sems.at[0],
                    recv_sem=self.sem,
                    device_id=device(*d),
                    device_id_type=MESH,
                )
                pl.when(exists(*d))(copy.start)

        def wait(self):
            pltpu.make_async_copy(self.recv, self.recv, self.sem).wait()

        def fill(self):
            for d, _, slot in self.messages:
                near, away = self.recv.at[slot], self.spare.at[slot]
                pool = zero_rows if near.shape[-2] == 1 else zeros
                none = pool.at[0] if len(near.shape) == 2 else pool.at[pl.ds(0, near.shape[0])]
                pl.when(jnp.logical_not(exists(-d[0], -d[1])))(
                    pltpu.make_async_copy(none, near, self.sem).start
                )
                pl.when(jnp.logical_not(exists(*d)))(
                    pltpu.make_async_copy(none, away, send_sems.at[0]).start
                )

    barrier = pltpu.get_barrier_semaphore()
    partners = FACES + CORNERS + FAR + FAR_CORNERS
    greeted = jnp.int32(0)
    for d in partners:
        there = exists(*d)
        greeted += there.astype(jnp.int32)

        @pl.when(there)
        def _():
            pl.semaphore_signal(barrier, inc=1, device_id=device(*d), device_id_type=MESH)

    sub, lane = iota(0), iota(1)
    perm = jnp.clip(
        lane + jnp.where(lane % 8 == 7, 1, 0) - jnp.where(lane % 8 == 0, 1, 0), 0, 127
    )
    elane = lane // 8
    top, bottom = sub == 0, sub == 7

    loads[0].wait()
    tab[0:4] = pack[0:4]
    columns = pack[PACKED - 1]
    for t in range(T_WJ, TILES):
        tab[t] = wide(columns[:, t : t + 1])
    wk, wj = pack[T_WK], tab[T_WJ]

    def sum_z(value):
        return value + tab[T_ZM] * jnp.take_along_axis(value, perm, axis=1)

    def edges(low, high):
        return jnp.where(top, low, jnp.where(bottom, high, 0.0))

    def row_of(ref, i):
        return wide(ref[i : i + 1, :])

    loads[2].wait()
    amet = jnp.zeros((8, 128), F32)
    for e in range(EZ):
        amet = jnp.where(elane == e, met[0, 0, e], amet)
    loads[1].wait()
    rhs = [sum_z(wk * src[i]) for i in range(8)]

    def lines_of(u):
        for i in range(8):
            ub[8 * i : 8 * i + 8, :] = u[i]
        return [ub[pl.ds(j, 8, stride=8), :] for j in range(8)]

    def edge_row(d):
        return 7 if d > 0 else 0

    def ends(u, group_range):
        lines = lines_of(u)
        return {
            d: total(float(STIFF[row, m]) * group[m] for m in group_range(row))
            for d, group, row in (
                ((1, 0), u, 7), ((-1, 0), u, 0), ((0, 1), lines, 7), ((0, -1), lines, 0)
            )
        }

    def opposite(d):
        return (-d[0], -d[1])

    center = (UPPER_BOUND + LOWER_BOUND) / 2.0
    half_width = (UPPER_BOUND - LOWER_BOUND) / 2.0
    bound = center / half_width
    rho = 1.0 / bound
    qk, qj = tab[T_QK], tab[T_QJ]
    plane, mixed = sum_z(wk * amet), sum_z(qk * amet + wk)
    early = []
    for i in range(8):
        w_i, q_i = float(WEIGHTS[i]), float(QDIAG[i])
        diagonal = (q_i * wj + w_i * qj) * plane + (w_i * wj) * mixed
        early.append((w_i / center) * (wj * rhs[i]) / diagonal)
    middle = ends(early, lambda row: range(1, 7))

    lines = lines_of(rhs)
    skin = {d: (rhs if d[0] else lines)[edge_row(d[0] + d[1])] for d in FACES}
    for n, d in enumerate(FACES):
        for f in FACES:
            hsend[n, PLACE[f]] = skin[f]
        hsend[n, 4] = jnp.where(top, amet, middle[d])
        hrs[n, 0] = amet[0:1, :]
        hrs[n, 1] = amet[0:1, :]
    for n, d in enumerate(CORNERS):
        hcs[n, 0] = skin[(d[0], 0)]
        hcs[n, 1] = jnp.where(sub == edge_row(d[0]), amet, skin[(0, d[1])])
    for n, d in enumerate(FAR_CORNERS):
        if abs(d[0]) == 2:
            face, row = skin[(d[0] // 2, 0)], edge_row(d[1])
        else:
            face, row = skin[(0, d[1] // 2)], edge_row(d[0])
        hrs[4 + n, 0] = face[row : row + 1, :]
        hrs[4 + n, 1] = amet[0:1, :]

    def slots(dirs, source):
        return [(d, source(n, d), n) for n, d in enumerate(dirs)]

    blocks_to = [((b - DRIFT, 0), dsend.at[b], n) for n, b in enumerate(AWAY)]
    blocks_back = [((DRIFT - b, 0), rsend.at[b], n) for n, b in enumerate(AWAY)]
    heads = Group(hrecv, slots(FACES, lambda n, d: hsend.at[n]))
    head_corners = Group(hcr, slots(CORNERS, lambda n, d: hcs.at[n]))
    head_far = Group(
        hfr, [(d, hsend.at[0, PLACE[(d[0] // 2, d[1] // 2)]], n) for n, d in enumerate(FAR)]
    )
    head_rows = Group(hrr, slots(FAR + FAR_CORNERS, lambda n, d: hrs.at[n]))
    drops = Group(drecv, blocks_to)
    near_two = Group(nrecv, slots(FACES, lambda n, d: nsend.at[PLACE[d]]))
    far_two = Group(
        grecv,
        [(d, nsend.at[PLACE[(d[0] // 2, d[1] // 2)]], n) for n, d in enumerate(FAR)]
        + [(d, nsend.at[pl.ds(PAIR[d], 2)], pl.ds(4 + 2 * n, 2)) for n, d in enumerate(CORNERS)],
    )
    tilde = Group(trecv, slots(FACES, lambda n, d: tsend.at[PLACE[d]]))
    backs = Group(rrecv, blocks_back)
    tails = Group(frecv, slots(FACES, lambda n, d: fsend.at[n]))
    tail_corners = Group(fcr, slots(CORNERS, lambda n, d: fcs.at[n]))

    @pl.when(jnp.logical_not(inside))
    def _():
        zeros[...] = jnp.zeros_like(zeros)
        zero_rows[...] = jnp.zeros_like(zero_rows)
        for group in groups:
            group.fill()

    def combine(value, recv, corner):
        def face(t):
            return recv(FACES.index((t, 0))) + edges(
                wide(corner(CORNERS.index((t, 1)))), wide(corner(CORNERS.index((t, -1))))
            )

        low, high = recv(FACES.index((0, 1))), recv(FACES.index((0, -1)))
        out = []
        for i in range(8):
            term = value[i] + edges(wide(low[i : i + 1, :]), wide(high[i : i + 1, :]))
            if i == 0:
                term += face(1)
            if i == 7:
                term += face(-1)
            out.append(term)
        return out

    def stage_drops():
        for b in range(REACH):
            for c in range(3):
                dsend[b, c : c + 1, :] = coord[3 * b + c]
                dsend[b, 3 + c : 4 + c, :] = dvel[3 * b + c]
            dsend[b, 6:7, :] = dprop[b, 0:1, :] * dprop[b, 1:2, :]
            dsend[b, 7:8, :] = jnp.where(
                lane[0:1] < cnt[0, 0, b], (elem[b] % EZ).astype(F32), -1.0
            )

    loads[3].wait()
    pltpu.make_async_copy(load_ledger, load_ledger, si.at[4]).wait()
    stage_drops()

    pl.semaphore_wait(barrier, greeted)
    head_rows.start()
    head_far.start()
    head_corners.start()
    heads.start()
    drops.start()

    khigh, klow = halves(
        jnp.concatenate([jnp.where(elane == e, tab[T_KT], 0.0) for e in range(EZ)], axis=0)
    )
    kz[0:128, 0:128] = khigh
    kz[0:128, 128:256] = klow
    kz[128:256, 0:128] = khigh
    kz[128:256, 128:256] = jnp.zeros((128, 128), BF16)

    def along_z(u):
        high, low = halves(jnp.concatenate(u, axis=0))
        both = jnp.dot(
            jnp.concatenate([high, low], axis=1), kz[...], preferred_element_type=F32
        )
        both = both[:, 0:128] + both[:, 128:256]
        return [both[8 * i : 8 * i + 8, :] for i in range(8)]

    def block_of(arrived, own, b):
        return own.at[b] if b == DRIFT else arrived.at[AWAY.index(b)]

    def basis_block(b):
        def basis(r):
            value = tab[T_LAG]
            for m in range(8):
                value = value * jnp.where(sub == m, 1.0, r - float(NODES[m]))
            return value, turned(value, tab, T_DT)

        tile = block_of(drecv, dsend, b)
        eid = row_of(tile, 7)
        lx[b], dx[b] = basis(row_of(tile, 0))
        ly[b], dy[b] = basis(row_of(tile, 1))
        span = slice(b * CAP, b * CAP + CAP)
        for part, ref in zip(basis(row_of(tile, 2)), (lz, ld)):
            high = part.astype(BF16).astype(F32)
            for piece, first in ((high, 0), (part - high, 128)):
                spread = jnp.concatenate(
                    [jnp.where(eid == float(e), piece, 0.0) for e in range(EZ)], axis=0
                )
                ref[first : first + 128, span] = spread.astype(BF16)

    def contract(planes, first, second):
        inner = total(row_of(first, i) * planes[i] for i in range(8))
        return jnp.sum(second[...] * inner, axis=0, keepdims=True)

    def stacked(value):
        high, low = halves(value)
        return jnp.concatenate(
            [
                jnp.concatenate([high, high], axis=1),
                jnp.concatenate([low, jnp.zeros_like(low)], axis=1),
            ],
            axis=0,
        )

    def base_values():
        loads[8].wait()
        left = stacked(jnp.concatenate([bvel[c, i] for c in range(3) for i in range(8)], axis=0))
        for b in range(REACH):
            span = slice(b * CAP, b * CAP + CAP)
            both = jnp.dot(left, lz[:, span], preferred_element_type=F32)
            both = both[0:192, :] + both[192:384, :]
            for c in range(3):
                planes = [both[64 * c + 8 * i : 64 * c + 8 * i + 8, :] for i in range(8)]
                fbase[b, c : c + 1, :] = contract(planes, lx.at[b], ly.at[b])

    basis_block(DRIFT)

    for group in (heads, head_corners, head_far, head_rows):
        group.wait()
    skins, factor, middle_of = {}, {(0, 0): amet}, {}
    for n, d in enumerate(FACES):
        at = opposite(d)
        skins[at] = {f: hrecv[n, PLACE[f]] for f in FACES}
        middle_of[at] = hrecv[n, 4]
        factor[at] = wide(middle_of[at][0:1, :])
    for n, d in enumerate(CORNERS):
        row = edge_row(d[0])
        skins[opposite(d)] = {(d[0], 0): hcr[n, 0], (0, d[1]): hcr[n, 1]}
        factor[opposite(d)] = wide(hcr[n, 1, row : row + 1, :])
    point = {}
    for n, d in enumerate(FAR + FAR_CORNERS):
        point[opposite(d)] = wide(hrr[n, 0])
        factor[opposite(d)] = wide(hrr[n, 1])

    def shared_row(n):
        row = edge_row(CORNERS[n][1])
        return hcr[n, 0, row : row + 1, :]

    residual = combine(rhs, lambda n: skins[opposite(FACES[n])][FACES[n]], shared_row)
    own_x = amet + edges(factor[(0, -1)], factor[(0, 1)])
    a_y = [amet + factor[(-1, 0)]] + [amet] * 6 + [amet + factor[(1, 0)]]
    side = {
        (t, 0): factor[(t, 0)] + edges(factor[(t, -1)], factor[(t, 1)]) for t in (-1, 1)
    }
    side |= {
        (0, t): factor[(0, t)] + edges(factor[(-1, t)], factor[(1, t)]) for t in (-1, 1)
    }
    a_sum = [own_x + side[(-1, 0)]] + [own_x] * 6 + [own_x + side[(1, 0)]]

    def present(ds, dc):
        return exists(ds, dc).astype(F32)

    count_y = 1.0 + edges(present(0, -1), present(0, 1))
    count_x = [1.0 + present(-1, 0)] + [1.0] * 6 + [1.0 + present(1, 0)]

    wkj = wk * wj
    mass = [wkj * (count_x[i] * count_y) for i in range(8)]
    planes = {}
    for i in (0, 1, 7):
        planes[i] = (sum_z(wk * a_sum[i]), sum_z(qk * a_sum[i] + wk * (count_x[i] * count_y)))
    inv_diag, update = [], []
    for i in range(8):
        w_i, q_i = float(WEIGHTS[i]), float(QDIAG[i])
        plane, mixed = planes[i if i in planes else 1]
        residual[i] = (w_i * wj) * residual[i]
        diagonal = (q_i * wj + w_i * qj) * plane + (w_i * wj) * mixed
        inv_diag.append(1.0 / diagonal)
        update.append(inv_diag[i] * residual[i] * (1.0 / center))
    iterate = update

    across = {d: wkj * side[d] for d in FACES}
    def own_part(u):
        flat, slope = along_z(u), stiff_x(u)
        out = []
        for i in range(8):
            w_i = float(WEIGHTS[i])
            out.append(
                sum_z(
                    wkj * own_x * slope[i]
                    + (w_i * wk) * a_y[i] * turned(u[i], tab, T_CY)
                    + (w_i * wj) * a_sum[i] * flat[i]
                    + w_i * mass[i] * u[i]
                )
            )
        return out

    def less_beside(value, flow):
        part = {d: sum_z(across[d] * flow[d]) for d in FACES}
        out = [
            value[i]
            - edges(wide(part[(0, -1)][i : i + 1, :]), wide(part[(0, 1)][i : i + 1, :]))
            for i in range(8)
        ]
        out[0] -= part[(-1, 0)]
        out[7] -= part[(1, 0)]
        return out

    steps = []
    for sweep in range(SWEEPS):
        rho_next = 1.0 / (2.0 * bound - rho)
        steps.append((rho_next * rho, 2.0 * rho_next / half_width))
        rho = rho_next

    def advanced(u, left, step):
        return [step[0] * u[i] + step[1] * (inv_diag[i] * left[i]) for i in range(8)]

    def outer(value, a_near, count):
        w_0, q_0 = float(WEIGHTS[0]), float(QDIAG[0])
        diagonal = (q_0 * wj + w_0 * qj) * sum_z(wk * a_near) + (w_0 * wj) * sum_z(
            qk * a_near + wk * jnp.maximum(count, 1.0)
        )
        inverse = 1.0 / diagonal
        return inverse, inverse * (((w_0 / center) * wj) * value)

    def plus(p, q):
        return (p[0] + q[0], p[1] + q[1])

    def rim_of(d, t):
        return (0, t) if d[0] else (t, 0)

    def ordered(at, far, near):
        return edges(far, near) if at[0] + at[1] < 0 else edges(near, far)

    def a_of(*places):
        return total(factor[p] for p in places)

    def n_of(*places):
        return total(present(*p) for p in places)

    shell, flow = {}, {}
    lines = lines_of(update)
    for n, d in enumerate(FACES):
        at = opposite(d)
        far = plus(at, at)
        forward = d[0] + d[1] > 0
        beside = {t: plus(at, rim_of(d, t)) for t in (-1, 1)}
        beyond = {t: plus(far, rim_of(d, t)) for t in (-1, 1)}
        row = edge_row(at[0] + at[1])
        corner_values = [
            wide(skins[beside[t]][opposite(rim_of(d, t))][row : row + 1, :]) + point[beyond[t]]
            for t in (-1, 1)
        ]
        inverse, value = outer(
            skins[at][at] + hfr[n] + edges(*corner_values),
            a_of(at, far) + edges(*[a_of(beside[t], beyond[t]) for t in (-1, 1)]),
            n_of(at, far) + edges(*[n_of(beside[t], beyond[t]) for t in (-1, 1)]),
        )
        weight = wkj * (factor[far] + edges(factor[beyond[-1]], factor[beyond[1]]))
        shell[at, at] = (weight, inverse)
        sums = []
        for t in (-1, 1):
            rim = rim_of(d, t)
            inverse, rim_value = outer(
                skins[at][rim] + skins[beside[t]][opposite(rim)],
                a_of(at, beside[t]) + ordered(at, a_of(far, beyond[t]), a_of((0, 0), rim)),
                n_of(at, beside[t]) + ordered(at, n_of(far, beyond[t]), n_of((0, 0), rim)),
            )
            weight = wkj * (factor[beside[t]] + ordered(at, factor[beyond[t]], factor[rim]))
            shell[at, rim] = (weight, inverse)
            weights = tab[T_END + (2 if forward else 3)]
            sums.append(wide(jnp.sum(weights * rim_value, axis=0, keepdims=True)))
        far_weight = float(STIFF[7, 0] if forward else STIFF[0, 7])
        near_weight = float(STIFF[7, 7] if forward else STIFF[0, 0])
        shared = (update if d[0] else lines)[0 if forward else 7]
        inner = jnp.where(top, sums[0], jnp.where(bottom, sums[1], middle_of[at]))
        flow[at] = inner + far_weight * value + near_weight * shared

    own = own_part(update)
    residual = less_beside([residual[i] - own[i] for i in range(8)], flow)
    update = advanced(update, residual, steps[0])
    iterate = [iterate[i] + update[i] for i in range(8)]

    for d, tile in ends(update, lambda row: range(8)).items():
        nsend[PLACE[d]] = tile
        if PLACE[d] == 0:
            nsend[4] = tile
    near_two.start()
    far_two.start()
    own = own_part(update)
    residual = [residual[i] - own[i] for i in range(8)]
    guess = advanced(update, residual, steps[1])
    for d, tile in ends(guess, lambda row: range(7) if row else range(1, 8)).items():
        tsend[PLACE[d]] = tile
    tilde.start()
    drops.wait()
    for b in AWAY:
        basis_block(b)
    base_values()

    near_two.wait()
    residual = less_beside(residual, {opposite(d): nrecv[n] for n, d in enumerate(FACES)})
    update = advanced(update, residual, steps[1])
    iterate = [iterate[i] + update[i] for i in range(8)]
    lines = lines_of(update)
    own = own_part(update)
    residual = [residual[i] - own[i] for i in range(8)]

    for group in (far_two, tilde):
        group.wait()

    def from_corner(at, along):
        d = opposite(at)
        return grecv[4 + 2 * CORNERS.index(d) + (PLACE[along] - PAIR[d]) % 4]

    flow = {}
    for n, d in enumerate(FACES):
        at = opposite(d)

        def change(face, across_it):
            weight, inverse = shell[at, face]
            return (-steps[1][1]) * (inverse * sum_z(weight * across_it))

        forward = d[0] + d[1] > 0
        far_weight = float(STIFF[7, 0] if forward else STIFF[0, 7])
        near_weight = float(STIFF[7, 7] if forward else STIFF[0, 0])
        weights = tab[T_END if forward else T_END + 1]
        rims = []
        for t in (-1, 1):
            rim = rim_of(d, t)
            corner = plus(at, rim)
            changed = change(rim, from_corner(corner, opposite(rim)))
            rims.append(wide(jnp.sum(weights * changed, axis=0, keepdims=True)))
        if d[0]:
            shared = update[0 if forward else 7]
        else:
            shared = lines[0 if forward else 7]
        flow[at] = (
            trecv[n] + far_weight * change(at, grecv[n]) + edges(*rims) + near_weight * shared
        )
    residual = less_beside(residual, flow)
    update = advanced(update, residual, steps[2])
    iterate = [iterate[i] + update[i] for i in range(8)]

    for i in range(8):
        p_out[i] = iterate[i]

    left = stacked(jnp.concatenate([amet * iterate[i] for i in range(8)], axis=0))
    forces = []
    for b in range(REACH):
        span = slice(b * CAP, b * CAP + CAP)

        def planes_of(ref):
            both = jnp.dot(left, ref[:, span], preferred_element_type=F32)
            both = both[0:64, :] + both[64:128, :]
            return [both[8 * i : 8 * i + 8, :] for i in range(8)]

        flat, slope = planes_of(lz), planes_of(ld)
        grads = [
            contract(flat, dx.at[b], ly.at[b]),
            contract(flat, lx.at[b], dy.at[b]),
            contract(slope, lx.at[b], ly.at[b]),
        ]
        tile = block_of(drecv, dsend, b)
        force = []
        for c in range(3):
            fluid = fbase[b, c : c + 1, :] - grads[c]
            rsend[b, c : c + 1, :] = fluid
            force.append(tile[6:7, :] * (tile[3 + c : 4 + c, :] - fluid))
        forces.append(force)
    backs.start()

    columns_high, columns_low = [], []
    for b in range(REACH):
        rows_ = []
        for c in range(3):
            weighted = wide(forces[b][c]) * ly[b]
            rows_ += [weighted * row_of(lx.at[b], i) for i in range(8)]
        high, low = halves(jnp.concatenate(rows_, axis=0))
        columns_high.append(high)
        columns_low.append(low)
    left = jnp.concatenate(
        [jnp.concatenate(columns_high, axis=1), jnp.concatenate(columns_low, axis=1)], axis=0
    )
    both = lax.dot_general(
        left, lz[...], (((1,), (1,)), ((), ())), preferred_element_type=F32
    )
    drag = both[0:192, 0:128] + both[0:192, 128:256] + both[192:384, 0:128]
    drag = [sum_z(drag[8 * i : 8 * i + 8, :]) for i in range(24)]
    for i in range(24):
        mb[8 * i : 8 * i + 8, :] = drag[i]
    for c in range(3):
        for n, d in enumerate(CORNERS):
            row = edge_row(d[1])
            fcs[n, c] = drag[8 * c + edge_row(d[0])][row : row + 1, :]
        for n, d in enumerate(FACES):
            row = edge_row(d[0] + d[1])
            if d[0]:
                fsend[n, c] = drag[8 * c + row]
            else:
                fsend[n, c] = mb[pl.ds(64 * c + row, 8, stride=8), :]
    tail_corners.start()
    tails.start()

    backs.wait()
    for b in range(REACH):
        tile = block_of(rrecv, rsend, b)
        for c in range(3):
            accel = dprop[b, 0:1, :] * (tile[c : c + 1, :] - dvel[3 * b + c])
            acc_out[3 * b + c] = jnp.where(lane[0:1] < cnt[0, 0, b], accel, 0.0)

    tails.wait()
    tail_corners.wait()
    for c in range(3):
        value = combine(
            drag[8 * c : 8 * c + 8], lambda n: frecv[n, c], lambda n: fcr[n, c]
        )
        for i in range(8):
            m_out[c, i] = value[i]

    pltpu.make_async_copy(ledger, ledger, send_sems.at[0]).wait()


def deliver(p_in, m_in, acc_in, p_out, m_out, acc_out, sems):
    copies = [
        pltpu.make_async_copy(near, far, sems.at[n])
        for n, (near, far) in enumerate([(m_in, m_out), (p_in, p_out), (acc_in, acc_out)])
    ]
    for copy in copies:
        copy.start()
    for copy in copies:
        copy.wait()


def on_device(source, metric, base, elem, coord, dvel, dprop, counts):
    vmem = pl.BlockSpec(memory_space=pltpu.VMEM)
    hbm = pl.BlockSpec(memory_space=pltpu.HBM)
    dma = pltpu.SemaphoreType.DMA
    elem = elem.reshape(REACH, 1, CAP)
    coord = coord.reshape(REACH * 3, 1, CAP)
    dvel = dvel.reshape(REACH * 3, 1, CAP)
    dprop = dprop.reshape(REACH, 2, CAP)
    tile = (8, 128)
    row = (1, 128)
    blocks = pltpu.VMEM((REACH,) + tile, F32)
    arrive_shapes = [
        (4, 5) + tile, (4, 2) + tile, (4,) + tile, (12, 2) + row, (4,) + tile, (4,) + tile,
        (12,) + tile, (4,) + tile, (4,) + tile, (4, 3) + tile, (4, 3) + row,
    ]
    arrive = [pltpu.VMEM(shape, F32) for shape in arrive_shapes]
    total_rows = sum(int(np.prod(shape)) for shape in arrive_shapes) // 128
    shapes = (
        jax.ShapeDtypeStruct((8, 8, 128), F32),
        jax.ShapeDtypeStruct((3, 8, 8, 128), F32),
        jax.ShapeDtypeStruct((REACH * 3, 1, CAP), F32),
    )
    operands = (source, metric, base, elem, coord, dvel, dprop, counts)
    operands += (jnp.asarray(constant_tiles()),)
    outs = pl.pallas_call(
        kernel,
        out_shape=shapes,
        in_specs=[hbm] * 9,
        out_specs=(vmem,) * 3,
        scratch_shapes=[
            pltpu.VMEM((8, 8, 128), F32),
            pltpu.SMEM((1, 1, EZ), F32),
            pltpu.VMEM((3, 8, 8, 128), F32),
            pltpu.VMEM((REACH, 1, CAP), jnp.int32),
            pltpu.VMEM((REACH * 3, 1, CAP), F32),
            pltpu.VMEM((REACH * 3, 1, CAP), F32),
            pltpu.VMEM((REACH, 2, CAP), F32),
            pltpu.SMEM((1, 1, REACH), jnp.int32),
            pltpu.VMEM((PACKED,) + tile, F32),
            pltpu.VMEM((TILES,) + tile, F32),
            pltpu.VMEM((64, 128), F32),
            pltpu.VMEM((192, 128), F32),
            pltpu.VMEM((256, 256), BF16),
            pltpu.VMEM((256, REACH * CAP), BF16),
            pltpu.VMEM((256, REACH * CAP), BF16),
            blocks,
            blocks,
            blocks,
            blocks,
            blocks,
            pltpu.VMEM((4, 5) + tile, F32),
            arrive[0],
            pltpu.VMEM((4, 2) + tile, F32),
            arrive[1],
            arrive[2],
            pltpu.VMEM((12, 2) + row, F32),
            arrive[3],
            pltpu.VMEM((5,) + tile, F32),
            arrive[5],
            pltpu.VMEM((4, 3) + tile, F32),
            arrive[9],
            pltpu.VMEM((4, 3) + row, F32),
            arrive[10],
            blocks,
            arrive[4],
            blocks,
            arrive[8],
            pltpu.VMEM((4,) + tile, F32),
            arrive[7],
            arrive[6],
            pltpu.VMEM((8,) + tile, F32),
            pltpu.VMEM((3,) + row, F32),
            *arrive,
            pltpu.VMEM((total_rows,) + row, F32),
            pltpu.VMEM((REACH * 9,) + row, F32),
            dma((6,)),
            dma((1,)),
            dma((len(arrive),)),
        ],
        compiler_params=pltpu.CompilerParams(
            collective_id=0, has_side_effects=True, vmem_limit_bytes=32 * 1024 * 1024
        ),
    )(*[pltpu.with_memory_space_constraint(operand, pltpu.HBM) for operand in operands])
    pressure, momentum, accel = pl.pallas_call(
        deliver,
        out_shape=shapes,
        in_specs=[vmem] * 3,
        out_specs=(hbm,) * 3,
        scratch_shapes=[dma((3,))],
        compiler_params=pltpu.CompilerParams(vmem_limit_bytes=1024 * 1024),
    )(*outs)
    return pressure, momentum, accel.reshape(1, 1, REACH, 3, CAP)


def solution(mesh):
    in_specs = (
        P("stream", "cross", None),
        P("stream", "cross", None),
        P(None, "stream", "cross", None),
        P("stream", "cross", None, None),
        P("stream", "cross", None, None, None),
        P("stream", "cross", None, None, None),
        P("stream", "cross", None, None, None),
        P("stream", "cross", None),
    )
    out_specs = (
        P("stream", "cross", None),
        P(None, "stream", "cross", None),
        P("stream", "cross", None, None, None),
    )
    return jax.shard_map(
        on_device, mesh=mesh, in_specs=in_specs, out_specs=out_specs, check_vma=False
    )
```

```python
import jax
import jax.numpy as jnp
import numpy as np
from jax import lax
from jax.experimental import pallas as pl
from jax.experimental.pallas import tpu as pltpu
from jax.sharding import PartitionSpec as P

SWEEPS = 3
UPPER_BOUND = 2.5
LOWER_BOUND = UPPER_BOUND / 30.0
REACH = 5
DRIFT = 2
CAP = 128
EZ = 16
GLL_POINTS = [
    -1.0,
    -0.8717401485096066,
    -0.5917001814331423,
    -0.2092992179024789,
    0.2092992179024789,
    0.5917001814331423,
    0.8717401485096066,
    1.0,
]
F32 = jnp.float32
BF16 = jnp.bfloat16
MESH = pl.DeviceIdType.MESH

FACES = [(1, 0), (-1, 0), (0, 1), (0, -1)]
CORNERS = [(1, 1), (1, -1), (-1, 1), (-1, -1)]
FAR = [(2, 0), (-2, 0), (0, 2), (0, -2)]
FAR_CORNERS = [(2, 1), (2, -1), (-2, 1), (-2, -1), (1, 2), (1, -2), (-1, 2), (-1, -2)]
AWAY = [0, 4, 1, 3]
PLACE = {(1, 0): 0, (0, 1): 1, (-1, 0): 2, (0, -1): 3}
PAIR = {(1, 1): 0, (-1, 1): 1, (-1, -1): 2, (1, -1): 3}


def legendre_seven(points):
    before = points * 0.0 + 1.0
    current = points
    for order in range(1, 7):
        following = ((2.0 * order + 1.0) * points * current - order * before) / (order + 1.0)
        before = current
        current = following
    return current


def gll_tables():
    nodes = np.array(GLL_POINTS)
    values = legendre_seven(nodes)
    weights = 2.0 / (56.0 * values * values)
    deriv = np.zeros((8, 8))
    for row in range(8):
        for col in range(8):
            if row != col:
                deriv[row, col] = values[row] / (values[col] * (nodes[row] - nodes[col]))
    deriv[0, 0] = -14.0
    deriv[7, 7] = 14.0
    return nodes, weights, deriv


NODES, WEIGHTS, DERIV = gll_tables()
STIFF = DERIV.T @ (WEIGHTS[:, None] * DERIV)
QDIAG = np.diag(STIFF)

PACKED = 5
T_WK, T_QK, T_KT, T_ZM, T_WJ, T_QJ, T_CY, T_DT, T_LAG, T_END = 0, 1, 2, 3, 4, 5, 6, 14, 22, 23
TILES = 27


def constant_tiles():
    lane = np.arange(128)
    row = np.arange(8)
    tiles = np.zeros((PACKED, 8, 128))
    tiles[T_WK] = WEIGHTS[lane % 8][None, :]
    tiles[T_QK] = QDIAG[lane % 8][None, :]
    tiles[T_KT] = STIFF[lane % 8, :].T
    last = (lane % 8 == 7) & (lane < 127)
    first = (lane % 8 == 0) & (lane > 0)
    tiles[T_ZM] = (last | first)[None, :]
    columns = tiles[PACKED - 1]
    columns[:, T_WJ] = WEIGHTS
    columns[:, T_QJ] = QDIAG
    for turn in range(8):
        columns[:, T_CY + turn] = STIFF[row, (row - turn) % 8]
        columns[:, T_DT + turn] = DERIV[(row - turn) % 8, row]
    gaps = NODES[:, None] - NODES[None, :] + np.eye(8)
    columns[:, T_LAG] = 1.0 / gaps.prod(1)
    columns[0:7, T_END] = STIFF[7, 0:7]
    columns[1:8, T_END + 1] = STIFF[0, 1:8]
    columns[1:7, T_END + 2] = STIFF[7, 1:7]
    columns[1:7, T_END + 3] = STIFF[0, 1:7]
    return tiles.astype(np.float32)


def iota(dim):
    return lax.broadcasted_iota(jnp.int32, (8, 128), dim)


def total(terms):
    terms = list(terms)
    while len(terms) > 1:
        pairs = [a + b for a, b in zip(terms[::2], terms[1::2])]
        if len(terms) % 2:
            pairs.append(terms[-1])
        terms = pairs
    return terms[0]


def wide(row):
    return jnp.broadcast_to(row, (8, 128))


def halves(value):
    high = value.astype(BF16)
    return high, (value - high.astype(F32)).astype(BF16)


def stiff_x(u):
    even = [u[m] + u[7 - m] for m in range(4)]
    odd = [u[m] - u[7 - m] for m in range(4)]
    out = [None] * 8
    for i in range(4):
        e = total(float((STIFF[i, m] + STIFF[i, 7 - m]) / 2.0) * even[m] for m in range(4))
        o = total(float((STIFF[i, m] - STIFF[i, 7 - m]) / 2.0) * odd[m] for m in range(4))
        out[i] = e + o
        out[7 - i] = e - o
    return out


def turned(value, tab, first):
    terms = [tab[first] * value]
    for turn in range(1, 8):
        terms.append(tab[first + turn] * pltpu.roll(value, turn, 0))
    return total(terms)


def kernel(
    src_h, met_h, bvel_h, elem_h, coord_h, dvel_h, dprop_h, cnt_h, tab_h,
    p_out, m_out, acc_out,
    src, met, bvel, elem, coord, dvel, dprop, cnt, pack, tab,
    ub, mb, kz, lzd, lzt, lx, dx, ly, dy, fbase,
    hsend, hrecv, hcs, hcr, hfr, hrs, hrr, nsend, nrecv, fsend, frecv, fcs, fcr,
    dsend, drecv, rsend, rrecv, tsend, trecv, grecv, zeros, zero_rows,
    *rest,
):
    *spare, ledger, load_ledger, si, send_sems, recv_sems = rest
    slabs, cols = lax.axis_size("stream"), lax.axis_size("cross")
    slab, col = lax.axis_index("stream"), lax.axis_index("cross")

    loads = [
        pltpu.make_async_copy(far, near, si.at[n])
        for far, near, n in [
            (tab_h, pack, 0), (src_h, src, 1), (met_h, met, 2), (cnt_h, cnt, 3), (elem_h, elem, 4),
            (coord_h, coord, 4), (dvel_h, dvel, 4), (dprop_h, dprop, 4), (bvel_h, bvel, 5),
        ]
    ]
    for load in loads:
        load.start()

    def device(ds, dc):
        return (slab + ds, col + dc)

    def exists(ds, dc):
        found = (slab + ds >= 0) & (slab + ds < slabs)
        return found & (col + dc >= 0) & (col + dc < cols)

    inside = (slab >= 2) & (slab < slabs - 2) & (col >= 2) & (col < cols - 2)
    groups = []

    class Group:
        def __init__(self, recv, messages):
            self.recv, self.messages = recv, messages
            self.sem = recv_sems.at[len(groups)]
            self.spare = spare[len(groups)]
            groups.append(self)

        def start(self):
            for d, source, slot in self.messages:
                copy = pltpu.make_async_remote_copy(
                    src_ref=source,
                    dst_ref=self.recv.at[slot],
                    send_sem=send_sems.at[0],
                    recv_sem=self.sem,
                    device_id=device(*d),
                    device_id_type=MESH,
                )
                pl.when(exists(*d))(copy.start)

        def wait(self):
            pltpu.make_async_copy(self.recv, self.recv, self.sem).wait()

        def fill(self):
            for d, _, slot in self.messages:
                near, away = self.recv.at[slot], self.spare.at[slot]
                pool = zero_rows if near.shape[-2] == 1 else zeros
                none = pool.at[0] if len(near.shape) == 2 else pool.at[pl.ds(0, near.shape[0])]
                pl.when(jnp.logical_not(exists(-d[0], -d[1])))(
                    pltpu.make_async_copy(none, near, self.sem).start
                )
                pl.when(jnp.logical_not(exists(*d)))(
                    pltpu.make_async_copy(none, away, send_sems.at[0]).start
                )

    barrier = pltpu.get_barrier_semaphore()
    partners = FAR_CORNERS + FAR + CORNERS + FACES
    greeted = jnp.int32(0)
    for d in partners:
        there = exists(*d)
        greeted += there.astype(jnp.int32)

        @pl.when(there)
        def _():
            pl.semaphore_signal(barrier, inc=1, device_id=device(*d), device_id_type=MESH)

    sub, lane = iota(0), iota(1)
    perm = jnp.clip(
        lane + jnp.where(lane % 8 == 7, 1, 0) - jnp.where(lane % 8 == 0, 1, 0), 0, 127
    )
    elane = lane // 8
    top, bottom = sub == 0, sub == 7

    loads[0].wait()
    tab[0:4] = pack[0:4]
    columns = pack[PACKED - 1]
    for t in range(T_WJ, TILES):
        tab[t] = wide(columns[:, t : t + 1])
    wk, wj = pack[T_WK], tab[T_WJ]

    def sum_z(value):
        return value + tab[T_ZM] * jnp.take_along_axis(value, perm, axis=1)

    def edges(low, high):
        return jnp.where(top, low, jnp.where(bottom, high, 0.0))

    def row_of(ref, i):
        return wide(ref[i : i + 1, :])

    loads[2].wait()
    amet = jnp.zeros((8, 128), F32)
    for e in range(EZ):
        amet = jnp.where(elane == e, met[0, 0, e], amet)
    loads[1].wait()
    rhs = [sum_z(wk * src[i]) for i in range(8)]

    def lines_of(u):
        for i in range(8):
            ub[8 * i : 8 * i + 8, :] = u[i]
        return [ub[pl.ds(j, 8, stride=8), :] for j in range(8)]

    def edge_row(d):
        return 7 if d > 0 else 0

    def ends(u, group_range):
        lines = lines_of(u)
        return {
            d: total(float(STIFF[row, m]) * group[m] for m in group_range(row))
            for d, group, row in (
                ((1, 0), u, 7), ((-1, 0), u, 0), ((0, 1), lines, 7), ((0, -1), lines, 0)
            )
        }

    def opposite(d):
        return (-d[0], -d[1])

    center = (UPPER_BOUND + LOWER_BOUND) / 2.0
    half_width = (UPPER_BOUND - LOWER_BOUND) / 2.0
    bound = center / half_width
    rho = 1.0 / bound
    qk, qj = tab[T_QK], tab[T_QJ]
    plane, mixed = sum_z(wk * amet), sum_z(qk * amet + wk)
    early = []
    for i in range(8):
        w_i, q_i = float(WEIGHTS[i]), float(QDIAG[i])
        diagonal = (q_i * wj + w_i * qj) * plane + (w_i * wj) * mixed
        early.append((w_i / center) * (wj * rhs[i]) / diagonal)
    middle = ends(early, lambda row: range(1, 7))

    lines = lines_of(rhs)
    skin = {d: (rhs if d[0] else lines)[edge_row(d[0] + d[1])] for d in FACES}
    for n, d in enumerate(FACES):
        for f in FACES:
            hsend[n, PLACE[f]] = skin[f]
        hsend[n, 4] = jnp.where(top, amet, middle[d])
        hrs[n, 0] = amet[0:1, :]
        hrs[n, 1] = amet[0:1, :]
    for n, d in enumerate(CORNERS):
        hcs[n, 0] = skin[(d[0], 0)]
        hcs[n, 1] = jnp.where(sub == edge_row(d[0]), amet, skin[(0, d[1])])
    for n, d in enumerate(FAR_CORNERS):
        if abs(d[0]) == 2:
            face, row = skin[(d[0] // 2, 0)], edge_row(d[1])
        else:
            face, row = skin[(0, d[1] // 2)], edge_row(d[0])
        hrs[4 + n, 0] = face[row : row + 1, :]
        hrs[4 + n, 1] = amet[0:1, :]

    def slots(dirs, source):
        return [(d, source(n, d), n) for n, d in enumerate(dirs)]

    blocks_to = [((b - DRIFT, 0), dsend.at[b], n) for n, b in enumerate(AWAY)]
    blocks_back = [((DRIFT - b, 0), rsend.at[b], n) for n, b in enumerate(AWAY)]
    heads = Group(hrecv, slots(FACES, lambda n, d: hsend.at[n]))
    head_corners = Group(hcr, slots(CORNERS, lambda n, d: hcs.at[n]))
    head_far = Group(
        hfr, [(d, hsend.at[0, PLACE[(d[0] // 2, d[1] // 2)]], n) for n, d in enumerate(FAR)]
    )
    head_rows = Group(hrr, slots(FAR + FAR_CORNERS, lambda n, d: hrs.at[n]))
    drops = Group(drecv, blocks_to)
    near_two = Group(nrecv, slots(FACES, lambda n, d: nsend.at[PLACE[d]]))
    far_two = Group(
        grecv,
        [(d, nsend.at[PLACE[(d[0] // 2, d[1] // 2)]], n) for n, d in enumerate(FAR)]
        + [(d, nsend.at[pl.ds(PAIR[d], 2)], pl.ds(4 + 2 * n, 2)) for n, d in enumerate(CORNERS)],
    )
    tilde = Group(trecv, slots(FACES, lambda n, d: tsend.at[PLACE[d]]))
    backs = Group(rrecv, blocks_back)
    tails = Group(frecv, slots(FACES, lambda n, d: fsend.at[n]))
    tail_corners = Group(fcr, slots(CORNERS, lambda n, d: fcs.at[n]))

    @pl.when(jnp.logical_not(inside))
    def _():
        zeros[...] = jnp.zeros_like(zeros)
        zero_rows[...] = jnp.zeros_like(zero_rows)
        for group in groups:
            group.fill()

    def combine(value, recv, corner):
        def face(t):
            return recv(FACES.index((t, 0))) + edges(
                wide(corner(CORNERS.index((t, 1)))), wide(corner(CORNERS.index((t, -1))))
            )

        low, high = recv(FACES.index((0, 1))), recv(FACES.index((0, -1)))
        out = []
        for i in range(8):
            term = value[i] + edges(wide(low[i : i + 1, :]), wide(high[i : i + 1, :]))
            if i == 0:
                term += face(1)
            if i == 7:
                term += face(-1)
            out.append(term)
        return out

    def stage_drops():
        for b in range(REACH):
            for c in range(3):
                dsend[b, c : c + 1, :] = coord[3 * b + c]
                dsend[b, 3 + c : 4 + c, :] = dvel[3 * b + c]
            dsend[b, 6:7, :] = dprop[b, 0:1, :] * dprop[b, 1:2, :]
            dsend[b, 7:8, :] = jnp.where(
                lane[0:1] < cnt[0, 0, b], (elem[b] % EZ).astype(F32), -1.0
            )

    loads[3].wait()
    pltpu.make_async_copy(load_ledger, load_ledger, si.at[4]).wait()
    stage_drops()

    pl.semaphore_wait(barrier, greeted)
    head_rows.start()
    head_far.start()
    head_corners.start()
    heads.start()
    drops.start()

    khigh, klow = halves(
        jnp.concatenate([jnp.where(elane == e, tab[T_KT], 0.0) for e in range(EZ)], axis=0)
    )
    kz[0:128, 0:128] = khigh
    kz[0:128, 128:256] = klow
    kz[128:256, 0:128] = khigh
    kz[128:256, 128:256] = jnp.zeros((128, 128), BF16)

    def along_z(u):
        high, low = halves(jnp.concatenate(u, axis=0))
        both = jnp.dot(
            jnp.concatenate([high, low], axis=1), kz[...], preferred_element_type=F32
        )
        both = both[:, 0:128] + both[:, 128:256]
        return [both[8 * i : 8 * i + 8, :] for i in range(8)]

    def block_of(arrived, own, b):
        return own.at[b] if b == DRIFT else arrived.at[AWAY.index(b)]

    def basis_block(b):
        def basis(r):
            value = tab[T_LAG]
            for m in range(8):
                value = value * jnp.where(sub == m, 1.0, r - float(NODES[m]))
            return value, turned(value, tab, T_DT)

        tile = block_of(drecv, dsend, b)
        eid = row_of(tile, 7)
        lx[b], dx[b] = basis(row_of(tile, 0))
        ly[b], dy[b] = basis(row_of(tile, 1))
        for side_by, part in enumerate(basis(row_of(tile, 2))):
            high = part.astype(BF16).astype(F32)
            for piece, first in ((high, 0), (part - high, 128)):
                spread = jnp.concatenate(
                    [jnp.where(eid == float(e), piece, 0.0) for e in range(EZ)], axis=0
                )
                spread = spread.astype(BF16)
                start = (2 * b + side_by) * CAP
                lzd[first : first + 128, start : start + CAP] = spread
                if not side_by:
                    lzt[b * CAP : b * CAP + CAP, first : first + 128] = jnp.transpose(spread)

    def contract(planes, first, second):
        inner = total(row_of(first, i) * planes[i] for i in range(8))
        return jnp.sum(second[...] * inner, axis=0, keepdims=True)

    def stacked(value):
        high, low = halves(value)
        return jnp.concatenate(
            [
                jnp.concatenate([high, high], axis=1),
                jnp.concatenate([low, jnp.zeros_like(low)], axis=1),
            ],
            axis=0,
        )

    def base_values():
        loads[8].wait()
        left = stacked(jnp.concatenate([bvel[c, i] for c in range(3) for i in range(8)], axis=0))
        for b in range(REACH):
            span = slice(2 * b * CAP, 2 * b * CAP + CAP)
            both = jnp.dot(left, lzd[:, span], preferred_element_type=F32)
            both = both[0:192, :] + both[192:384, :]
            for c in range(3):
                planes = [both[64 * c + 8 * i : 64 * c + 8 * i + 8, :] for i in range(8)]
                fbase[b, c : c + 1, :] = contract(planes, lx.at[b], ly.at[b])

    basis_block(DRIFT)

    for group in (heads, head_corners, head_far, head_rows):
        group.wait()
    skins, factor, middle_of = {}, {(0, 0): amet}, {}
    for n, d in enumerate(FACES):
        at = opposite(d)
        skins[at] = {f: hrecv[n, PLACE[f]] for f in FACES}
        middle_of[at] = hrecv[n, 4]
        factor[at] = wide(middle_of[at][0:1, :])
    for n, d in enumerate(CORNERS):
        row = edge_row(d[0])
        skins[opposite(d)] = {(d[0], 0): hcr[n, 0], (0, d[1]): hcr[n, 1]}
        factor[opposite(d)] = wide(hcr[n, 1, row : row + 1, :])
    point = {}
    for n, d in enumerate(FAR + FAR_CORNERS):
        point[opposite(d)] = wide(hrr[n, 0])
        factor[opposite(d)] = wide(hrr[n, 1])

    def shared_row(n):
        row = edge_row(CORNERS[n][1])
        return hcr[n, 0, row : row + 1, :]

    residual = combine(rhs, lambda n: skins[opposite(FACES[n])][FACES[n]], shared_row)
    own_x = amet + edges(factor[(0, -1)], factor[(0, 1)])
    a_y = [amet + factor[(-1, 0)]] + [amet] * 6 + [amet + factor[(1, 0)]]
    side = {
        (t, 0): factor[(t, 0)] + edges(factor[(t, -1)], factor[(t, 1)]) for t in (-1, 1)
    }
    side |= {
        (0, t): factor[(0, t)] + edges(factor[(-1, t)], factor[(1, t)]) for t in (-1, 1)
    }
    a_sum = [own_x + side[(-1, 0)]] + [own_x] * 6 + [own_x + side[(1, 0)]]

    def present(ds, dc):
        return exists(ds, dc).astype(F32)

    count_y = 1.0 + edges(present(0, -1), present(0, 1))
    count_x = [1.0 + present(-1, 0)] + [1.0] * 6 + [1.0 + present(1, 0)]

    wkj = wk * wj
    mass = [wkj * (count_x[i] * count_y) for i in range(8)]
    planes = {}
    for i in (0, 1, 7):
        planes[i] = (sum_z(wk * a_sum[i]), sum_z(qk * a_sum[i] + wk * (count_x[i] * count_y)))
    inv_diag, update = [], []
    for i in range(8):
        w_i, q_i = float(WEIGHTS[i]), float(QDIAG[i])
        plane, mixed = planes[i if i in planes else 1]
        residual[i] = (w_i * wj) * residual[i]
        diagonal = (q_i * wj + w_i * qj) * plane + (w_i * wj) * mixed
        inv_diag.append(1.0 / diagonal)
        update.append(inv_diag[i] * residual[i] * (1.0 / center))
    iterate = update

    across = {d: wkj * side[d] for d in FACES}
    def own_part(u):
        flat, slope = along_z(u), stiff_x(u)
        out = []
        for i in range(8):
            w_i = float(WEIGHTS[i])
            out.append(
                sum_z(
                    wkj * own_x * slope[i]
                    + (w_i * wk) * a_y[i] * turned(u[i], tab, T_CY)
                    + (w_i * wj) * a_sum[i] * flat[i]
                    + w_i * mass[i] * u[i]
                )
            )
        return out

    def less_beside(value, flow):
        part = {d: sum_z(across[d] * flow[d]) for d in FACES}
        out = [
            value[i]
            - edges(wide(part[(0, -1)][i : i + 1, :]), wide(part[(0, 1)][i : i + 1, :]))
            for i in range(8)
        ]
        out[0] -= part[(-1, 0)]
        out[7] -= part[(1, 0)]
        return out

    steps = []
    for sweep in range(SWEEPS):
        rho_next = 1.0 / (2.0 * bound - rho)
        steps.append((rho_next * rho, 2.0 * rho_next / half_width))
        rho = rho_next

    def advanced(u, left, step):
        return [step[0] * u[i] + step[1] * (inv_diag[i] * left[i]) for i in range(8)]

    def outer(value, a_near, count):
        w_0, q_0 = float(WEIGHTS[0]), float(QDIAG[0])
        diagonal = (q_0 * wj + w_0 * qj) * sum_z(wk * a_near) + (w_0 * wj) * sum_z(
            qk * a_near + wk * jnp.maximum(count, 1.0)
        )
        inverse = 1.0 / diagonal
        return inverse, inverse * (((w_0 / center) * wj) * value)

    def plus(p, q):
        return (p[0] + q[0], p[1] + q[1])

    def rim_of(d, t):
        return (0, t) if d[0] else (t, 0)

    def ordered(at, far, near):
        return edges(far, near) if at[0] + at[1] < 0 else edges(near, far)

    def a_of(*places):
        return total(factor[p] for p in places)

    def n_of(*places):
        return total(present(*p) for p in places)

    shell, flow = {}, {}
    lines = lines_of(update)
    for n, d in enumerate(FACES):
        at = opposite(d)
        far = plus(at, at)
        forward = d[0] + d[1] > 0
        beside = {t: plus(at, rim_of(d, t)) for t in (-1, 1)}
        beyond = {t: plus(far, rim_of(d, t)) for t in (-1, 1)}
        row = edge_row(at[0] + at[1])
        corner_values = [
            wide(skins[beside[t]][opposite(rim_of(d, t))][row : row + 1, :]) + point[beyond[t]]
            for t in (-1, 1)
        ]
        inverse, value = outer(
            skins[at][at] + hfr[n] + edges(*corner_values),
            a_of(at, far) + edges(*[a_of(beside[t], beyond[t]) for t in (-1, 1)]),
            n_of(at, far) + edges(*[n_of(beside[t], beyond[t]) for t in (-1, 1)]),
        )
        weight = wkj * (factor[far] + edges(factor[beyond[-1]], factor[beyond[1]]))
        shell[at, at] = (weight, inverse)
        sums = []
        for t in (-1, 1):
            rim = rim_of(d, t)
            inverse, rim_value = outer(
                skins[at][rim] + skins[beside[t]][opposite(rim)],
                a_of(at, beside[t]) + ordered(at, a_of(far, beyond[t]), a_of((0, 0), rim)),
                n_of(at, beside[t]) + ordered(at, n_of(far, beyond[t]), n_of((0, 0), rim)),
            )
            weight = wkj * (factor[beside[t]] + ordered(at, factor[beyond[t]], factor[rim]))
            shell[at, rim] = (weight, inverse)
            weights = tab[T_END + (2 if forward else 3)]
            sums.append(wide(jnp.sum(weights * rim_value, axis=0, keepdims=True)))
        far_weight = float(STIFF[7, 0] if forward else STIFF[0, 7])
        near_weight = float(STIFF[7, 7] if forward else STIFF[0, 0])
        shared = (update if d[0] else lines)[0 if forward else 7]
        inner = jnp.where(top, sums[0], jnp.where(bottom, sums[1], middle_of[at]))
        flow[at] = inner + far_weight * value + near_weight * shared

    own = own_part(update)
    residual = less_beside([residual[i] - own[i] for i in range(8)], flow)
    update = advanced(update, residual, steps[0])
    iterate = [iterate[i] + update[i] for i in range(8)]

    for d, tile in ends(update, lambda row: range(8)).items():
        nsend[PLACE[d]] = tile
        if PLACE[d] == 0:
            nsend[4] = tile
    near_two.start()
    far_two.start()
    own = own_part(update)
    residual = [residual[i] - own[i] for i in range(8)]
    guess = advanced(update, residual, steps[1])
    for d, tile in ends(guess, lambda row: range(7) if row else range(1, 8)).items():
        tsend[PLACE[d]] = tile
    tilde.start()
    drops.wait()
    for b in AWAY:
        basis_block(b)
    base_values()

    near_two.wait()
    residual = less_beside(residual, {opposite(d): nrecv[n] for n, d in enumerate(FACES)})
    update = advanced(update, residual, steps[1])
    iterate = [iterate[i] + update[i] for i in range(8)]
    lines = lines_of(update)
    own = own_part(update)
    residual = [residual[i] - own[i] for i in range(8)]

    for group in (far_two, tilde):
        group.wait()

    def from_corner(at, along):
        d = opposite(at)
        return grecv[4 + 2 * CORNERS.index(d) + (PLACE[along] - PAIR[d]) % 4]

    flow = {}
    for n, d in enumerate(FACES):
        at = opposite(d)

        def change(face, across_it):
            weight, inverse = shell[at, face]
            return (-steps[1][1]) * (inverse * sum_z(weight * across_it))

        forward = d[0] + d[1] > 0
        far_weight = float(STIFF[7, 0] if forward else STIFF[0, 7])
        near_weight = float(STIFF[7, 7] if forward else STIFF[0, 0])
        weights = tab[T_END if forward else T_END + 1]
        rims = []
        for t in (-1, 1):
            rim = rim_of(d, t)
            corner = plus(at, rim)
            changed = change(rim, from_corner(corner, opposite(rim)))
            rims.append(wide(jnp.sum(weights * changed, axis=0, keepdims=True)))
        if d[0]:
            shared = update[0 if forward else 7]
        else:
            shared = lines[0 if forward else 7]
        flow[at] = (
            trecv[n] + far_weight * change(at, grecv[n]) + edges(*rims) + near_weight * shared
        )
    residual = less_beside(residual, flow)
    update = advanced(update, residual, steps[2])
    iterate = [iterate[i] + update[i] for i in range(8)]

    for i in range(8):
        p_out[i] = iterate[i]

    left = stacked(jnp.concatenate([amet * iterate[i] for i in range(8)], axis=0))
    forces = []
    for b in range(REACH):
        span = slice(2 * b * CAP, 2 * b * CAP + 2 * CAP)
        both = jnp.dot(left, lzd[:, span], preferred_element_type=F32)
        both = both[0:64, :] + both[64:128, :]
        flat = [both[8 * i : 8 * i + 8, 0:CAP] for i in range(8)]
        slope = [both[8 * i : 8 * i + 8, CAP : 2 * CAP] for i in range(8)]
        grads = [
            contract(flat, dx.at[b], ly.at[b]),
            contract(flat, lx.at[b], dy.at[b]),
            contract(slope, lx.at[b], ly.at[b]),
        ]
        tile = block_of(drecv, dsend, b)
        force = []
        for c in range(3):
            fluid = fbase[b, c : c + 1, :] - grads[c]
            rsend[b, c] = fluid
            force.append(tile[6:7, :] * (tile[3 + c : 4 + c, :] - fluid))
        forces.append(force)
    backs.start()

    columns_high, columns_low = [], []
    for b in range(REACH):
        rows_ = []
        for c in range(3):
            weighted = wide(forces[b][c]) * ly[b]
            rows_ += [weighted * row_of(lx.at[b], i) for i in range(8)]
        high, low = halves(jnp.concatenate(rows_, axis=0))
        columns_high.append(high)
        columns_low.append(low)
    left = jnp.concatenate(
        [jnp.concatenate(columns_high, axis=1), jnp.concatenate(columns_low, axis=1)], axis=0
    )
    both = jnp.dot(left, lzt[...], preferred_element_type=F32)
    drag = both[0:192, 0:128] + both[0:192, 128:256] + both[192:384, 0:128]
    drag = [drag[8 * i : 8 * i + 8, :] for i in range(24)]
    for c in range(3):
        for i in (0, 7):
            drag[8 * c + i] = sum_z(drag[8 * c + i])
    for i in range(24):
        mb[8 * i : 8 * i + 8, :] = drag[i]
    for c in range(3):
        for n, d in enumerate(CORNERS):
            row = edge_row(d[1])
            fcs[n, c] = drag[8 * c + edge_row(d[0])][row : row + 1, :]
    tail_corners.start()
    for c in range(3):
        for n, d in enumerate(FACES):
            row = edge_row(d[0] + d[1])
            if d[0]:
                fsend[n, c] = drag[8 * c + row]
            else:
                line = mb[pl.ds(64 * c + row, 8, stride=8), :]
                fsend[n, c] = jnp.where(top | bottom, line, sum_z(line))
    tails.start()
    for c in range(3):
        for i in range(1, 7):
            drag[8 * c + i] = sum_z(drag[8 * c + i])

    backs.wait()
    for b in range(REACH):
        tile = block_of(rrecv, rsend, b)
        for c in range(3):
            accel = dprop[b, 0:1, :] * (tile[c] - dvel[3 * b + c])
            acc_out[3 * b + c] = jnp.where(lane[0:1] < cnt[0, 0, b], accel, 0.0)

    tails.wait()
    tail_corners.wait()
    for c in range(3):
        value = combine(
            drag[8 * c : 8 * c + 8], lambda n: frecv[n, c], lambda n: fcr[n, c]
        )
        for i in range(8):
            m_out[c, i] = value[i]

    pltpu.make_async_copy(ledger, ledger, send_sems.at[0]).wait()


def deliver(p_in, m_in, acc_in, p_out, m_out, acc_out, sems):
    copies = [
        pltpu.make_async_copy(near, far, sems.at[n])
        for n, (near, far) in enumerate([(m_in, m_out), (p_in, p_out), (acc_in, acc_out)])
    ]
    for copy in copies:
        copy.start()
    for copy in copies:
        copy.wait()


def on_device(source, metric, base, elem, coord, dvel, dprop, counts):
    vmem = pl.BlockSpec(memory_space=pltpu.VMEM)
    hbm = pl.BlockSpec(memory_space=pltpu.HBM)
    dma = pltpu.SemaphoreType.DMA
    elem = elem.reshape(REACH, 1, CAP)
    coord = coord.reshape(REACH * 3, 1, CAP)
    dvel = dvel.reshape(REACH * 3, 1, CAP)
    dprop = dprop.reshape(REACH, 2, CAP)
    tile = (8, 128)
    row = (1, 128)
    blocks = pltpu.VMEM((REACH,) + tile, F32)
    arrive_shapes = [
        (4, 5) + tile, (4, 2) + tile, (4,) + tile, (12, 2) + row, (4,) + tile, (4,) + tile,
        (12,) + tile, (4,) + tile, (4, 3) + row, (4, 3) + tile, (4, 3) + row,
    ]
    arrive = [pltpu.VMEM(shape, F32) for shape in arrive_shapes]
    total_rows = sum(int(np.prod(shape)) for shape in arrive_shapes) // 128
    shapes = (
        jax.ShapeDtypeStruct((8, 8, 128), F32),
        jax.ShapeDtypeStruct((3, 8, 8, 128), F32),
        jax.ShapeDtypeStruct((REACH * 3, 1, CAP), F32),
    )
    operands = (source, metric, base, elem, coord, dvel, dprop, counts)
    operands += (jnp.asarray(constant_tiles()),)
    outs = pl.pallas_call(
        kernel,
        out_shape=shapes,
        in_specs=[hbm] * 9,
        out_specs=(vmem,) * 3,
        scratch_shapes=[
            pltpu.VMEM((8, 8, 128), F32),
            pltpu.SMEM((1, 1, EZ), F32),
            pltpu.VMEM((3, 8, 8, 128), F32),
            pltpu.VMEM((REACH, 1, CAP), jnp.int32),
            pltpu.VMEM((REACH * 3, 1, CAP), F32),
            pltpu.VMEM((REACH * 3, 1, CAP), F32),
            pltpu.VMEM((REACH, 2, CAP), F32),
            pltpu.SMEM((1, 1, REACH), jnp.int32),
            pltpu.VMEM((PACKED,) + tile, F32),
            pltpu.VMEM((TILES,) + tile, F32),
            pltpu.VMEM((64, 128), F32),
            pltpu.VMEM((192, 128), F32),
            pltpu.VMEM((256, 256), BF16),
            pltpu.VMEM((256, 2 * REACH * CAP), BF16),
            pltpu.VMEM((REACH * CAP, 256), BF16),
            blocks,
            blocks,
            blocks,
            blocks,
            blocks,
            pltpu.VMEM((4, 5) + tile, F32),
            arrive[0],
            pltpu.VMEM((4, 2) + tile, F32),
            arrive[1],
            arrive[2],
            pltpu.VMEM((12, 2) + row, F32),
            arrive[3],
            pltpu.VMEM((5,) + tile, F32),
            arrive[5],
            pltpu.VMEM((4, 3) + tile, F32),
            arrive[9],
            pltpu.VMEM((4, 3) + row, F32),
            arrive[10],
            blocks,
            arrive[4],
            pltpu.VMEM((REACH, 3) + row, F32),
            arrive[8],
            pltpu.VMEM((4,) + tile, F32),
            arrive[7],
            arrive[6],
            pltpu.VMEM((8,) + tile, F32),
            pltpu.VMEM((3,) + row, F32),
            *arrive,
            pltpu.VMEM((total_rows,) + row, F32),
            pltpu.VMEM((REACH * 9,) + row, F32),
            dma((6,)),
            dma((1,)),
            dma((len(arrive),)),
        ],
        compiler_params=pltpu.CompilerParams(
            collective_id=0, has_side_effects=True, vmem_limit_bytes=32 * 1024 * 1024
        ),
    )(*[pltpu.with_memory_space_constraint(operand, pltpu.HBM) for operand in operands])
    pressure, momentum, accel = pl.pallas_call(
        deliver,
        out_shape=shapes,
        in_specs=[vmem] * 3,
        out_specs=(hbm,) * 3,
        scratch_shapes=[dma((3,))],
        compiler_params=pltpu.CompilerParams(vmem_limit_bytes=1024 * 1024),
    )(*outs)
    return pressure, momentum, accel.reshape(1, 1, REACH, 3, CAP)


def solution(mesh):
    in_specs = (
        P("stream", "cross", None),
        P("stream", "cross", None),
        P(None, "stream", "cross", None),
        P("stream", "cross", None, None),
        P("stream", "cross", None, None, None),
        P("stream", "cross", None, None, None),
        P("stream", "cross", None, None, None),
        P("stream", "cross", None),
    )
    out_specs = (
        P("stream", "cross", None),
        P(None, "stream", "cross", None),
        P("stream", "cross", None, None, None),
    )
    return jax.shard_map(
        on_device, mesh=mesh, in_specs=in_specs, out_specs=out_specs, check_vma=False
    )
```

```python
import jax
import jax.numpy as jnp
import numpy as np
from jax import lax
from jax.experimental import pallas as pl
from jax.experimental.pallas import tpu as pltpu
from jax.sharding import PartitionSpec as P

SWEEPS = 3
UPPER_BOUND = 2.5
LOWER_BOUND = UPPER_BOUND / 30.0
REACH = 5
DRIFT = 2
CAP = 128
EZ = 16
GLL_POINTS = [
    -1.0,
    -0.8717401485096066,
    -0.5917001814331423,
    -0.2092992179024789,
    0.2092992179024789,
    0.5917001814331423,
    0.8717401485096066,
    1.0,
]
F32 = jnp.float32
BF16 = jnp.bfloat16
MESH = pl.DeviceIdType.MESH

FACES = [(1, 0), (-1, 0), (0, 1), (0, -1)]
CORNERS = [(1, 1), (1, -1), (-1, 1), (-1, -1)]
FAR = [(2, 0), (-2, 0), (0, 2), (0, -2)]
FAR_CORNERS = [(2, 1), (2, -1), (-2, 1), (-2, -1), (1, 2), (1, -2), (-1, 2), (-1, -2)]
AWAY = [0, 4, 1, 3]
PLACE = {(1, 0): 0, (0, 1): 1, (-1, 0): 2, (0, -1): 3}
PAIR = {(1, 1): 0, (-1, 1): 1, (-1, -1): 2, (1, -1): 3}


def legendre_seven(points):
    before = points * 0.0 + 1.0
    current = points
    for order in range(1, 7):
        following = ((2.0 * order + 1.0) * points * current - order * before) / (order + 1.0)
        before = current
        current = following
    return current


def gll_tables():
    nodes = np.array(GLL_POINTS)
    values = legendre_seven(nodes)
    weights = 2.0 / (56.0 * values * values)
    deriv = np.zeros((8, 8))
    for row in range(8):
        for col in range(8):
            if row != col:
                deriv[row, col] = values[row] / (values[col] * (nodes[row] - nodes[col]))
    deriv[0, 0] = -14.0
    deriv[7, 7] = 14.0
    return nodes, weights, deriv


NODES, WEIGHTS, DERIV = gll_tables()
STIFF = DERIV.T @ (WEIGHTS[:, None] * DERIV)
QDIAG = np.diag(STIFF)

PACKED = 5
T_WK, T_QK, T_KT, T_ZM, T_WJ, T_QJ, T_CY, T_DT, T_LAG, T_END = 0, 1, 2, 3, 4, 5, 6, 14, 22, 23
TILES = 27


def constant_tiles():
    lane = np.arange(128)
    row = np.arange(8)
    tiles = np.zeros((PACKED, 8, 128))
    tiles[T_WK] = WEIGHTS[lane % 8][None, :]
    tiles[T_QK] = QDIAG[lane % 8][None, :]
    tiles[T_KT] = STIFF[lane % 8, :].T
    last = (lane % 8 == 7) & (lane < 127)
    first = (lane % 8 == 0) & (lane > 0)
    tiles[T_ZM] = (last | first)[None, :]
    columns = tiles[PACKED - 1]
    columns[:, T_WJ] = WEIGHTS
    columns[:, T_QJ] = QDIAG
    for turn in range(8):
        columns[:, T_CY + turn] = STIFF[row, (row - turn) % 8]
        columns[:, T_DT + turn] = DERIV[(row - turn) % 8, row]
    gaps = NODES[:, None] - NODES[None, :] + np.eye(8)
    columns[:, T_LAG] = 1.0 / gaps.prod(1)
    columns[0:7, T_END] = STIFF[7, 0:7]
    columns[1:8, T_END + 1] = STIFF[0, 1:8]
    columns[1:7, T_END + 2] = STIFF[7, 1:7]
    columns[1:7, T_END + 3] = STIFF[0, 1:7]
    return tiles.astype(np.float32)


def iota(dim):
    return lax.broadcasted_iota(jnp.int32, (8, 128), dim)


def total(terms):
    terms = list(terms)
    while len(terms) > 1:
        pairs = [a + b for a, b in zip(terms[::2], terms[1::2])]
        if len(terms) % 2:
            pairs.append(terms[-1])
        terms = pairs
    return terms[0]


def wide(row):
    return jnp.broadcast_to(row, (8, 128))


def halves(value):
    high = value.astype(BF16)
    return high, (value - high.astype(F32)).astype(BF16)


def stiff_x(u):
    even = [u[m] + u[7 - m] for m in range(4)]
    odd = [u[m] - u[7 - m] for m in range(4)]
    out = [None] * 8
    for i in range(4):
        e = total(float((STIFF[i, m] + STIFF[i, 7 - m]) / 2.0) * even[m] for m in range(4))
        o = total(float((STIFF[i, m] - STIFF[i, 7 - m]) / 2.0) * odd[m] for m in range(4))
        out[i] = e + o
        out[7 - i] = e - o
    return out


def turned(value, tab, first):
    terms = [tab[first] * value]
    for turn in range(1, 8):
        terms.append(tab[first + turn] * pltpu.roll(value, turn, 0))
    return total(terms)


def kernel(
    src_h, met_h, bvel_h, elem_h, coord_h, dvel_h, dprop_h, cnt_h, tab_h,
    p_out, m_out, acc_out,
    src, met, bvel, elem, coord, dvel, dprop, cnt, pack, tab,
    ub, mb, kz, lzd, lzt, lx, dx, ly, dy, fbase,
    hsend, hrecv, hcs, hcr, hfr, hrs, hrr, nsend, nrecv, fsend, frecv, fcs, fcr,
    dsend, drecv, rsend, rrecv, tsend, trecv, grecv, zeros, zero_rows,
    *rest,
):
    *spare, ledger, load_ledger, si, send_sems, recv_sems = rest
    slabs, cols = lax.axis_size("stream"), lax.axis_size("cross")
    slab, col = lax.axis_index("stream"), lax.axis_index("cross")

    loads = [
        pltpu.make_async_copy(far, near, si.at[n])
        for far, near, n in [
            (tab_h, pack, 0), (src_h, src, 1), (met_h, met, 2), (cnt_h, cnt, 3), (elem_h, elem, 4),
            (coord_h, coord, 4), (dvel_h, dvel, 4), (dprop_h, dprop, 4), (bvel_h, bvel, 5),
        ]
    ]
    for load in loads:
        load.start()

    def device(ds, dc):
        return (slab + ds, col + dc)

    def exists(ds, dc):
        found = (slab + ds >= 0) & (slab + ds < slabs)
        return found & (col + dc >= 0) & (col + dc < cols)

    inside = (slab >= 2) & (slab < slabs - 2) & (col >= 2) & (col < cols - 2)
    groups = []

    class Group:
        def __init__(self, recv, messages):
            self.recv, self.messages = recv, messages
            self.sem = recv_sems.at[len(groups)]
            self.spare = spare[len(groups)]
            groups.append(self)

        def start(self):
            for d, source, slot in self.messages:
                copy = pltpu.make_async_remote_copy(
                    src_ref=source,
                    dst_ref=self.recv.at[slot],
                    send_sem=send_sems.at[0],
                    recv_sem=self.sem,
                    device_id=device(*d),
                    device_id_type=MESH,
                )
                pl.when(exists(*d))(copy.start)

        def wait(self):
            pltpu.make_async_copy(self.recv, self.recv, self.sem).wait()

        def fill(self):
            for d, _, slot in self.messages:
                near, away = self.recv.at[slot], self.spare.at[slot]
                pool = zero_rows if near.shape[-2] == 1 else zeros
                none = pool.at[0] if len(near.shape) == 2 else pool.at[pl.ds(0, near.shape[0])]
                pl.when(jnp.logical_not(exists(-d[0], -d[1])))(
                    pltpu.make_async_copy(none, near, self.sem).start
                )
                pl.when(jnp.logical_not(exists(*d)))(
                    pltpu.make_async_copy(none, away, send_sems.at[0]).start
                )

    barrier = pltpu.get_barrier_semaphore()
    partners = FAR_CORNERS + FAR + CORNERS + FACES
    greeted = jnp.int32(0)
    for d in partners:
        there = exists(*d)
        greeted += there.astype(jnp.int32)

        @pl.when(there)
        def _():
            pl.semaphore_signal(barrier, inc=1, device_id=device(*d), device_id_type=MESH)

    sub, lane = iota(0), iota(1)
    perm = jnp.clip(
        lane + jnp.where(lane % 8 == 7, 1, 0) - jnp.where(lane % 8 == 0, 1, 0), 0, 127
    )
    elane = lane // 8
    top, bottom = sub == 0, sub == 7

    loads[0].wait()
    tab[0:4] = pack[0:4]
    columns = pack[PACKED - 1]
    for t in range(T_WJ, TILES):
        tab[t] = wide(columns[:, t : t + 1])
    wk, wj = pack[T_WK], tab[T_WJ]

    def sum_z(value):
        return value + tab[T_ZM] * jnp.take_along_axis(value, perm, axis=1)

    def edges(low, high):
        return jnp.where(top, low, jnp.where(bottom, high, 0.0))

    def row_of(ref, i):
        return wide(ref[i : i + 1, :])

    loads[2].wait()
    amet = jnp.zeros((8, 128), F32)
    for e in range(EZ):
        amet = jnp.where(elane == e, met[0, 0, e], amet)
    loads[1].wait()
    rhs = [sum_z(wk * src[i]) for i in range(8)]

    def lines_of(u):
        for i in range(8):
            ub[8 * i : 8 * i + 8, :] = u[i]
        return [ub[pl.ds(j, 8, stride=8), :] for j in range(8)]

    def edge_row(d):
        return 7 if d > 0 else 0

    def ends(u, group_range, lines=None):
        lines = lines or lines_of(u)
        return {
            d: total(float(STIFF[row, m]) * group[m] for m in group_range(row))
            for d, group, row in (
                ((1, 0), u, 7), ((-1, 0), u, 0), ((0, 1), lines, 7), ((0, -1), lines, 0)
            )
        }

    def opposite(d):
        return (-d[0], -d[1])

    center = (UPPER_BOUND + LOWER_BOUND) / 2.0
    half_width = (UPPER_BOUND - LOWER_BOUND) / 2.0
    bound = center / half_width
    rho = 1.0 / bound
    qk, qj = tab[T_QK], tab[T_QJ]
    plane, mixed = sum_z(wk * amet), sum_z(qk * amet + wk)
    early = []
    for i in range(8):
        w_i, q_i = float(WEIGHTS[i]), float(QDIAG[i])
        diagonal = (q_i * wj + w_i * qj) * plane + (w_i * wj) * mixed
        early.append((w_i / center) * (wj * rhs[i]) / diagonal)
    middle = ends(early, lambda row: range(1, 7))

    lines = lines_of(rhs)
    skin = {d: (rhs if d[0] else lines)[edge_row(d[0] + d[1])] for d in FACES}
    for n, d in enumerate(FACES):
        for f in FACES:
            hsend[n, PLACE[f]] = skin[f]
        hsend[n, 4] = jnp.where(top, amet, middle[d])
        hrs[n, 0] = amet[0:1, :]
        hrs[n, 1] = amet[0:1, :]
    for n, d in enumerate(CORNERS):
        hcs[n, 0] = skin[(d[0], 0)]
        hcs[n, 1] = jnp.where(sub == edge_row(d[0]), amet, skin[(0, d[1])])
    for n, d in enumerate(FAR_CORNERS):
        if abs(d[0]) == 2:
            face, row = skin[(d[0] // 2, 0)], edge_row(d[1])
        else:
            face, row = skin[(0, d[1] // 2)], edge_row(d[0])
        hrs[4 + n, 0] = face[row : row + 1, :]
        hrs[4 + n, 1] = amet[0:1, :]

    def slots(dirs, source):
        return [(d, source(n, d), n) for n, d in enumerate(dirs)]

    blocks_to = [((b - DRIFT, 0), dsend.at[b], n) for n, b in enumerate(AWAY)]
    blocks_back = [((DRIFT - b, 0), rsend.at[b], n) for n, b in enumerate(AWAY)]
    heads = Group(hrecv, slots(FACES, lambda n, d: hsend.at[n]))
    head_corners = Group(hcr, slots(CORNERS, lambda n, d: hcs.at[n]))
    head_far = Group(
        hfr, [(d, hsend.at[0, PLACE[(d[0] // 2, d[1] // 2)]], n) for n, d in enumerate(FAR)]
    )
    head_rows = Group(hrr, slots(FAR + FAR_CORNERS, lambda n, d: hrs.at[n]))
    drops = Group(drecv, blocks_to)
    near_two = Group(nrecv, slots(FACES, lambda n, d: nsend.at[PLACE[d]]))
    far_two = Group(
        grecv,
        [(d, nsend.at[PLACE[(d[0] // 2, d[1] // 2)]], n) for n, d in enumerate(FAR)]
        + [(d, nsend.at[pl.ds(PAIR[d], 2)], pl.ds(4 + 2 * n, 2)) for n, d in enumerate(CORNERS)],
    )
    tilde = Group(trecv, slots(FACES, lambda n, d: tsend.at[PLACE[d]]))
    backs = Group(rrecv, blocks_back)
    tails = Group(frecv, slots(FACES, lambda n, d: fsend.at[n]))
    tail_corners = Group(fcr, slots(CORNERS, lambda n, d: fcs.at[n]))

    @pl.when(jnp.logical_not(inside))
    def _():
        zeros[...] = jnp.zeros_like(zeros)
        zero_rows[...] = jnp.zeros_like(zero_rows)
        for group in groups:
            group.fill()

    def combine(value, recv, corner):
        def face(t):
            return recv(FACES.index((t, 0))) + edges(
                wide(corner(CORNERS.index((t, 1)))), wide(corner(CORNERS.index((t, -1))))
            )

        low, high = recv(FACES.index((0, 1))), recv(FACES.index((0, -1)))
        out = []
        for i in range(8):
            term = value[i] + edges(wide(low[i : i + 1, :]), wide(high[i : i + 1, :]))
            if i == 0:
                term += face(1)
            if i == 7:
                term += face(-1)
            out.append(term)
        return out

    def stage_drops():
        for b in range(REACH):
            for c in range(3):
                dsend[b, c : c + 1, :] = coord[3 * b + c]
                dsend[b, 3 + c : 4 + c, :] = dvel[3 * b + c]
            dsend[b, 6:7, :] = dprop[b, 0:1, :] * dprop[b, 1:2, :]
            dsend[b, 7:8, :] = jnp.where(
                lane[0:1] < cnt[0, 0, b], (elem[b] % EZ).astype(F32), -1.0
            )

    loads[3].wait()
    pltpu.make_async_copy(load_ledger, load_ledger, si.at[4]).wait()
    stage_drops()

    pl.semaphore_wait(barrier, greeted)
    head_rows.start()
    head_far.start()
    head_corners.start()
    heads.start()
    drops.start()

    khigh, klow = halves(
        jnp.concatenate([jnp.where(elane == e, tab[T_KT], 0.0) for e in range(EZ)], axis=0)
    )
    kz[0:128, 0:128] = khigh
    kz[0:128, 128:256] = klow
    kz[128:256, 0:128] = khigh
    kz[128:256, 128:256] = jnp.zeros((128, 128), BF16)

    def along_z(u):
        high, low = halves(jnp.concatenate(u, axis=0))
        both = jnp.dot(
            jnp.concatenate([high, low], axis=1), kz[...], preferred_element_type=F32
        )
        both = both[:, 0:128] + both[:, 128:256]
        return [both[8 * i : 8 * i + 8, :] for i in range(8)]

    def block_of(arrived, own, b):
        return own.at[b] if b == DRIFT else arrived.at[AWAY.index(b)]

    def basis_block(b):
        def basis(r):
            value = tab[T_LAG]
            for m in range(8):
                value = value * jnp.where(sub == m, 1.0, r - float(NODES[m]))
            return value, turned(value, tab, T_DT)

        tile = block_of(drecv, dsend, b)
        eid = row_of(tile, 7)
        lx[b], dx[b] = basis(row_of(tile, 0))
        ly[b], dy[b] = basis(row_of(tile, 1))
        for side_by, part in enumerate(basis(row_of(tile, 2))):
            high = part.astype(BF16).astype(F32)
            for piece, first in ((high, 0), (part - high, 128)):
                spread = jnp.concatenate(
                    [jnp.where(eid == float(e), piece, 0.0) for e in range(EZ)], axis=0
                )
                spread = spread.astype(BF16)
                start = (2 * b + side_by) * CAP
                lzd[first : first + 128, start : start + CAP] = spread
                if not side_by:
                    lzt[b * CAP : b * CAP + CAP, first : first + 128] = jnp.transpose(spread)

    def contract(planes, first, second):
        inner = total(row_of(first, i) * planes[i] for i in range(8))
        return jnp.sum(second[...] * inner, axis=0, keepdims=True)

    def stacked(value):
        high, low = halves(value)
        return jnp.concatenate(
            [
                jnp.concatenate([high, high], axis=1),
                jnp.concatenate([low, jnp.zeros_like(low)], axis=1),
            ],
            axis=0,
        )

    def base_values():
        loads[8].wait()
        left = stacked(jnp.concatenate([bvel[c, i] for c in range(3) for i in range(8)], axis=0))
        for b in range(REACH):
            span = slice(2 * b * CAP, 2 * b * CAP + CAP)
            both = jnp.dot(left, lzd[:, span], preferred_element_type=F32)
            both = both[0:192, :] + both[192:384, :]
            for c in range(3):
                planes = [both[64 * c + 8 * i : 64 * c + 8 * i + 8, :] for i in range(8)]
                fbase[b, c : c + 1, :] = contract(planes, lx.at[b], ly.at[b])

    basis_block(DRIFT)

    for group in (heads, head_corners, head_far, head_rows):
        group.wait()
    skins, factor, middle_of = {}, {(0, 0): amet}, {}
    for n, d in enumerate(FACES):
        at = opposite(d)
        skins[at] = {f: hrecv[n, PLACE[f]] for f in FACES}
        middle_of[at] = hrecv[n, 4]
        factor[at] = wide(middle_of[at][0:1, :])
    for n, d in enumerate(CORNERS):
        row = edge_row(d[0])
        skins[opposite(d)] = {(d[0], 0): hcr[n, 0], (0, d[1]): hcr[n, 1]}
        factor[opposite(d)] = wide(hcr[n, 1, row : row + 1, :])
    point = {}
    for n, d in enumerate(FAR + FAR_CORNERS):
        point[opposite(d)] = wide(hrr[n, 0])
        factor[opposite(d)] = wide(hrr[n, 1])

    def shared_row(n):
        row = edge_row(CORNERS[n][1])
        return hcr[n, 0, row : row + 1, :]

    residual = combine(rhs, lambda n: skins[opposite(FACES[n])][FACES[n]], shared_row)
    own_x = amet + edges(factor[(0, -1)], factor[(0, 1)])
    a_y = [amet + factor[(-1, 0)]] + [amet] * 6 + [amet + factor[(1, 0)]]
    side = {
        (t, 0): factor[(t, 0)] + edges(factor[(t, -1)], factor[(t, 1)]) for t in (-1, 1)
    }
    side |= {
        (0, t): factor[(0, t)] + edges(factor[(-1, t)], factor[(1, t)]) for t in (-1, 1)
    }
    a_sum = [own_x + side[(-1, 0)]] + [own_x] * 6 + [own_x + side[(1, 0)]]

    def present(ds, dc):
        return exists(ds, dc).astype(F32)

    count_y = 1.0 + edges(present(0, -1), present(0, 1))
    count_x = [1.0 + present(-1, 0)] + [1.0] * 6 + [1.0 + present(1, 0)]

    wkj = wk * wj
    mass = [wkj * (count_x[i] * count_y) for i in range(8)]
    planes = {}
    for i in (0, 1, 7):
        planes[i] = (sum_z(wk * a_sum[i]), sum_z(qk * a_sum[i] + wk * (count_x[i] * count_y)))
    inv_diag, update = [], []
    for i in range(8):
        w_i, q_i = float(WEIGHTS[i]), float(QDIAG[i])
        plane, mixed = planes[i if i in planes else 1]
        residual[i] = (w_i * wj) * residual[i]
        diagonal = (q_i * wj + w_i * qj) * plane + (w_i * wj) * mixed
        inv_diag.append(1.0 / diagonal)
        update.append(inv_diag[i] * residual[i] * (1.0 / center))
    iterate = update

    across = {d: wkj * side[d] for d in FACES}
    def own_part(u, lines):
        flat, slope = along_z(u), stiff_x(u)
        for j, tile in enumerate(stiff_x(lines)):
            mb[pl.ds(j, 8, stride=8), :] = tile
        out = []
        for i in range(8):
            w_i = float(WEIGHTS[i])
            out.append(
                sum_z(
                    wkj * own_x * slope[i]
                    + (w_i * wk) * a_y[i] * mb[8 * i : 8 * i + 8, :]
                    + (w_i * wj) * a_sum[i] * flat[i]
                    + w_i * mass[i] * u[i]
                )
            )
        return out

    def less_beside(value, flow):
        part = {d: sum_z(across[d] * flow[d]) for d in FACES}
        out = [
            value[i]
            - edges(wide(part[(0, -1)][i : i + 1, :]), wide(part[(0, 1)][i : i + 1, :]))
            for i in range(8)
        ]
        out[0] -= part[(-1, 0)]
        out[7] -= part[(1, 0)]
        return out

    steps = []
    for sweep in range(SWEEPS):
        rho_next = 1.0 / (2.0 * bound - rho)
        steps.append((rho_next * rho, 2.0 * rho_next / half_width))
        rho = rho_next

    def advanced(u, left, step):
        return [step[0] * u[i] + step[1] * (inv_diag[i] * left[i]) for i in range(8)]

    def outer(value, a_near, count):
        w_0, q_0 = float(WEIGHTS[0]), float(QDIAG[0])
        diagonal = (q_0 * wj + w_0 * qj) * sum_z(wk * a_near) + (w_0 * wj) * sum_z(
            qk * a_near + wk * jnp.maximum(count, 1.0)
        )
        inverse = 1.0 / diagonal
        return inverse, inverse * (((w_0 / center) * wj) * value)

    def plus(p, q):
        return (p[0] + q[0], p[1] + q[1])

    def rim_of(d, t):
        return (0, t) if d[0] else (t, 0)

    def ordered(at, far, near):
        return edges(far, near) if at[0] + at[1] < 0 else edges(near, far)

    def a_of(*places):
        return total(factor[p] for p in places)

    def n_of(*places):
        return total(present(*p) for p in places)

    shell, flow = {}, {}
    lines = lines_of(update)
    for n, d in enumerate(FACES):
        at = opposite(d)
        far = plus(at, at)
        forward = d[0] + d[1] > 0
        beside = {t: plus(at, rim_of(d, t)) for t in (-1, 1)}
        beyond = {t: plus(far, rim_of(d, t)) for t in (-1, 1)}
        row = edge_row(at[0] + at[1])
        corner_values = [
            wide(skins[beside[t]][opposite(rim_of(d, t))][row : row + 1, :]) + point[beyond[t]]
            for t in (-1, 1)
        ]
        inverse, value = outer(
            skins[at][at] + hfr[n] + edges(*corner_values),
            a_of(at, far) + edges(*[a_of(beside[t], beyond[t]) for t in (-1, 1)]),
            n_of(at, far) + edges(*[n_of(beside[t], beyond[t]) for t in (-1, 1)]),
        )
        weight = wkj * (factor[far] + edges(factor[beyond[-1]], factor[beyond[1]]))
        shell[at, at] = (weight, inverse)
        sums = []
        for t in (-1, 1):
            rim = rim_of(d, t)
            inverse, rim_value = outer(
                skins[at][rim] + skins[beside[t]][opposite(rim)],
                a_of(at, beside[t]) + ordered(at, a_of(far, beyond[t]), a_of((0, 0), rim)),
                n_of(at, beside[t]) + ordered(at, n_of(far, beyond[t]), n_of((0, 0), rim)),
            )
            weight = wkj * (factor[beside[t]] + ordered(at, factor[beyond[t]], factor[rim]))
            shell[at, rim] = (weight, inverse)
            weights = tab[T_END + (2 if forward else 3)]
            sums.append(wide(jnp.sum(weights * rim_value, axis=0, keepdims=True)))
        far_weight = float(STIFF[7, 0] if forward else STIFF[0, 7])
        near_weight = float(STIFF[7, 7] if forward else STIFF[0, 0])
        shared = (update if d[0] else lines)[0 if forward else 7]
        inner = jnp.where(top, sums[0], jnp.where(bottom, sums[1], middle_of[at]))
        flow[at] = inner + far_weight * value + near_weight * shared

    own = own_part(update, lines)
    residual = less_beside([residual[i] - own[i] for i in range(8)], flow)
    update = advanced(update, residual, steps[0])
    iterate = [iterate[i] + update[i] for i in range(8)]

    lines = lines_of(update)
    for d, tile in ends(update, lambda row: range(8), lines).items():
        nsend[PLACE[d]] = tile
        if PLACE[d] == 0:
            nsend[4] = tile
    near_two.start()
    far_two.start()
    own = own_part(update, lines)
    residual = [residual[i] - own[i] for i in range(8)]
    guess = advanced(update, residual, steps[1])
    for d, tile in ends(guess, lambda row: range(7) if row else range(1, 8)).items():
        tsend[PLACE[d]] = tile
    tilde.start()
    drops.wait()
    for b in AWAY:
        basis_block(b)
    base_values()

    near_two.wait()
    residual = less_beside(residual, {opposite(d): nrecv[n] for n, d in enumerate(FACES)})
    update = advanced(update, residual, steps[1])
    iterate = [iterate[i] + update[i] for i in range(8)]
    lines = lines_of(update)
    own = own_part(update, lines)
    residual = [residual[i] - own[i] for i in range(8)]

    for group in (far_two, tilde):
        group.wait()

    def from_corner(at, along):
        d = opposite(at)
        return grecv[4 + 2 * CORNERS.index(d) + (PLACE[along] - PAIR[d]) % 4]

    flow = {}
    for n, d in enumerate(FACES):
        at = opposite(d)

        def change(face, across_it):
            weight, inverse = shell[at, face]
            return (-steps[1][1]) * (inverse * sum_z(weight * across_it))

        forward = d[0] + d[1] > 0
        far_weight = float(STIFF[7, 0] if forward else STIFF[0, 7])
        near_weight = float(STIFF[7, 7] if forward else STIFF[0, 0])
        weights = tab[T_END if forward else T_END + 1]
        rims = []
        for t in (-1, 1):
            rim = rim_of(d, t)
            corner = plus(at, rim)
            changed = change(rim, from_corner(corner, opposite(rim)))
            rims.append(wide(jnp.sum(weights * changed, axis=0, keepdims=True)))
        if d[0]:
            shared = update[0 if forward else 7]
        else:
            shared = lines[0 if forward else 7]
        flow[at] = (
            trecv[n] + far_weight * change(at, grecv[n]) + edges(*rims) + near_weight * shared
        )
    residual = less_beside(residual, flow)
    update = advanced(update, residual, steps[2])
    iterate = [iterate[i] + update[i] for i in range(8)]

    for i in range(8):
        p_out[i] = iterate[i]

    left = stacked(jnp.concatenate([amet * iterate[i] for i in range(8)], axis=0))
    forces = []
    for b in range(REACH):
        span = slice(2 * b * CAP, 2 * b * CAP + 2 * CAP)
        both = jnp.dot(left, lzd[:, span], preferred_element_type=F32)
        both = both[0:64, :] + both[64:128, :]
        flat = [both[8 * i : 8 * i + 8, 0:CAP] for i in range(8)]
        slope = [both[8 * i : 8 * i + 8, CAP : 2 * CAP] for i in range(8)]
        grads = [
            contract(flat, dx.at[b], ly.at[b]),
            contract(flat, lx.at[b], dy.at[b]),
            contract(slope, lx.at[b], ly.at[b]),
        ]
        tile = block_of(drecv, dsend, b)
        force = []
        for c in range(3):
            fluid = fbase[b, c : c + 1, :] - grads[c]
            rsend[b, c] = fluid
            force.append(tile[6:7, :] * (tile[3 + c : 4 + c, :] - fluid))
        forces.append(force)
    backs.start()

    columns_high, columns_low = [], []
    for b in range(REACH):
        rows_ = []
        for c in range(3):
            weighted = wide(forces[b][c]) * ly[b]
            rows_ += [weighted * row_of(lx.at[b], i) for i in range(8)]
        high, low = halves(jnp.concatenate(rows_, axis=0))
        columns_high.append(high)
        columns_low.append(low)
    left = jnp.concatenate(
        [jnp.concatenate(columns_high, axis=1), jnp.concatenate(columns_low, axis=1)], axis=0
    )
    both = jnp.dot(left, lzt[...], preferred_element_type=F32)
    drag = both[0:192, 0:128] + both[0:192, 128:256] + both[192:384, 0:128]
    drag = [drag[8 * i : 8 * i + 8, :] for i in range(24)]
    for c in range(3):
        for i in (0, 7):
            drag[8 * c + i] = sum_z(drag[8 * c + i])
    for i in range(24):
        mb[8 * i : 8 * i + 8, :] = drag[i]
    for c in range(3):
        for n, d in enumerate(CORNERS):
            row = edge_row(d[1])
            fcs[n, c] = drag[8 * c + edge_row(d[0])][row : row + 1, :]
    tail_corners.start()
    for c in range(3):
        for n, d in enumerate(FACES):
            row = edge_row(d[0] + d[1])
            if d[0]:
                fsend[n, c] = drag[8 * c + row]
            else:
                line = mb[pl.ds(64 * c + row, 8, stride=8), :]
                fsend[n, c] = jnp.where(top | bottom, line, sum_z(line))
    tails.start()
    for c in range(3):
        for i in range(1, 7):
            drag[8 * c + i] = sum_z(drag[8 * c + i])

    backs.wait()
    for b in range(REACH):
        tile = block_of(rrecv, rsend, b)
        for c in range(3):
            accel = dprop[b, 0:1, :] * (tile[c] - dvel[3 * b + c])
            acc_out[3 * b + c] = jnp.where(lane[0:1] < cnt[0, 0, b], accel, 0.0)

    tails.wait()
    tail_corners.wait()
    for c in range(3):
        value = combine(
            drag[8 * c : 8 * c + 8], lambda n: frecv[n, c], lambda n: fcr[n, c]
        )
        for i in range(8):
            m_out[c, i] = value[i]

    pltpu.make_async_copy(ledger, ledger, send_sems.at[0]).wait()


def deliver(p_in, m_in, acc_in, p_out, m_out, acc_out, sems):
    copies = [
        pltpu.make_async_copy(near, far, sems.at[n])
        for n, (near, far) in enumerate([(m_in, m_out), (p_in, p_out), (acc_in, acc_out)])
    ]
    for copy in copies:
        copy.start()
    for copy in copies:
        copy.wait()


def on_device(source, metric, base, elem, coord, dvel, dprop, counts):
    vmem = pl.BlockSpec(memory_space=pltpu.VMEM)
    hbm = pl.BlockSpec(memory_space=pltpu.HBM)
    dma = pltpu.SemaphoreType.DMA
    elem = elem.reshape(REACH, 1, CAP)
    coord = coord.reshape(REACH * 3, 1, CAP)
    dvel = dvel.reshape(REACH * 3, 1, CAP)
    dprop = dprop.reshape(REACH, 2, CAP)
    tile = (8, 128)
    row = (1, 128)
    blocks = pltpu.VMEM((REACH,) + tile, F32)
    arrive_shapes = [
        (4, 5) + tile, (4, 2) + tile, (4,) + tile, (12, 2) + row, (4,) + tile, (4,) + tile,
        (12,) + tile, (4,) + tile, (4, 3) + row, (4, 3) + tile, (4, 3) + row,
    ]
    arrive = [pltpu.VMEM(shape, F32) for shape in arrive_shapes]
    total_rows = sum(int(np.prod(shape)) for shape in arrive_shapes) // 128
    shapes = (
        jax.ShapeDtypeStruct((8, 8, 128), F32),
        jax.ShapeDtypeStruct((3, 8, 8, 128), F32),
        jax.ShapeDtypeStruct((REACH * 3, 1, CAP), F32),
    )
    operands = (source, metric, base, elem, coord, dvel, dprop, counts)
    operands += (jnp.asarray(constant_tiles()),)
    outs = pl.pallas_call(
        kernel,
        out_shape=shapes,
        in_specs=[hbm] * 9,
        out_specs=(vmem,) * 3,
        scratch_shapes=[
            pltpu.VMEM((8, 8, 128), F32),
            pltpu.SMEM((1, 1, EZ), F32),
            pltpu.VMEM((3, 8, 8, 128), F32),
            pltpu.VMEM((REACH, 1, CAP), jnp.int32),
            pltpu.VMEM((REACH * 3, 1, CAP), F32),
            pltpu.VMEM((REACH * 3, 1, CAP), F32),
            pltpu.VMEM((REACH, 2, CAP), F32),
            pltpu.SMEM((1, 1, REACH), jnp.int32),
            pltpu.VMEM((PACKED,) + tile, F32),
            pltpu.VMEM((TILES,) + tile, F32),
            pltpu.VMEM((64, 128), F32),
            pltpu.VMEM((192, 128), F32),
            pltpu.VMEM((256, 256), BF16),
            pltpu.VMEM((256, 2 * REACH * CAP), BF16),
            pltpu.VMEM((REACH * CAP, 256), BF16),
            blocks,
            blocks,
            blocks,
            blocks,
            blocks,
            pltpu.VMEM((4, 5) + tile, F32),
            arrive[0],
            pltpu.VMEM((4, 2) + tile, F32),
            arrive[1],
            arrive[2],
            pltpu.VMEM((12, 2) + row, F32),
            arrive[3],
            pltpu.VMEM((5,) + tile, F32),
            arrive[5],
            pltpu.VMEM((4, 3) + tile, F32),
            arrive[9],
            pltpu.VMEM((4, 3) + row, F32),
            arrive[10],
            blocks,
            arrive[4],
            pltpu.VMEM((REACH, 3) + row, F32),
            arrive[8],
            pltpu.VMEM((4,) + tile, F32),
            arrive[7],
            arrive[6],
            pltpu.VMEM((8,) + tile, F32),
            pltpu.VMEM((3,) + row, F32),
            *arrive,
            pltpu.VMEM((total_rows,) + row, F32),
            pltpu.VMEM((REACH * 9,) + row, F32),
            dma((6,)),
            dma((1,)),
            dma((len(arrive),)),
        ],
        compiler_params=pltpu.CompilerParams(
            collective_id=0, has_side_effects=True, vmem_limit_bytes=32 * 1024 * 1024
        ),
    )(*[pltpu.with_memory_space_constraint(operand, pltpu.HBM) for operand in operands])
    pressure, momentum, accel = pl.pallas_call(
        deliver,
        out_shape=shapes,
        in_specs=[vmem] * 3,
        out_specs=(hbm,) * 3,
        scratch_shapes=[dma((3,))],
        compiler_params=pltpu.CompilerParams(vmem_limit_bytes=1024 * 1024),
    )(*outs)
    return pressure, momentum, accel.reshape(1, 1, REACH, 3, CAP)


def solution(mesh):
    in_specs = (
        P("stream", "cross", None),
        P("stream", "cross", None),
        P(None, "stream", "cross", None),
        P("stream", "cross", None, None),
        P("stream", "cross", None, None, None),
        P("stream", "cross", None, None, None),
        P("stream", "cross", None, None, None),
        P("stream", "cross", None),
    )
    out_specs = (
        P("stream", "cross", None),
        P(None, "stream", "cross", None),
        P("stream", "cross", None, None, None),
    )
    return jax.shard_map(
        on_device, mesh=mesh, in_specs=in_specs, out_specs=out_specs, check_vma=False
    )
```

```python
import jax
import jax.numpy as jnp
import numpy as np
from jax import lax
from jax.experimental import pallas as pl
from jax.experimental.pallas import tpu as pltpu
from jax.sharding import PartitionSpec as P

SWEEPS = 3
UPPER_BOUND = 2.5
LOWER_BOUND = UPPER_BOUND / 30.0
REACH = 5
DRIFT = 2
CAP = 128
EZ = 16
GLL_POINTS = [
    -1.0,
    -0.8717401485096066,
    -0.5917001814331423,
    -0.2092992179024789,
    0.2092992179024789,
    0.5917001814331423,
    0.8717401485096066,
    1.0,
]
F32 = jnp.float32
BF16 = jnp.bfloat16
MESH = pl.DeviceIdType.MESH

FACES = [(1, 0), (-1, 0), (0, 1), (0, -1)]
CORNERS = [(1, 1), (1, -1), (-1, 1), (-1, -1)]
FAR = [(2, 0), (-2, 0), (0, 2), (0, -2)]
FAR_CORNERS = [(2, 1), (2, -1), (-2, 1), (-2, -1), (1, 2), (1, -2), (-1, 2), (-1, -2)]
AWAY = [0, 4, 1, 3]
PLACE = {(1, 0): 0, (0, 1): 1, (-1, 0): 2, (0, -1): 3}
PAIR = {(1, 1): 0, (-1, 1): 1, (-1, -1): 2, (1, -1): 3}


def legendre_seven(points):
    before = points * 0.0 + 1.0
    current = points
    for order in range(1, 7):
        following = ((2.0 * order + 1.0) * points * current - order * before) / (order + 1.0)
        before = current
        current = following
    return current


def gll_tables():
    nodes = np.array(GLL_POINTS)
    values = legendre_seven(nodes)
    weights = 2.0 / (56.0 * values * values)
    deriv = np.zeros((8, 8))
    for row in range(8):
        for col in range(8):
            if row != col:
                deriv[row, col] = values[row] / (values[col] * (nodes[row] - nodes[col]))
    deriv[0, 0] = -14.0
    deriv[7, 7] = 14.0
    return nodes, weights, deriv


NODES, WEIGHTS, DERIV = gll_tables()
STIFF = DERIV.T @ (WEIGHTS[:, None] * DERIV)
QDIAG = np.diag(STIFF)

PACKED = 5
T_WK, T_QK, T_KT, T_ZM, T_WJ, T_QJ, T_CY, T_DT, T_LAG, T_END = 0, 1, 2, 3, 4, 5, 6, 14, 22, 23
TILES = 27


def constant_tiles():
    lane = np.arange(128)
    row = np.arange(8)
    tiles = np.zeros((PACKED, 8, 128))
    tiles[T_WK] = WEIGHTS[lane % 8][None, :]
    tiles[T_QK] = QDIAG[lane % 8][None, :]
    tiles[T_KT] = STIFF[lane % 8, :].T
    last = (lane % 8 == 7) & (lane < 127)
    first = (lane % 8 == 0) & (lane > 0)
    tiles[T_ZM] = (last | first)[None, :]
    columns = tiles[PACKED - 1]
    columns[:, T_WJ] = WEIGHTS
    columns[:, T_QJ] = QDIAG
    for turn in range(8):
        columns[:, T_CY + turn] = STIFF[row, (row - turn) % 8]
        columns[:, T_DT + turn] = DERIV[(row - turn) % 8, row]
    gaps = NODES[:, None] - NODES[None, :] + np.eye(8)
    columns[:, T_LAG] = 1.0 / gaps.prod(1)
    columns[0:7, T_END] = STIFF[7, 0:7]
    columns[1:8, T_END + 1] = STIFF[0, 1:8]
    columns[1:7, T_END + 2] = STIFF[7, 1:7]
    columns[1:7, T_END + 3] = STIFF[0, 1:7]
    return tiles.astype(np.float32)


def iota(dim):
    return lax.broadcasted_iota(jnp.int32, (8, 128), dim)


def total(terms):
    terms = list(terms)
    while len(terms) > 1:
        pairs = [a + b for a, b in zip(terms[::2], terms[1::2])]
        if len(terms) % 2:
            pairs.append(terms[-1])
        terms = pairs
    return terms[0]


def wide(row):
    return jnp.broadcast_to(row, (8, 128))


def halves(value):
    high = value.astype(BF16)
    return high, (value - high.astype(F32)).astype(BF16)


def stiff_x(u):
    even = [u[m] + u[7 - m] for m in range(4)]
    odd = [u[m] - u[7 - m] for m in range(4)]
    out = [None] * 8
    for i in range(4):
        e = total(float((STIFF[i, m] + STIFF[i, 7 - m]) / 2.0) * even[m] for m in range(4))
        o = total(float((STIFF[i, m] - STIFF[i, 7 - m]) / 2.0) * odd[m] for m in range(4))
        out[i] = e + o
        out[7 - i] = e - o
    return out


def turned(value, tab, first):
    terms = [tab[first] * value]
    for turn in range(1, 8):
        terms.append(tab[first + turn] * pltpu.roll(value, turn, 0))
    return total(terms)


def kernel(
    src_h, met_h, bvel_h, elem_h, coord_h, dvel_h, dprop_h, cnt_h, tab_h,
    p_out, m_out, acc_out,
    src, met, bvel, elem, coord, dvel, dprop, cnt, pack, tab,
    ub, mb, kz, lzd, lzt, lx, dx, ly, dy, fbase,
    hsend, hrecv, hcs, hcr, hfr, hrs, hrr, nsend, nrecv, fsend, frecv, fcs, fcr,
    dsend, drecv, rsend, rrecv, tsend, trecv, grecv, zeros, zero_rows,
    *rest,
):
    *spare, ledger, load_ledger, si, send_sems, recv_sems = rest
    slabs, cols = lax.axis_size("stream"), lax.axis_size("cross")
    slab, col = lax.axis_index("stream"), lax.axis_index("cross")

    loads = [
        pltpu.make_async_copy(far, near, si.at[n])
        for far, near, n in [
            (tab_h, pack, 0), (src_h, src, 1), (met_h, met, 2), (cnt_h, cnt, 3), (elem_h, elem, 4),
            (coord_h, coord, 4), (dvel_h, dvel, 4), (dprop_h, dprop, 4), (bvel_h, bvel, 5),
        ]
    ]
    for load in loads:
        load.start()

    def device(ds, dc):
        return (slab + ds, col + dc)

    def exists(ds, dc):
        found = (slab + ds >= 0) & (slab + ds < slabs)
        return found & (col + dc >= 0) & (col + dc < cols)

    inside = (slab >= 2) & (slab < slabs - 2) & (col >= 2) & (col < cols - 2)
    groups = []

    class Group:
        def __init__(self, recv, messages):
            self.recv, self.messages = recv, messages
            self.sem = recv_sems.at[len(groups)]
            self.spare = spare[len(groups)]
            groups.append(self)

        def start(self):
            for d, source, slot in self.messages:
                copy = pltpu.make_async_remote_copy(
                    src_ref=source,
                    dst_ref=self.recv.at[slot],
                    send_sem=send_sems.at[0],
                    recv_sem=self.sem,
                    device_id=device(*d),
                    device_id_type=MESH,
                )
                pl.when(exists(*d))(copy.start)

        def wait(self):
            pltpu.make_async_copy(self.recv, self.recv, self.sem).wait()

        def fill(self):
            for d, _, slot in self.messages:
                near, away = self.recv.at[slot], self.spare.at[slot]
                pool = zero_rows if near.shape[-2] == 1 else zeros
                none = pool.at[0] if len(near.shape) == 2 else pool.at[pl.ds(0, near.shape[0])]
                pl.when(jnp.logical_not(exists(-d[0], -d[1])))(
                    pltpu.make_async_copy(none, near, self.sem).start
                )
                pl.when(jnp.logical_not(exists(*d)))(
                    pltpu.make_async_copy(none, away, send_sems.at[0]).start
                )

    barrier = pltpu.get_barrier_semaphore()
    partners = sorted(FAR_CORNERS + FAR + CORNERS + FACES, key=lambda d: (-abs(d[0]), -abs(d[1])))
    greeted = jnp.int32(0)
    for d in partners:
        there = exists(*d)
        greeted += there.astype(jnp.int32)

        @pl.when(there)
        def _():
            pl.semaphore_signal(barrier, inc=1, device_id=device(*d), device_id_type=MESH)

    sub, lane = iota(0), iota(1)
    perm = jnp.clip(
        lane + jnp.where(lane % 8 == 7, 1, 0) - jnp.where(lane % 8 == 0, 1, 0), 0, 127
    )
    elane = lane // 8
    top, bottom = sub == 0, sub == 7

    loads[0].wait()
    tab[0:4] = pack[0:4]
    columns = pack[PACKED - 1]
    for t in range(T_WJ, TILES):
        tab[t] = wide(columns[:, t : t + 1])
    wk, wj = pack[T_WK], tab[T_WJ]

    def sum_z(value):
        return value + tab[T_ZM] * jnp.take_along_axis(value, perm, axis=1)

    def edges(low, high):
        return jnp.where(top, low, jnp.where(bottom, high, 0.0))

    def row_of(ref, i):
        return wide(ref[i : i + 1, :])

    loads[2].wait()
    amet = jnp.zeros((8, 128), F32)
    for e in range(EZ):
        amet = jnp.where(elane == e, met[0, 0, e], amet)
    loads[1].wait()
    rhs = [sum_z(wk * src[i]) for i in range(8)]

    def lines_of(u):
        for i in range(8):
            ub[8 * i : 8 * i + 8, :] = u[i]
        return [ub[pl.ds(j, 8, stride=8), :] for j in range(8)]

    def edge_row(d):
        return 7 if d > 0 else 0

    def ends(u, group_range, lines=None):
        lines = lines or lines_of(u)
        return {
            d: total(float(STIFF[row, m]) * group[m] for m in group_range(row))
            for d, group, row in (
                ((1, 0), u, 7), ((-1, 0), u, 0), ((0, 1), lines, 7), ((0, -1), lines, 0)
            )
        }

    def opposite(d):
        return (-d[0], -d[1])

    center = (UPPER_BOUND + LOWER_BOUND) / 2.0
    half_width = (UPPER_BOUND - LOWER_BOUND) / 2.0
    bound = center / half_width
    rho = 1.0 / bound
    qk, qj = tab[T_QK], tab[T_QJ]
    plane, mixed = sum_z(wk * amet), sum_z(qk * amet + wk)
    early = []
    for i in range(8):
        w_i, q_i = float(WEIGHTS[i]), float(QDIAG[i])
        diagonal = (q_i * wj + w_i * qj) * plane + (w_i * wj) * mixed
        early.append((w_i / center) * (wj * rhs[i]) / diagonal)
    middle = ends(early, lambda row: range(1, 7))

    lines = lines_of(rhs)
    skin = {d: (rhs if d[0] else lines)[edge_row(d[0] + d[1])] for d in FACES}
    for n, d in enumerate(FACES):
        for f in FACES:
            hsend[n, PLACE[f]] = skin[f]
        hsend[n, 4] = jnp.where(top, amet, middle[d])
        hrs[n, 0] = amet[0:1, :]
        hrs[n, 1] = amet[0:1, :]
    for n, d in enumerate(CORNERS):
        hcs[n, 0] = skin[(d[0], 0)]
        hcs[n, 1] = jnp.where(sub == edge_row(d[0]), amet, skin[(0, d[1])])
    for n, d in enumerate(FAR_CORNERS):
        if abs(d[0]) == 2:
            face, row = skin[(d[0] // 2, 0)], edge_row(d[1])
        else:
            face, row = skin[(0, d[1] // 2)], edge_row(d[0])
        hrs[4 + n, 0] = face[row : row + 1, :]
        hrs[4 + n, 1] = amet[0:1, :]

    def slots(dirs, source):
        return [(d, source(n, d), n) for n, d in enumerate(dirs)]

    blocks_to = [((b - DRIFT, 0), dsend.at[b], n) for n, b in enumerate(AWAY)]
    blocks_back = [((DRIFT - b, 0), rsend.at[b], n) for n, b in enumerate(AWAY)]
    heads = Group(hrecv, slots(FACES, lambda n, d: hsend.at[n]))
    head_corners = Group(hcr, slots(CORNERS, lambda n, d: hcs.at[n]))
    head_far = Group(
        hfr, [(d, hsend.at[0, PLACE[(d[0] // 2, d[1] // 2)]], n) for n, d in enumerate(FAR)]
    )
    head_rows = Group(hrr, slots(FAR + FAR_CORNERS, lambda n, d: hrs.at[n]))
    drops = Group(drecv, blocks_to)
    near_two = Group(nrecv, slots(FACES, lambda n, d: nsend.at[PLACE[d]]))
    far_two = Group(
        grecv,
        [(d, nsend.at[PLACE[(d[0] // 2, d[1] // 2)]], n) for n, d in enumerate(FAR)]
        + [(d, nsend.at[pl.ds(PAIR[d], 2)], pl.ds(4 + 2 * n, 2)) for n, d in enumerate(CORNERS)],
    )
    tilde = Group(trecv, slots(FACES, lambda n, d: tsend.at[PLACE[d]]))
    backs = Group(rrecv, blocks_back)
    tails = Group(frecv, slots(FACES, lambda n, d: fsend.at[n]))
    tail_corners = Group(fcr, slots(CORNERS, lambda n, d: fcs.at[n]))

    @pl.when(jnp.logical_not(inside))
    def _():
        zeros[...] = jnp.zeros_like(zeros)
        zero_rows[...] = jnp.zeros_like(zero_rows)
        for group in groups:
            group.fill()

    def combine(value, recv, corner):
        def face(t):
            return recv(FACES.index((t, 0))) + edges(
                wide(corner(CORNERS.index((t, 1)))), wide(corner(CORNERS.index((t, -1))))
            )

        low, high = recv(FACES.index((0, 1))), recv(FACES.index((0, -1)))
        out = []
        for i in range(8):
            term = value[i] + edges(wide(low[i : i + 1, :]), wide(high[i : i + 1, :]))
            if i == 0:
                term += face(1)
            if i == 7:
                term += face(-1)
            out.append(term)
        return out

    def stage_drops():
        for b in range(REACH):
            for c in range(3):
                dsend[b, c : c + 1, :] = coord[3 * b + c]
                dsend[b, 3 + c : 4 + c, :] = dvel[3 * b + c]
            dsend[b, 6:7, :] = dprop[b, 0:1, :] * dprop[b, 1:2, :]
            dsend[b, 7:8, :] = jnp.where(
                lane[0:1] < cnt[0, 0, b], (elem[b] % EZ).astype(F32), -1.0
            )

    loads[3].wait()
    pltpu.make_async_copy(load_ledger, load_ledger, si.at[4]).wait()
    stage_drops()

    pl.semaphore_wait(barrier, greeted)
    head_rows.start()
    head_far.start()
    head_corners.start()
    heads.start()
    drops.start()

    khigh, klow = halves(
        jnp.concatenate([jnp.where(elane == e, tab[T_KT], 0.0) for e in range(EZ)], axis=0)
    )
    kz[0:128, 0:128] = khigh
    kz[0:128, 128:256] = klow
    kz[128:256, 0:128] = khigh
    kz[128:256, 128:256] = jnp.zeros((128, 128), BF16)

    def along_z(u):
        high, low = halves(jnp.concatenate(u, axis=0))
        both = jnp.dot(
            jnp.concatenate([high, low], axis=1), kz[...], preferred_element_type=F32
        )
        both = both[:, 0:128] + both[:, 128:256]
        return [both[8 * i : 8 * i + 8, :] for i in range(8)]

    def block_of(arrived, own, b):
        return own.at[b] if b == DRIFT else arrived.at[AWAY.index(b)]

    def basis_block(b):
        def basis(r):
            value = tab[T_LAG]
            for m in range(8):
                value = value * jnp.where(sub == m, 1.0, r - float(NODES[m]))
            return value, turned(value, tab, T_DT)

        tile = block_of(drecv, dsend, b)
        eid = row_of(tile, 7)
        lx[b], dx[b] = basis(row_of(tile, 0))
        ly[b], dy[b] = basis(row_of(tile, 1))
        for side_by, part in enumerate(basis(row_of(tile, 2))):
            high = part.astype(BF16).astype(F32)
            for piece, first in ((high, 0), (part - high, 128)):
                spread = jnp.concatenate(
                    [jnp.where(eid == float(e), piece, 0.0) for e in range(EZ)], axis=0
                )
                spread = spread.astype(BF16)
                start = (2 * b + side_by) * CAP
                lzd[first : first + 128, start : start + CAP] = spread
                if not side_by:
                    lzt[b * CAP : b * CAP + CAP, first : first + 128] = jnp.transpose(spread)

    def contract(planes, first, second):
        inner = total(row_of(first, i) * planes[i] for i in range(8))
        return jnp.sum(second[...] * inner, axis=0, keepdims=True)

    def stacked(value):
        high, low = halves(value)
        return jnp.concatenate(
            [
                jnp.concatenate([high, high], axis=1),
                jnp.concatenate([low, jnp.zeros_like(low)], axis=1),
            ],
            axis=0,
        )

    def base_values():
        loads[8].wait()
        left = stacked(jnp.concatenate([bvel[c, i] for c in range(3) for i in range(8)], axis=0))
        for b in range(REACH):
            span = slice(2 * b * CAP, 2 * b * CAP + CAP)
            both = jnp.dot(left, lzd[:, span], preferred_element_type=F32)
            both = both[0:192, :] + both[192:384, :]
            for c in range(3):
                planes = [both[64 * c + 8 * i : 64 * c + 8 * i + 8, :] for i in range(8)]
                fbase[b, c : c + 1, :] = contract(planes, lx.at[b], ly.at[b])

    basis_block(DRIFT)

    for group in (heads, head_corners, head_far, head_rows):
        group.wait()
    skins, factor, middle_of = {}, {(0, 0): amet}, {}
    for n, d in enumerate(FACES):
        at = opposite(d)
        skins[at] = {f: hrecv[n, PLACE[f]] for f in FACES}
        middle_of[at] = hrecv[n, 4]
        factor[at] = wide(middle_of[at][0:1, :])
    for n, d in enumerate(CORNERS):
        row = edge_row(d[0])
        skins[opposite(d)] = {(d[0], 0): hcr[n, 0], (0, d[1]): hcr[n, 1]}
        factor[opposite(d)] = wide(hcr[n, 1, row : row + 1, :])
    point = {}
    for n, d in enumerate(FAR + FAR_CORNERS):
        point[opposite(d)] = wide(hrr[n, 0])
        factor[opposite(d)] = wide(hrr[n, 1])

    def shared_row(n):
        row = edge_row(CORNERS[n][1])
        return hcr[n, 0, row : row + 1, :]

    residual = combine(rhs, lambda n: skins[opposite(FACES[n])][FACES[n]], shared_row)
    own_x = amet + edges(factor[(0, -1)], factor[(0, 1)])
    a_y = [amet + factor[(-1, 0)]] + [amet] * 6 + [amet + factor[(1, 0)]]
    side = {
        (t, 0): factor[(t, 0)] + edges(factor[(t, -1)], factor[(t, 1)]) for t in (-1, 1)
    }
    side |= {
        (0, t): factor[(0, t)] + edges(factor[(-1, t)], factor[(1, t)]) for t in (-1, 1)
    }
    a_sum = [own_x + side[(-1, 0)]] + [own_x] * 6 + [own_x + side[(1, 0)]]

    def present(ds, dc):
        return exists(ds, dc).astype(F32)

    count_y = 1.0 + edges(present(0, -1), present(0, 1))
    count_x = [1.0 + present(-1, 0)] + [1.0] * 6 + [1.0 + present(1, 0)]

    wkj = wk * wj
    mass = [wkj * (count_x[i] * count_y) for i in range(8)]
    planes = {}
    for i in (0, 1, 7):
        planes[i] = (sum_z(wk * a_sum[i]), sum_z(qk * a_sum[i] + wk * (count_x[i] * count_y)))
    inv_diag, update = [], []
    for i in range(8):
        w_i, q_i = float(WEIGHTS[i]), float(QDIAG[i])
        plane, mixed = planes[i if i in planes else 1]
        residual[i] = (w_i * wj) * residual[i]
        diagonal = (q_i * wj + w_i * qj) * plane + (w_i * wj) * mixed
        inv_diag.append(1.0 / diagonal)
        update.append(inv_diag[i] * residual[i] * (1.0 / center))
    iterate = update

    across = {d: wkj * side[d] for d in FACES}
    def own_part(u, lines):
        flat, slope = along_z(u), stiff_x(u)
        for j, tile in enumerate(stiff_x(lines)):
            mb[pl.ds(j, 8, stride=8), :] = tile
        out = []
        for i in range(8):
            w_i = float(WEIGHTS[i])
            out.append(
                sum_z(
                    wkj * own_x * slope[i]
                    + (w_i * wk) * a_y[i] * mb[8 * i : 8 * i + 8, :]
                    + (w_i * wj) * a_sum[i] * flat[i]
                    + w_i * mass[i] * u[i]
                )
            )
        return out

    def less_beside(value, flow):
        part = {d: sum_z(across[d] * flow[d]) for d in FACES}
        out = [
            value[i]
            - edges(wide(part[(0, -1)][i : i + 1, :]), wide(part[(0, 1)][i : i + 1, :]))
            for i in range(8)
        ]
        out[0] -= part[(-1, 0)]
        out[7] -= part[(1, 0)]
        return out

    steps = []
    for sweep in range(SWEEPS):
        rho_next = 1.0 / (2.0 * bound - rho)
        steps.append((rho_next * rho, 2.0 * rho_next / half_width))
        rho = rho_next

    def advanced(u, left, step):
        return [step[0] * u[i] + step[1] * (inv_diag[i] * left[i]) for i in range(8)]

    def outer(value, a_near, count):
        w_0, q_0 = float(WEIGHTS[0]), float(QDIAG[0])
        diagonal = (q_0 * wj + w_0 * qj) * sum_z(wk * a_near) + (w_0 * wj) * sum_z(
            qk * a_near + wk * jnp.maximum(count, 1.0)
        )
        inverse = 1.0 / diagonal
        return inverse, inverse * (((w_0 / center) * wj) * value)

    def plus(p, q):
        return (p[0] + q[0], p[1] + q[1])

    def rim_of(d, t):
        return (0, t) if d[0] else (t, 0)

    def ordered(at, far, near):
        return edges(far, near) if at[0] + at[1] < 0 else edges(near, far)

    def a_of(*places):
        return total(factor[p] for p in places)

    def n_of(*places):
        return total(present(*p) for p in places)

    shell, flow = {}, {}
    lines = lines_of(update)
    for n, d in enumerate(FACES):
        at = opposite(d)
        far = plus(at, at)
        forward = d[0] + d[1] > 0
        beside = {t: plus(at, rim_of(d, t)) for t in (-1, 1)}
        beyond = {t: plus(far, rim_of(d, t)) for t in (-1, 1)}
        row = edge_row(at[0] + at[1])
        corner_values = [
            wide(skins[beside[t]][opposite(rim_of(d, t))][row : row + 1, :]) + point[beyond[t]]
            for t in (-1, 1)
        ]
        inverse, value = outer(
            skins[at][at] + hfr[n] + edges(*corner_values),
            a_of(at, far) + edges(*[a_of(beside[t], beyond[t]) for t in (-1, 1)]),
            n_of(at, far) + edges(*[n_of(beside[t], beyond[t]) for t in (-1, 1)]),
        )
        weight = wkj * (factor[far] + edges(factor[beyond[-1]], factor[beyond[1]]))
        shell[at, at] = (weight, inverse)
        sums = []
        for t in (-1, 1):
            rim = rim_of(d, t)
            inverse, rim_value = outer(
                skins[at][rim] + skins[beside[t]][opposite(rim)],
                a_of(at, beside[t]) + ordered(at, a_of(far, beyond[t]), a_of((0, 0), rim)),
                n_of(at, beside[t]) + ordered(at, n_of(far, beyond[t]), n_of((0, 0), rim)),
            )
            weight = wkj * (factor[beside[t]] + ordered(at, factor[beyond[t]], factor[rim]))
            shell[at, rim] = (weight, inverse)
            weights = tab[T_END + (2 if forward else 3)]
            sums.append(wide(jnp.sum(weights * rim_value, axis=0, keepdims=True)))
        far_weight = float(STIFF[7, 0] if forward else STIFF[0, 7])
        near_weight = float(STIFF[7, 7] if forward else STIFF[0, 0])
        shared = (update if d[0] else lines)[0 if forward else 7]
        inner = jnp.where(top, sums[0], jnp.where(bottom, sums[1], middle_of[at]))
        flow[at] = inner + far_weight * value + near_weight * shared

    own = own_part(update, lines)
    residual = less_beside([residual[i] - own[i] for i in range(8)], flow)
    update = advanced(update, residual, steps[0])
    iterate = [iterate[i] + update[i] for i in range(8)]

    lines = lines_of(update)
    for d, tile in ends(update, lambda row: range(8), lines).items():
        nsend[PLACE[d]] = tile
        if PLACE[d] == 0:
            nsend[4] = tile
    near_two.start()
    far_two.start()
    own = own_part(update, lines)
    residual = [residual[i] - own[i] for i in range(8)]
    guess = advanced(update, residual, steps[1])
    for d, tile in ends(guess, lambda row: range(7) if row else range(1, 8)).items():
        tsend[PLACE[d]] = tile
    tilde.start()
    drops.wait()
    for b in AWAY:
        basis_block(b)
    base_values()

    near_two.wait()
    residual = less_beside(residual, {opposite(d): nrecv[n] for n, d in enumerate(FACES)})
    update = advanced(update, residual, steps[1])
    iterate = [iterate[i] + update[i] for i in range(8)]
    lines = lines_of(update)
    own = own_part(update, lines)
    residual = [residual[i] - own[i] for i in range(8)]

    for group in (far_two, tilde):
        group.wait()

    def from_corner(at, along):
        d = opposite(at)
        return grecv[4 + 2 * CORNERS.index(d) + (PLACE[along] - PAIR[d]) % 4]

    flow = {}
    for n, d in enumerate(FACES):
        at = opposite(d)

        def change(face, across_it):
            weight, inverse = shell[at, face]
            return (-steps[1][1]) * (inverse * sum_z(weight * across_it))

        forward = d[0] + d[1] > 0
        far_weight = float(STIFF[7, 0] if forward else STIFF[0, 7])
        near_weight = float(STIFF[7, 7] if forward else STIFF[0, 0])
        weights = tab[T_END if forward else T_END + 1]
        rims = []
        for t in (-1, 1):
            rim = rim_of(d, t)
            corner = plus(at, rim)
            changed = change(rim, from_corner(corner, opposite(rim)))
            rims.append(wide(jnp.sum(weights * changed, axis=0, keepdims=True)))
        if d[0]:
            shared = update[0 if forward else 7]
        else:
            shared = lines[0 if forward else 7]
        flow[at] = (
            trecv[n] + far_weight * change(at, grecv[n]) + edges(*rims) + near_weight * shared
        )
    residual = less_beside(residual, flow)
    update = advanced(update, residual, steps[2])
    iterate = [iterate[i] + update[i] for i in range(8)]

    for i in range(8):
        p_out[i] = iterate[i]

    left = stacked(jnp.concatenate([amet * iterate[i] for i in range(8)], axis=0))
    forces = []
    for b in range(REACH):
        span = slice(2 * b * CAP, 2 * b * CAP + 2 * CAP)
        both = jnp.dot(left, lzd[:, span], preferred_element_type=F32)
        both = both[0:64, :] + both[64:128, :]
        flat = [both[8 * i : 8 * i + 8, 0:CAP] for i in range(8)]
        slope = [both[8 * i : 8 * i + 8, CAP : 2 * CAP] for i in range(8)]
        grads = [
            contract(flat, dx.at[b], ly.at[b]),
            contract(flat, lx.at[b], dy.at[b]),
            contract(slope, lx.at[b], ly.at[b]),
        ]
        tile = block_of(drecv, dsend, b)
        force = []
        for c in range(3):
            fluid = fbase[b, c : c + 1, :] - grads[c]
            rsend[b, c] = fluid
            force.append(tile[6:7, :] * (tile[3 + c : 4 + c, :] - fluid))
        forces.append(force)
    backs.start()

    columns_high, columns_low = [], []
    for b in range(REACH):
        rows_ = []
        for c in range(3):
            weighted = wide(forces[b][c]) * ly[b]
            rows_ += [weighted * row_of(lx.at[b], i) for i in range(8)]
        high, low = halves(jnp.concatenate(rows_, axis=0))
        columns_high.append(high)
        columns_low.append(low)
    left = jnp.concatenate(
        [jnp.concatenate(columns_high, axis=1), jnp.concatenate(columns_low, axis=1)], axis=0
    )
    both = jnp.dot(left, lzt[...], preferred_element_type=F32)
    drag = both[0:192, 0:128] + both[0:192, 128:256] + both[192:384, 0:128]
    drag = [drag[8 * i : 8 * i + 8, :] for i in range(24)]
    for c in range(3):
        for i in (0, 7):
            drag[8 * c + i] = sum_z(drag[8 * c + i])
    for i in range(24):
        mb[8 * i : 8 * i + 8, :] = drag[i]
    for c in range(3):
        for n, d in enumerate(CORNERS):
            row = edge_row(d[1])
            fcs[n, c] = drag[8 * c + edge_row(d[0])][row : row + 1, :]
    tail_corners.start()
    for c in range(3):
        for n, d in enumerate(FACES):
            row = edge_row(d[0] + d[1])
            if d[0]:
                fsend[n, c] = drag[8 * c + row]
            else:
                line = mb[pl.ds(64 * c + row, 8, stride=8), :]
                fsend[n, c] = jnp.where(top | bottom, line, sum_z(line))
    tails.start()
    for c in range(3):
        for i in range(1, 7):
            drag[8 * c + i] = sum_z(drag[8 * c + i])

    backs.wait()
    for b in range(REACH):
        tile = block_of(rrecv, rsend, b)
        for c in range(3):
            accel = dprop[b, 0:1, :] * (tile[c] - dvel[3 * b + c])
            acc_out[3 * b + c] = jnp.where(lane[0:1] < cnt[0, 0, b], accel, 0.0)

    tails.wait()
    tail_corners.wait()
    for c in range(3):
        value = combine(
            drag[8 * c : 8 * c + 8], lambda n: frecv[n, c], lambda n: fcr[n, c]
        )
        for i in range(8):
            m_out[c, i] = value[i]

    pltpu.make_async_copy(ledger, ledger, send_sems.at[0]).wait()


def deliver(p_in, m_in, acc_in, p_out, m_out, acc_out, sems):
    copies = [
        pltpu.make_async_copy(near, far, sems.at[n])
        for n, (near, far) in enumerate([(m_in, m_out), (p_in, p_out), (acc_in, acc_out)])
    ]
    for copy in copies:
        copy.start()
    for copy in copies:
        copy.wait()


def on_device(source, metric, base, elem, coord, dvel, dprop, counts):
    vmem = pl.BlockSpec(memory_space=pltpu.VMEM)
    hbm = pl.BlockSpec(memory_space=pltpu.HBM)
    dma = pltpu.SemaphoreType.DMA
    elem = elem.reshape(REACH, 1, CAP)
    coord = coord.reshape(REACH * 3, 1, CAP)
    dvel = dvel.reshape(REACH * 3, 1, CAP)
    dprop = dprop.reshape(REACH, 2, CAP)
    tile = (8, 128)
    row = (1, 128)
    blocks = pltpu.VMEM((REACH,) + tile, F32)
    arrive_shapes = [
        (4, 5) + tile, (4, 2) + tile, (4,) + tile, (12, 2) + row, (4,) + tile, (4,) + tile,
        (12,) + tile, (4,) + tile, (4, 3) + row, (4, 3) + tile, (4, 3) + row,
    ]
    arrive = [pltpu.VMEM(shape, F32) for shape in arrive_shapes]
    total_rows = sum(int(np.prod(shape)) for shape in arrive_shapes) // 128
    shapes = (
        jax.ShapeDtypeStruct((8, 8, 128), F32),
        jax.ShapeDtypeStruct((3, 8, 8, 128), F32),
        jax.ShapeDtypeStruct((REACH * 3, 1, CAP), F32),
    )
    operands = (source, metric, base, elem, coord, dvel, dprop, counts)
    operands += (jnp.asarray(constant_tiles()),)
    outs = pl.pallas_call(
        kernel,
        out_shape=shapes,
        in_specs=[hbm] * 9,
        out_specs=(vmem,) * 3,
        scratch_shapes=[
            pltpu.VMEM((8, 8, 128), F32),
            pltpu.SMEM((1, 1, EZ), F32),
            pltpu.VMEM((3, 8, 8, 128), F32),
            pltpu.VMEM((REACH, 1, CAP), jnp.int32),
            pltpu.VMEM((REACH * 3, 1, CAP), F32),
            pltpu.VMEM((REACH * 3, 1, CAP), F32),
            pltpu.VMEM((REACH, 2, CAP), F32),
            pltpu.SMEM((1, 1, REACH), jnp.int32),
            pltpu.VMEM((PACKED,) + tile, F32),
            pltpu.VMEM((TILES,) + tile, F32),
            pltpu.VMEM((64, 128), F32),
            pltpu.VMEM((192, 128), F32),
            pltpu.VMEM((256, 256), BF16),
            pltpu.VMEM((256, 2 * REACH * CAP), BF16),
            pltpu.VMEM((REACH * CAP, 256), BF16),
            blocks,
            blocks,
            blocks,
            blocks,
            blocks,
            pltpu.VMEM((4, 5) + tile, F32),
            arrive[0],
            pltpu.VMEM((4, 2) + tile, F32),
            arrive[1],
            arrive[2],
            pltpu.VMEM((12, 2) + row, F32),
            arrive[3],
            pltpu.VMEM((5,) + tile, F32),
            arrive[5],
            pltpu.VMEM((4, 3) + tile, F32),
            arrive[9],
            pltpu.VMEM((4, 3) + row, F32),
            arrive[10],
            blocks,
            arrive[4],
            pltpu.VMEM((REACH, 3) + row, F32),
            arrive[8],
            pltpu.VMEM((4,) + tile, F32),
            arrive[7],
            arrive[6],
            pltpu.VMEM((8,) + tile, F32),
            pltpu.VMEM((3,) + row, F32),
            *arrive,
            pltpu.VMEM((total_rows,) + row, F32),
            pltpu.VMEM((REACH * 9,) + row, F32),
            dma((6,)),
            dma((1,)),
            dma((len(arrive),)),
        ],
        compiler_params=pltpu.CompilerParams(
            collective_id=0, has_side_effects=True, vmem_limit_bytes=32 * 1024 * 1024
        ),
    )(*[pltpu.with_memory_space_constraint(operand, pltpu.HBM) for operand in operands])
    pressure, momentum, accel = pl.pallas_call(
        deliver,
        out_shape=shapes,
        in_specs=[vmem] * 3,
        out_specs=(hbm,) * 3,
        scratch_shapes=[dma((3,))],
        compiler_params=pltpu.CompilerParams(vmem_limit_bytes=1024 * 1024),
    )(*outs)
    return pressure, momentum, accel.reshape(1, 1, REACH, 3, CAP)


def solution(mesh):
    in_specs = (
        P("stream", "cross", None),
        P("stream", "cross", None),
        P(None, "stream", "cross", None),
        P("stream", "cross", None, None),
        P("stream", "cross", None, None, None),
        P("stream", "cross", None, None, None),
        P("stream", "cross", None, None, None),
        P("stream", "cross", None),
    )
    out_specs = (
        P("stream", "cross", None),
        P(None, "stream", "cross", None),
        P("stream", "cross", None, None, None),
    )
    return jax.shard_map(
        on_device, mesh=mesh, in_specs=in_specs, out_specs=out_specs, check_vma=False
    )
```
